32 devices in a mesh: wide: 8 (over z, x), blk: 4 (over y, core).
Axes of the slice: x: 2, y: 2, z: 4, core: 2. Of those that a mesh axis runs over, the one named last changes fastest.
Arguments:
- tokens: bfloat16 [16, 256, 768], P('wide', 'blk'), may hold values from -21 to 21
- cotangent: bfloat16 [16, 256, 768], P('wide', 'blk'), may hold values from -4 to 4
- row_counts: int32 [16, 4], P('wide', 'blk'), may hold values from 3 to 4, as said below
- mask_flags: int32 [16, 256], P('wide', 'blk'), may hold values from 0 to 1, as said below
- ln1_gain: float32 [768], replicated, may hold values from 0.5 to 1.5
- ln1_bias: float32 [768], replicated, may hold values from -1 to 1
- w_qkv: bfloat16 [768, 2304], replicated, may hold values from -0.21875 to 0.21875
- q_bias: float32 [768], replicated, may hold values from -1 to 1
- v_bias: float32 [768], replicated, may hold values from -1 to 1
- w_out: bfloat16 [768, 768], replicated, may hold values from -1.75 to 1.75
- out_bias: float32 [768], replicated, may hold values from -1 to 1
- ln2_gain: float32 [768], replicated, may hold values from 0.5 to 1.5
- ln2_bias: float32 [768], replicated, may hold values from -1 to 1
- w_fc1: bfloat16 [768, 3072], replicated, may hold values from -0.21875 to 0.21875
- fc1_bias: float32 [3072], replicated, may hold values from -1 to 1
- w_fc2: bfloat16 [3072, 768], replicated, may hold values from -0.109375 to 0.109375
- fc2_bias: float32 [768], replicated, may hold values from -1 to 1
Outputs:
- layer_out: bfloat16 [16, 256, 768], P('wide', 'blk')
- grad_tokens: bfloat16 [16, 256, 768], P('wide', 'blk')
- grad_ln1_gain: float32 [768], replicated
- grad_ln1_bias: float32 [768], replicated
- grad_w_qkv: float32 [768, 2304], replicated
- grad_q_bias: float32 [768], replicated
- grad_v_bias: float32 [768], replicated
- grad_w_out: float32 [768, 768], replicated
- grad_out_bias: float32 [768], replicated
- grad_ln2_gain: float32 [768], replicated
- grad_ln2_bias: float32 [768], replicated
- grad_w_fc1: float32 [768, 3072], replicated
- grad_fc1_bias: float32 [3072], replicated
- grad_w_fc2: float32 [3072, 768], replicated
- grad_fc2_bias: float32 [768], replicated
The draws below stay inside these ranges and needn't reach their ends.
Inputs may be any that keep to these rules, and one draw needn't show every extreme that they name: `row_counts`: each image's 4 counts are two of 4 and two of 3 in an order drawn for that image; blk index c holds the image's live patches in its first 14 * count slots. `mask_flags`: each image has its own share of ones, between 40 and 80 in 100.
All inputs are finite; a program needn't handle non-finite values.
Results may differ from the reference program's by a relative error of at most 0.015.
Values may be sent and summed in bfloat16 or wider, within the bound.
A program may use at most 192 MiB of HBM per device.

```python
import math
import jax
import jax.numpy as jnp
from jax import lax

D = 768
HEADS = 12
HEAD_DIM = 64
FF = 3072
ROW_LEN = 14
IMG_DEV = 2
SLOTS = 64
SEQ = 256
IMAGES = 16
N_WIDE = 8
N_BLK = 4


def draw_tokens(key, part):
    key = jax.random.fold_in(key, 37)
    key_base, key_rows, key_cols = jax.random.split(key, 3)
    shape_all = (IMAGES, N_BLK * SLOTS, D)
    base_values = jnp.clip(jax.random.normal(key_base, shape_all, jnp.float32), -3.5, 3.5)
    row_scale = jnp.exp(jax.random.uniform(key_rows, (IMAGES, N_BLK * SLOTS, 1), jnp.float32, math.log(0.5), math.log(3.0)))
    col_scale = jnp.exp(jax.random.uniform(key_cols, (1, 1, D), jnp.float32, math.log(0.7), math.log(2.0)))
    return (base_values * row_scale * col_scale).astype(jnp.bfloat16)


def draw_row_counts(key, part):
    key = jax.random.fold_in(key, 11)
    ranks = jax.random.randint(key, (IMAGES, N_BLK), 0, 1 << 20) * N_BLK
    ranks = ranks + lax.broadcasted_iota(jnp.int32, (IMAGES, N_BLK), 1)
    order = jnp.argsort(ranks, axis=1)
    return jnp.where(order < 2, 4, 3).astype(jnp.int32)


def draw_mask_flags(key, part):
    key = jax.random.fold_in(key, 23)
    key_ratio, key_rolls = jax.random.split(key)
    mask_ratio = jax.random.randint(key_ratio, (IMAGES, 1), 40, 81)
    dice_rolls = jax.random.randint(key_rolls, (IMAGES, N_BLK * SLOTS), 0, 100)
    return (dice_rolls < mask_ratio).astype(jnp.int32)


def block_scale(rng, dims, cuts, least, high):
    level, own = 1.0, jax.random.fold_in(rng, 6)
    for dim, blocks in cuts:
        steps = jnp.exp(jax.random.uniform(jax.random.fold_in(own, dim), (blocks,), jnp.float32, least / len(cuts), high / len(cuts)))
        level = level * jnp.repeat(steps, dims[dim] // blocks).reshape([-1 if axis == dim else 1 for axis in range(len(dims))])
    return level


def noise(rng, dims, scale, reach, cuts=(), kind=jnp.bfloat16):
    factor_of = block_scale(rng, dims, cuts, -0.22, 0.18) if cuts else 1.0
    result = jax.random.normal(rng, dims, jnp.float32) * scale * factor_of
    return jnp.minimum(jnp.maximum(result, -reach), reach).astype(kind)


def setup_inputs(seed: int = 0) -> dict:
    key_list = jax.random.split(jax.random.key(seed), 18)
    return {
        "tokens": draw_tokens(jax.random.fold_in(key_list[17], 71), 0),
        "cotangent": noise(key_list[1], (IMAGES, SEQ, D), 1.0, 4.0, ((0, 8), (1, 4))),
        "row_counts": draw_row_counts(jax.random.fold_in(key_list[17], 71), 0),
        "mask_flags": draw_mask_flags(jax.random.fold_in(key_list[17], 71), 0),
        "ln1_gain": jnp.clip(1.0 + 0.1 * jax.random.normal(key_list[4], (D,), jnp.float32), 0.5, 1.5),
        "ln1_bias": noise(key_list[5], (D,), 0.2, 1.0, (), jnp.float32),
        "w_qkv": noise(key_list[6], (D, 3 * D), D ** -0.5, 0.21875),
        "q_bias": noise(key_list[7], (D,), 0.2, 1.0, (), jnp.float32),
        "v_bias": noise(key_list[8], (D,), 0.2, 1.0, (), jnp.float32),
        "w_out": noise(key_list[9], (D, D), (D // 64) ** -0.5, 1.75),
        "out_bias": noise(key_list[10], (D,), 0.2, 1.0, (), jnp.float32),
        "ln2_gain": jnp.clip(1.0 + 0.1 * jax.random.normal(key_list[11], (D,), jnp.float32), 0.5, 1.5),
        "ln2_bias": noise(key_list[12], (D,), 0.2, 1.0, (), jnp.float32),
        "w_fc1": noise(key_list[13], (D, FF), D ** -0.5, 0.21875),
        "fc1_bias": noise(key_list[14], (FF,), 0.2, 1.0, (), jnp.float32),
        "w_fc2": noise(key_list[15], (FF, D), FF ** -0.5, 0.109375),
        "fc2_bias": noise(key_list[16], (D,), 0.2, 1.0, (), jnp.float32),
    }


@jax.custom_vjp
def low(v):
    return lax.optimization_barrier(v.astype(jnp.bfloat16)).astype(jnp.float32)

@jax.custom_vjp
def low_back(v):
    return v

def low_keep(v):
    return (low(v), None)

def low_pass(kept, grad):
    return (grad,)

def back_keep(v):
    return (v, None)

def back_low(kept, grad):
    return (low(grad),)
low.defvjp(low_keep, low_pass)
low_back.defvjp(back_keep, back_low)

def layer_norm(values_in, norm_gain, norm_bias):
    mean_val = lax.optimization_barrier(jnp.mean(values_in, -1, keepdims=True))
    centred = values_in - mean_val
    variance = lax.optimization_barrier(jnp.mean(centred * centred, -1, keepdims=True))
    return centred * lax.rsqrt(variance + 1e-06) * norm_gain + norm_bias

def forward(params, tokens, live_slot):
    ln1_gain, ln1_bias, w_qkv, q_bias, v_bias, w_out, out_bias, ln2_gain, ln2_bias, w_fc1, fc1_bias, w_fc2, fc2_bias = params
    highest = lax.Precision.HIGHEST
    groups, seq_len, width = tokens.shape
    normed_first = low(layer_norm(tokens, ln1_gain, ln1_bias))
    qkv_proj = jnp.einsum('gsd,de->gse', normed_first, w_qkv, precision=highest)
    queries = low(low_back(qkv_proj[..., :width] + q_bias))
    keys_low = low(low_back(qkv_proj[..., width:2 * width]))
    values_low = low(low_back(qkv_proj[..., 2 * width:] + v_bias))
    query_heads = queries.reshape(groups, seq_len, HEADS, HEAD_DIM)
    key_heads = keys_low.reshape(groups, seq_len, HEADS, HEAD_DIM)
    value_heads = values_low.reshape(groups, seq_len, HEADS, HEAD_DIM)
    raw_scores = jnp.einsum('gqhe,gkhe->ghqk', query_heads, key_heads, precision=highest)
    scores = low_back(HEAD_DIM ** (-0.5) * raw_scores)
    key_live = (live_slot > 0.5)[:, None, None, :]
    masked = jnp.where(key_live, scores, -1e+30)
    row_top = lax.optimization_barrier(jnp.max(masked, -1, keepdims=True))
    expo_vals = jnp.where(key_live, jnp.exp(masked - row_top), 0.0)
    probs_low = low(expo_vals / lax.optimization_barrier(jnp.sum(expo_vals, -1, keepdims=True)))
    mixed_heads = jnp.einsum('ghqk,gkhe->gqhe', probs_low, value_heads, precision=highest)
    merged = low(low_back(mixed_heads.reshape(groups, seq_len, width)))
    attn_out = low_back(jnp.einsum('gsd,de->gse', merged, w_out, precision=highest) + out_bias)
    residual = tokens + attn_out
    normed_second = low(layer_norm(residual, ln2_gain, ln2_bias))
    hidden = low_back(jnp.einsum('gsd,df->gsf', normed_second, w_fc1, precision=highest) + fc1_bias)
    activated = low(jax.nn.gelu(hidden, approximate=False))
    mlp_out = low_back(jnp.einsum('gsf,fd->gsd', activated, w_fc2, precision=highest) + fc2_bias)
    return residual + mlp_out

def grouped(array_in):
    return array_in.reshape((N_WIDE, IMG_DEV) + array_in.shape[1:])

def reference(tokens, cotangent, row_counts, mask_flags, ln1_gain, ln1_bias, w_qkv, q_bias, v_bias, w_out, out_bias, ln2_gain, ln2_bias, w_fc1, fc1_bias, w_fc2, fc2_bias):
    params = tuple((tensor.astype(jnp.float32) for tensor in (ln1_gain, ln1_bias, w_qkv, q_bias, v_bias, w_out, out_bias, ln2_gain, ln2_bias, w_fc1, fc1_bias, w_fc2, fc2_bias)))
    seq_len = N_BLK * SLOTS
    within = jnp.arange(seq_len, dtype=jnp.int32) % SLOTS
    limits = jnp.repeat(row_counts, SLOTS, axis=1) * ROW_LEN
    live_slot = (within[None, :] < limits).astype(jnp.float32)
    weight = live_slot * mask_flags.astype(jnp.float32)
    inputs_all = (grouped(tokens.astype(jnp.float32)), grouped(cotangent.astype(jnp.float32)), grouped(live_slot), grouped(weight))
    zero_grads = jax.tree.map(jnp.zeros_like, params)

    def scan_step(totals, group_in):
        tok_group, cot_group, live_group, weight_group = group_in
        outputs, pull_back = jax.vjp(lambda par, tok: forward(par, tok, live_group), params, tok_group)
        param_grads, token_grads = pull_back(cot_group * weight_group[..., None])
        totals = jax.tree.map(jnp.add, totals, param_grads)
        return (totals, (outputs.astype(jnp.bfloat16), token_grads.astype(jnp.bfloat16)))
    totals, (out_groups, grad_groups) = lax.scan(scan_step, zero_grads, inputs_all)
    factor = float(IMAGES * seq_len) ** (-0.5)
    g_ln1_gain, g_ln1_bias, g_qkv, g_q_bias, g_v_bias, g_out, g_out_bias, g_ln2_gain, g_ln2_bias, g_fc1, g_fc1_bias, g_fc2, g_fc2_bias = tuple((tensor * factor for tensor in totals))
    layer_out = out_groups.reshape(IMAGES, seq_len, D)
    grad_tokens = grad_groups.reshape(IMAGES, seq_len, D)
    return (layer_out, grad_tokens, g_ln1_gain, g_ln1_bias, g_qkv, g_q_bias, g_v_bias, g_out, g_out_bias, g_ln2_gain, g_ln2_bias, g_fc1, g_fc1_bias, g_fc2, g_fc2_bias)
```

```python
import functools

import jax
import jax.numpy as jnp
from jax import lax
from jax.experimental import pallas as pl
from jax.experimental.pallas import tpu as pltpu
from jax.sharding import PartitionSpec as P

HEADS = 12
ROW_LEN = 14
EPS = 1e-06
RING = 8
BF = jnp.bfloat16
F32 = jnp.float32
MESH = pl.DeviceIdType.MESH
NT = (((1,), (1,)), ((), ()))
TN = (((0,), (0,)), ((), ()))


def dot(a, b, dims=(((1,), (0,)), ((), ()))):
    return lax.dot_general(a, b, dims, preferred_element_type=F32)


def ring_place(r):
    return jnp.where(r % 2 == 0, r // 2, RING - 1 - r // 2)


def ring_member(q):
    return jnp.where(q < RING // 2, 2 * q, 2 * RING - 1 - 2 * q)


def al(v, m):
    return pl.multiple_of(v, m)


class Stream:
    def __init__(self, way, local, final, bufs, kind, rows, cols):
        self.way, self.local, self.final, self.bufs, self.kind = way, local, final, bufs, kind
        self.rows, self.cols = rows, cols


def layer_kernel(n_wide, factor, *refs):
    (
        tok, cot, counts, flags, g1, b1, qb, vb, ob, g2, b2, fb1, fb2, wqkv_h, wout_h, w1_h, w2_h,
        lo_out, gt_out, f2, f1, fq, fo, sall,
        wqkv, wout, w1, w2, xs, cs, meta, n1, n1t, u1, inv1, qkv, probs, mix, mrg, exs, exr, res, n2, n2t, u2, inv2,
        act, gd, gh, gres, ga, gm, gqkv, mps, mpr, lo_s, gt_s, sg, sy, sv,
        l2, l1, lq, lout, r768, r384, rqn, rqp, y768, yqn, yqp, x768, x384, gsh, gsv,
        w_sem, t_send, t_recv, e_send, e_recv, o_send, o_recv,
        rs_send, rs_recv, yb_send, yb_recv, ya_send, ya_recv, ag_send, ag_recv, yg_send, yg_recv,
        c_send, c_recv, s_send, s_recv, g_send, g_recv,
    ) = refs
    groups = n_wide // RING
    seq, width = xs.shape
    half = width // 2
    ffh = w1.shape[1]
    slots = seq // 4
    w = lax.axis_index("wide")
    b = lax.axis_index("blk")
    y, c = b // 2, b % 2
    group, inner = w // RING, w % RING
    p = ring_place(inner)

    def at_place(q):
        return (group * RING + ring_member(lax.rem(q + RING, RING)), b)

    nxt, prv = at_place(p + 1), at_place(p - 1)
    core = (w, 2 * y + 1 - c)
    ydev = (w, 2 * (1 - y) + c)
    ydiag = (w, 2 * (1 - y) + 1 - c)
    others = [(lax.rem(group + j, groups) * RING + inner, b) for j in range(1, groups)]

    bar = pltpu.get_barrier_semaphore()
    greeted = [core, ydev, ydiag, nxt, prv] + others
    for dev in greeted:
        pl.semaphore_signal(bar, inc=1, device_id=dev, device_id_type=MESH)
    half_c = al(c * half, 128)
    ffh_c = al(c * ffh, 128)
    loads = [
        pltpu.make_async_copy(wqkv_h.at[:, pl.ds(al(j * width + c * half, 128), half)], wqkv.at[:, pl.ds(j * half, half)], w_sem.at[j])
        for j in range(3)
    ] + [
        pltpu.make_async_copy(wout_h.at[pl.ds(half_c, half), :], wout, w_sem.at[3]),
        pltpu.make_async_copy(w1_h.at[:, pl.ds(ffh_c, ffh)], w1, w_sem.at[4]),
        pltpu.make_async_copy(w2_h.at[pl.ds(ffh_c, ffh), :], w2, w_sem.at[5]),
    ]
    for load in loads:
        load.start()

    def remote(src, dst, send, recv, dev):
        return pltpu.make_async_remote_copy(
            src_ref=src, dst_ref=dst, send_sem=send, recv_sem=recv, device_id=dev, device_id_type=MESH
        )

    lane64 = lax.broadcasted_iota(jnp.int32, (1, slots), 1)
    zero64 = jnp.zeros((1, slots), F32)
    for img in range(2):
        live = (lane64 < counts[pl.ds(img, 1), :] * ROW_LEN).astype(F32)
        weight = live * flags[pl.ds(img, 1), :].astype(F32)
        for row, val in ((0, live), (1, weight)):
            low = jnp.concatenate([val, zero64], 1)
            high = jnp.concatenate([zero64, val], 1)
            meta[4 + img, pl.ds(row, 1), :] = jnp.where(c == 0, low, high)
    seg = al(b * slots, slots)
    xs[pl.ds(seg, slots), :] = tok[y]
    cs[pl.ds(seg, slots), :] = cot[y]
    meta[b] = meta[4 + y]

    pl.semaphore_wait(bar, len(greeted))
    first = []
    for i, (dev, img) in enumerate(((core, y), (ydev, 1 - y), (ydiag, 1 - y))):
        first.append([
            remote(meta.at[4 + img], meta.at[b], t_send.at[3 * i], t_recv.at[3 * i], dev),
            remote(tok.at[img], xs.at[pl.ds(seg, slots), :], t_send.at[3 * i + 1], t_recv.at[3 * i + 1], dev),
            remote(cot.at[img], cs.at[pl.ds(seg, slots), :], t_send.at[3 * i + 2], t_recv.at[3 * i + 2], dev),
        ])
    for kind in range(3):
        for trio in first:
            trio[kind].start()
    for kind in range(2):
        for trio in first:
            trio[kind].wait_recv()

    blocks = seq // 64

    def rows_of(i):
        return pl.ds(al(i * 64, 64), 64)

    def norm(src, gain, bias, unit_ref, inv_ref, out):
        def body(i, carry):
            r = rows_of(i)
            v = src[r, :].astype(F32)
            cen = v - jnp.mean(v, -1, keepdims=True)
            inv = lax.rsqrt(jnp.mean(cen * cen, -1, keepdims=True) + EPS)
            unit = cen * inv
            unit_ref[r, :] = unit
            inv_ref[r, :] = inv
            out[r, :] = (unit * gain[...] + bias[...]).astype(BF)
            return carry
        lax.fori_loop(0, blocks, body, 0)

    norm(xs, g1, b1, u1, inv1, n1)
    loads[0].wait()
    loads[1].wait()
    loads[2].wait()
    qkv[:, pl.ds(0, half)] = (dot(n1[...], wqkv[:, pl.ds(0, half)]) + qb[:, pl.ds(half_c, half)]).astype(BF)
    qkv[:, pl.ds(half, half)] = dot(n1[...], wqkv[:, pl.ds(half, half)]).astype(BF)
    qkv[:, pl.ds(2 * half, half)] = (
        dot(n1[...], wqkv[:, pl.ds(2 * half, half)]) + vb[:, pl.ds(half_c, half)]
    ).astype(BF)

    live_row = jnp.concatenate([meta[0, 0:1, :] + meta[1, 0:1, :], meta[2, 0:1, :] + meta[3, 0:1, :]], 1)
    weight_row = jnp.concatenate([meta[0, 1:2, :] + meta[1, 1:2, :], meta[2, 1:2, :] + meta[3, 1:2, :]], 1)
    key_live = live_row > 0.5
    lane = lax.broadcasted_iota(jnp.int32, (1, 128), 1)
    low_lanes = lane < 64
    head_mask = [low_lanes.astype(BF), (lane >= 64).astype(BF)]
    head_dim = width // HEADS
    scale = head_dim ** -0.5

    def attend(pair, carry):
        off = al(pair * 128, 128)
        qp = qkv[:, pl.ds(off, 128)]
        kp = qkv[:, pl.ds(al(half + off, 128), 128)]
        vp = qkv[:, pl.ds(al(2 * half + off, 128), 128)]
        outs = []
        for hh in range(2):
            s = dot(qp * head_mask[hh], kp, NT) * scale
            s = jnp.where(key_live, s, -1e30)
            e = jnp.exp(s - jnp.max(s, -1, keepdims=True))
            pr = (e / jnp.sum(e, -1, keepdims=True)).astype(BF)
            probs[2 * pair + hh] = pr
            outs.append(dot(pr, vp))
        o = jnp.where(low_lanes, outs[0], outs[1])
        mix[:, pl.ds(off, 128)] = o
        mrg[:, pl.ds(off, 128)] = o.astype(BF)
        return carry

    lax.fori_loop(0, half // 128, attend, 0)

    def swap(i):
        return remote(exs.at[i], exr.at[i], e_send.at[i], e_recv.at[i], core)

    loads[3].wait()
    exs[0] = dot(mrg[...], wout[...]).astype(BF)
    swap(0).start()
    n1t[...] = n1[...].T
    eye = lax.broadcasted_iota(jnp.int32, (seq, seq), 0) == lax.broadcasted_iota(jnp.int32, (seq, seq), 1)
    weight_col = jnp.sum(jnp.where(eye, weight_row, 0.0), -1, keepdims=True)
    for trio in first:
        trio[2].wait_recv()
    cs[...] = (cs[...].astype(F32) * weight_col).astype(BF)
    swap(0).wait_recv()

    def residual(i, carry):
        r = rows_of(i)
        res[r, :] = xs[r, :].astype(F32) + exs[0, r, :].astype(F32) + exr[0, r, :].astype(F32) + ob[...]
        return carry

    lax.fori_loop(0, blocks, residual, 0)
    norm(res, g2, b2, u2, inv2, n2)
    n2t[...] = n2[...].T
    loads[4].wait()
    tile = 256
    root_half = 0.5 ** 0.5
    pdf_scale = (2.0 * jnp.pi) ** -0.5

    def hidden(j, carry):
        cols = pl.ds(al(j * tile, 128), tile)
        h = dot(n2[...], w1[:, cols]) + fb1[:, pl.ds(al(ffh_c + j * tile, 128), tile)]
        cdf = 0.5 * (1.0 + lax.erf(h * root_half))
        act[:, cols] = (h * cdf).astype(BF)
        gd[:, cols] = cdf + h * (jnp.exp(-0.5 * h * h) * pdf_scale)
        return carry

    lax.fori_loop(0, ffh // tile, hidden, 0)
    loads[5].wait()

    def grad_two(j, carry):
        cols = pl.ds(al(j * tile, 128), tile)
        l2[cols, :] = (dot(act[:, cols], cs[...], TN) * factor).astype(BF)
        d = dot(cs[...], w2[cols, :], NT) * gd[:, cols]
        low = d.astype(BF)
        gh[:, cols] = low
        row = j // 3
        sv[pl.ds(row, 1), pl.ds(al((j - 3 * row) * tile, 128), tile)] = (
            jnp.sum(low.astype(F32), 0, keepdims=True) * factor
        )
        l1[:, cols] = (dot(n2t[...], low) * factor).astype(BF)
        return carry

    lax.fori_loop(0, ffh // tile, grad_two, 0)
    exs[1] = dot(gh[...], w1[...], NT).astype(BF)
    swap(1).start()
    mps[...] = dot(act[...], w2[...]).astype(BF)

    def seg_rows(s):
        return pl.ds(al(s * slots, slots), slots)

    mlp_sends = [
        remote(mps.at[seg_rows(2 * k + 1 - c)], mpr.at[seg_rows(2 * k + 1 - c)], o_send.at[k], o_recv.at[k], core)
        for k in range(2)
    ]
    for send in mlp_sends:
        send.start()
    swap(1).wait_recv()

    zero_row = jnp.zeros((1, width), F32)

    def norm_back(slot, unit_ref, inv_ref, gain, base):
        def body(i, sums):
            r = rows_of(i)
            g = exs[slot, r, :].astype(F32) + exr[slot, r, :].astype(F32)
            unit = unit_ref[r, :]
            scaled = g * gain[...]
            inner_grad = inv_ref[r, :] * (
                scaled - jnp.mean(scaled, -1, keepdims=True) - unit * jnp.mean(scaled * unit, -1, keepdims=True)
            )
            total = base(r) + inner_grad
            gres[r, :] = total
            low = total.astype(BF)
            ga[r, :] = low
            return (
                sums[0] + jnp.sum(g * unit, 0, keepdims=True),
                sums[1] + jnp.sum(g, 0, keepdims=True),
                sums[2] + jnp.sum(low.astype(F32), 0, keepdims=True),
                sums[3] + jnp.sum(cs[r, :].astype(F32), 0, keepdims=True),
            )
        return lax.fori_loop(0, blocks, body, (zero_row,) * 4)

    def mine(row):
        return jnp.where(c == 0, row[:, :half], row[:, half:]) * factor

    s_gain, s_bias, s_out, s_two = norm_back(1, u2, inv2, g2, lambda r: cs[r, :].astype(F32))
    sv[pl.ds(5, 1), pl.ds(0, half)] = mine(s_gain)
    sv[pl.ds(5, 1), pl.ds(half, half)] = mine(s_bias)
    sv[pl.ds(4, 1), pl.ds(0, half)] = mine(s_out)
    sv[pl.ds(4, 1), pl.ds(half, half)] = mine(s_two)
    sv[pl.ds(6, 2), :] = jnp.zeros((2, width), F32)
    lout[...] = (dot(mrg[...], ga[...], TN) * factor).astype(BF)
    gm[...] = dot(ga[...], wout[...], NT).astype(BF)

    def attend_back(pair, carry):
        off = al(pair * 128, 128)
        offk = al(half + off, 128)
        offv = al(2 * half + off, 128)
        qp = qkv[:, pl.ds(off, 128)]
        kp = qkv[:, pl.ds(offk, 128)]
        vp = qkv[:, pl.ds(offv, 128)]
        gmp = gm[:, pl.ds(off, 128)]
        op = mix[:, pl.ds(off, 128)]
        dq, dk, dv = [], [], []
        for hh in range(2):
            gmh = gmp * head_mask[hh]
            gp = dot(gmh, vp, NT)
            delta = jnp.sum(gmh.astype(F32) * op, -1, keepdims=True)
            pr = probs[2 * pair + hh]
            ds = (pr.astype(F32) * (gp - delta)).astype(BF)
            dq.append(dot(ds, kp))
            dk.append(dot(ds, qp, TN))
            dv.append(dot(pr, gmp, TN))
        gqkv[:, pl.ds(off, 128)] = (jnp.where(low_lanes, dq[0], dq[1]) * scale).astype(BF)
        gqkv[:, pl.ds(offk, 128)] = (jnp.where(low_lanes, dk[0], dk[1]) * scale).astype(BF)
        gqkv[:, pl.ds(offv, 128)] = jnp.where(low_lanes, dv[0], dv[1]).astype(BF)
        return carry

    lax.fori_loop(0, half // 128, attend_back, 0)
    for j in range(3):
        cols = pl.ds(j * half, half)
        lq[:, cols] = (dot(n1t[...], gqkv[:, cols]) * factor).astype(BF)
    sv[pl.ds(2, 1), pl.ds(0, half)] = jnp.sum(gqkv[:, pl.ds(0, half)].astype(F32), 0, keepdims=True) * factor
    sv[pl.ds(2, 1), pl.ds(half, half)] = (
        jnp.sum(gqkv[:, pl.ds(2 * half, half)].astype(F32), 0, keepdims=True) * factor
    )
    exs[2] = dot(gqkv[...], wqkv[...], NT).astype(BF)
    swap(2).start()

    def finish(target, landing, value, sends, sem0):
        for k in range(2):
            val = value(seg_rows(2 * k + c)).astype(BF)
            @pl.when(y == k)
            def _():
                target[y] = val
            @pl.when(y != k)
            def _():
                landing[0] = val
        send = remote(landing.at[0], landing.at[1], o_send.at[sem0], o_recv.at[sem0], ydev)
        send.start()
        return send

    for send in mlp_sends:
        send.wait_recv()
    lo_send = finish(
        lo_out, lo_s,
        lambda r: res[r, :] + mps[r, :].astype(F32) + mpr[r, :].astype(F32) + fb2[...], None, 2,
    )
    swap(2).wait_recv()
    s_gain, s_bias, _, _ = norm_back(2, u1, inv1, g1, lambda r: gres[r, :])
    gt_send = finish(gt_out, gt_s, lambda r: gres[r, :], None, 3)
    sv[pl.ds(3, 1), pl.ds(0, half)] = mine(s_gain)
    sv[pl.ds(3, 1), pl.ds(half, half)] = mine(s_bias)

    def chunk(q):
        return lax.rem(q + 2 * RING, RING)

    streams = []
    for way in (1, -1):
        d = 0 if way == 1 else 1
        for sub in range(2):
            i = 2 * d + sub
            streams.append(Stream(
                way,
                functools.partial(lambda k, i: l2.at[pl.ds(al(k * 192 + 48 * i, 16), 48), :], i=i),
                functools.partial(lambda k, i: f2.at[c, pl.ds(al(k * 192 + 48 * i, 16), 48), :], i=i),
                (r768.at[i], x768.at[i], None), "a", 48, width,
            ))
        streams.append(Stream(
            way,
            functools.partial(lambda k, yy, d: l1.at[pl.ds(al(k * 96 + 48 * d, 16), 48), pl.ds(al(yy * width, 128), width)], d=d),
            functools.partial(lambda k, yy, d: f1.at[c, pl.ds(al(k * 96 + 48 * d, 16), 48), pl.ds(al(yy * width, 128), width)], d=d),
            (r768.at[4 + d], None, y768.at[d]), "b", 48, width,
        ))
        lo, n = (0, 640) if d == 0 else (640, 512)
        streams.append(Stream(
            way,
            functools.partial(lambda k, yy, lo, n: lq.at[pl.ds(al(k * 96 + 48 * yy, 16), 48), pl.ds(lo, n)], lo=lo, n=n),
            functools.partial(lambda k, yy, lo, n: fq.at[c, pl.ds(al(k * 96 + 48 * yy, 16), 48), pl.ds(lo, n)], lo=lo, n=n),
            ((rqn, rqp)[d], None, (yqn, yqp)[d]), "b", 48, n,
        ))
        streams.append(Stream(
            way,
            functools.partial(lambda k, d: lout.at[pl.ds(al(k * 48, 16), 48), pl.ds(half * d, half)], d=d),
            functools.partial(lambda k, d: fo.at[c, pl.ds(al(k * 48, 16), 48), pl.ds(half * d, half)], d=d),
            (r384.at[d], x384.at[d], None), "a", 48, half,
        ))
    streams = [s for pair in zip(streams[:5], streams[5:]) for s in pair]
    for i, s in enumerate(streams):
        s.i = i
        s.dev = nxt if s.way == 1 else prv
    a_streams = [s for s in streams if s.kind == "a"]
    b_streams = [s for s in streams if s.kind == "b"]
    for i, s in enumerate(a_streams):
        s.a = i
    for i, s in enumerate(b_streams):
        s.b = i

    def local(s, k):
        return s.local(k) if s.kind == "a" else s.local(k, y)

    def final(s, k, yy=None):
        return s.final(k) if s.kind == "a" else s.final(k, y if yy is None else yy)

    def rs_chunk(s, step):
        return chunk(p - s.way * (1 + step))

    def y_copy(s, step):
        return remote(
            s.local(rs_chunk(s, step), 1 - y), s.bufs[2].at[step], yb_send.at[s.b, step], yb_recv.at[s.b, step], ydev
        )

    for step in range(RING):
        for s in b_streams:
            y_copy(s, step).start()

    s_own = remote(sv, sg.at[p], s_send.at[0], s_recv.at[0], nxt)
    s_own_back = remote(sv, sg.at[p], s_send.at[1], s_recv.at[1], prv)
    s_own.start()
    s_own_back.start()
    sg[p] = sv[...]

    def rs_send_copy(s, step):
        src = local(s, rs_chunk(s, 0)) if (s.kind == "a" and isinstance(step, int) and step == 0) else s.bufs[0].at[step - 1]
        return src

    def rs_copy(s, src, step):
        return remote(src, s.bufs[0].at[step], rs_send.at[s.i], rs_recv.at[s.i, step], s.dev)

    def gathered(s, step):
        total = local(s, rs_chunk(s, step))[...].astype(F32)
        if s.kind == "b":
            y_copy(s, step).wait_recv()
            total = total + s.bufs[2][step].astype(F32)
        return total

    for s in streams:
        if s.kind == "a":
            rs_copy(s, local(s, rs_chunk(s, 0)), 0).start()
        else:
            s.bufs[2][0] = gathered(s, 0).astype(BF)
            rs_copy(s, s.bufs[2].at[0], 0).start()

    def rs_step(step, carry):
        for s in streams:
            total = gathered(s, step)
            rs_copy(s, s.bufs[0].at[step - 1], step - 1).wait()
            s.bufs[0][step - 1] = (total + s.bufs[0][step - 1].astype(F32)).astype(BF)
            rs_copy(s, s.bufs[0].at[step - 1], step).start()
        return carry

    lax.fori_loop(1, RING - 1, rs_step, 0)
    last = RING - 2
    ya = [remote(s.bufs[0].at[last], s.bufs[1], ya_send.at[s.a], ya_recv.at[s.a], ydev) for s in a_streams]
    for s in streams:
        total = gathered(s, RING - 1)
        rs_copy(s, s.bufs[0].at[last], last).wait()
        total = (total + s.bufs[0][last].astype(F32)).astype(BF)
        if s.kind == "a":
            s.bufs[0][last] = total
            ya[s.a].start()
        else:
            final(s, p)[...] = total
    for s in a_streams:
        ya[s.a].wait()
        final(s, p)[...] = (s.bufs[0][last].astype(F32) + s.bufs[1][...].astype(F32)).astype(BF)

    if groups > 1:
        for s in streams:
            slot = gsh.at[s.i, :, :, pl.ds(0, s.cols)]
            slot[group] = final(s, p)[...]
            sends = [
                remote(slot.at[group], slot.at[group], g_send.at[s.i, j], g_recv.at[s.i, j], dev)
                for j, dev in enumerate(others)
            ]
            for send in sends:
                send.start()
            for send in sends:
                send.wait()
            total = slot[0].astype(F32)
            for j in range(1, groups):
                total = total + slot[j].astype(F32)
            final(s, p)[...] = total.astype(BF)

    def ag_chunk(s, step):
        return chunk(p - s.way * step)

    def ag_copy(s, step):
        here = final(s, ag_chunk(s, step))
        return remote(here, here, ag_send.at[s.i], ag_recv.at[s.i, step], s.dev)

    def yg_copy(s, step):
        here = final(s, ag_chunk(s, step))
        return remote(here, here, yg_send.at[s.b, step], yg_recv.at[s.b, step], ydev)

    def core_copy(s, step, yy=None):
        here = final(s, ag_chunk(s, step), yy)
        n = 0 if yy is None else 1
        return remote(here, here, c_send.at[n, s.i, step], c_recv.at[n, s.i, step], core)

    def spread(s, step):
        core_copy(s, step).start()
        if s.kind == "b":
            yg_copy(s, step).start()

    for s in b_streams + a_streams:
        ag_copy(s, 0).start()
        spread(s, 0)

    def y_arrived(s, step):
        yg_copy(s, step).wait_recv()
        core_copy(s, step, 1 - y).start()

    def ag_step(step, carry):
        for s in b_streams + a_streams:
            ag_copy(s, step - 1).wait()
            ag_copy(s, step).start()
            spread(s, step)
            if s.kind == "b":
                y_arrived(s, step - 1)
        return carry

    lax.fori_loop(1, RING - 1, ag_step, 0)
    for s in b_streams + a_streams:
        ag_copy(s, last).wait()
        spread(s, RING - 1)
        if s.kind == "b":
            y_arrived(s, last)
    for s in b_streams:
        y_arrived(s, RING - 1)

    s_own.wait()
    s_own_back.wait()
    for step in range(1, RING // 2):
        onward = remote(sg.at[chunk(p - step)], sg.at[chunk(p - step)], s_send.at[0], s_recv.at[1 + step], nxt)
        onward.start()
        if step < RING // 2 - 1:
            back = remote(sg.at[chunk(p + step)], sg.at[chunk(p + step)], s_send.at[1], s_recv.at[4 + step], prv)
            back.start()
            back.wait()
        onward.wait()
    total = sg[0]
    for k in range(1, RING):
        total = total + sg[k]
    sy[0] = total
    y_small = remote(sy.at[0], sy.at[1], s_send.at[2], s_recv.at[8], ydev)
    y_small.start()
    y_small.wait()
    total = sy[0] + sy[1]
    if groups > 1:
        gsv[group] = total
        sends = [
            remote(gsv.at[group], gsv.at[group], g_send.at[len(streams), j], g_recv.at[len(streams), j], dev)
            for j, dev in enumerate(others)
        ]
        for send in sends:
            send.start()
        for send in sends:
            send.wait()
        total = gsv[0]
        for j in range(1, groups):
            total = total + gsv[j]
    sall[c] = total
    core_small = remote(sall.at[c], sall.at[c], s_send.at[3], s_recv.at[9], core)
    core_small.start()
    core_small.wait()

    lo_send.wait()
    lo_out[1 - y] = lo_s[1]
    gt_send.wait()
    gt_out[1 - y] = gt_s[1]

    for trio in first:
        for copy in trio:
            copy.wait_send()
    for i in range(3):
        swap(i).wait_send()
    for send in mlp_sends:
        send.wait_send()

    def drain(step, carry):
        for s in b_streams:
            y_copy(s, step).wait_send()
            yg_copy(s, step).wait_send()
            core_copy(s, step, 1 - y).wait()
        for s in streams:
            core_copy(s, step).wait()
        return carry

    lax.fori_loop(0, RING, drain, 0)


def write_kernel(f2, f1, fq, fo, sall, o_ln1g, o_ln1b, o_qkv, o_qb, o_vb, o_out, o_ob, o_ln2g, o_ln2b, o_fc1, o_fb1, o_fc2, o_fb2, stage, sems):
    width = f2.shape[2]
    half = width // 2
    ffh = f2.shape[1]
    n_buf = stage.shape[0]
    jobs = []
    for c in range(2):
        for k in range(ffh // 192):
            jobs.append((f2, (c, 192 * k, 192, 0, width), lambda c=c, k=k: o_fc2.at[pl.ds(c * ffh + 192 * k, 192), :]))
        for k in range(width // 192):
            for h in range(2):
                jobs.append((f1, (c, 192 * k, 192, width * h, width), lambda c=c, k=k, h=h: o_fc1.at[pl.ds(192 * k, 192), pl.ds(c * ffh + width * h, width)]))
            for j in range(3):
                jobs.append((fq, (c, 192 * k, 192, half * j, half), lambda c=c, k=k, j=j: o_qkv.at[pl.ds(192 * k, 192), pl.ds(j * width + c * half, half)]))
        for k in range(half // 192):
            jobs.append((fo, (c, 192 * k, 192, 0, width), lambda c=c, k=k: o_out.at[pl.ds(c * half + 192 * k, 192), :]))
    copies = []
    for i, (src, (c, row, rows, col, cols), target) in enumerate(jobs):
        slot = i % n_buf
        if i >= n_buf:
            copies[i - n_buf].wait()
        stage[slot, :, pl.ds(0, cols)] = src[c, pl.ds(row, rows), pl.ds(col, cols)].astype(F32)
        copy = pltpu.make_async_copy(stage.at[slot, :, pl.ds(0, cols)], target(), sems.at[slot])
        copy.start()
        copies.append(copy)
    for c in range(2):
        here = pl.ds(c * half, half)
        o_fb1[:, pl.ds(c * ffh, width)] = sall[c, 0:1, :]
        o_fb1[:, pl.ds(c * ffh + width, width)] = sall[c, 1:2, :]
        for row, lo, hi in ((2, o_qb, o_vb), (3, o_ln1g, o_ln1b), (4, o_ob, o_fb2), (5, o_ln2g, o_ln2b)):
            lo[:, here] = sall[c, row : row + 1, pl.ds(0, half)]
            hi[:, here] = sall[c, row : row + 1, pl.ds(half, half)]
    for copy in copies[-n_buf:]:
        copy.wait()


def shards(n_wide, tokens, cotangent, row_counts, mask_flags, ln1_gain, ln1_bias, w_qkv, q_bias, v_bias, w_out, out_bias, ln2_gain, ln2_bias, w_fc1, fc1_bias, w_fc2, fc2_bias):
    images, slots, width = tokens.shape
    ff = w_fc1.shape[1]
    n_blk = lax.axis_size("blk")
    seq, half, ffh = slots * n_blk, width // 2, ff // 2
    groups = n_wide // RING
    factor = float(images * slots * n_wide * n_blk) ** -0.5
    row = lambda v: v.reshape(1, -1)
    vm, dma = pltpu.VMEM, pltpu.SemaphoreType.DMA
    vspec, anyspec = pl.BlockSpec(memory_space=pltpu.VMEM), pl.BlockSpec(memory_space=pl.ANY)
    n_heads = HEADS // 2
    scratch = [
        vm((width, 3 * half), BF), vm((half, width), BF), vm((width, ffh), BF), vm((ffh, width), BF),
        vm((seq, width), BF), vm((seq, width), BF), vm((6, 8, 128), F32),
        vm((seq, width), BF), vm((width, seq), BF), vm((seq, width), F32), vm((seq, 1), F32),
        vm((seq, 3 * half), BF), vm((n_heads, seq, seq), BF), vm((seq, half), F32), vm((seq, half), BF),
        vm((3, seq, width), BF), vm((3, seq, width), BF), vm((seq, width), F32),
        vm((seq, width), BF), vm((width, seq), BF), vm((seq, width), F32), vm((seq, 1), F32),
        vm((seq, ffh), BF), vm((seq, ffh), F32), vm((seq, ffh), BF), vm((seq, width), F32), vm((seq, width), BF),
        vm((seq, half), BF), vm((seq, 3 * half), BF), vm((seq, width), BF), vm((seq, width), BF),
        vm((2, slots, width), BF), vm((2, slots, width), BF),
        vm((RING, 8, width), F32), vm((2, 8, width), F32), vm((8, width), F32),
        vm((ffh, width), BF), vm((width, ffh), BF), vm((width, 3 * half), BF), vm((half, width), BF),
        vm((6, RING - 1, 48, width), BF), vm((2, RING - 1, 48, half), BF),
        vm((RING - 1, 48, 640), BF), vm((RING - 1, 48, 512), BF),
        vm((2, RING, 48, width), BF), vm((RING, 48, 640), BF), vm((RING, 48, 512), BF),
        vm((4, 48, width), BF), vm((2, 48, half), BF),
        vm((10, groups, 48, width) if groups > 1 else (1, 1, 16, 128), BF),
        vm((groups, 8, width) if groups > 1 else (1, 8, 128), F32),
        dma((6,)), dma((9,)), dma((9,)), dma((3,)), dma((3,)), dma((4,)), dma((4,)),
        dma((10,)), dma((10, RING - 1)), dma((4, RING)), dma((4, RING)), dma((6,)), dma((6,)),
        dma((10,)), dma((10, RING - 1)), dma((4, RING)), dma((4, RING)),
        dma((2, 10, RING)), dma((2, 10, RING)), dma((4,)), dma((10,)),
        dma((11, max(groups - 1, 1))), dma((11, max(groups - 1, 1))),
    ]
    outs = [
        jax.ShapeDtypeStruct(tokens.shape, BF), jax.ShapeDtypeStruct(tokens.shape, BF),
        vm((2, ffh, width), BF), vm((2, width, ffh), BF), vm((2, width, 3 * half), BF), vm((2, half, width), BF),
        vm((2, 8, width), F32),
    ]
    lo, gt, f2, f1, fq, fo, sall = pl.pallas_call(
        functools.partial(layer_kernel, n_wide, factor),
        out_shape=outs,
        in_specs=[vspec] * 13 + [anyspec] * 4,
        out_specs=[vspec] * 7,
        scratch_shapes=scratch,
        compiler_params=pltpu.CompilerParams(collective_id=0, has_side_effects=True, vmem_limit_bytes=46 * 2**20),
        name="layer",
    )(
        tokens, cotangent, row_counts, mask_flags, row(ln1_gain), row(ln1_bias), row(q_bias), row(v_bias), row(out_bias),
        row(ln2_gain), row(ln2_bias), row(fc1_bias), row(fc2_bias), w_qkv, w_out, w_fc1, w_fc2,
    )
    vec = jax.ShapeDtypeStruct((1, width), F32)
    mat = lambda *shape: jax.ShapeDtypeStruct(shape, F32)
    n_buf = 6
    grads = pl.pallas_call(
        write_kernel,
        out_shape=[vec, vec, mat(width, 3 * width), vec, vec, mat(width, width), vec, vec, vec, mat(width, ff), mat(1, ff), mat(ff, width), vec],
        in_specs=[vspec] * 5,
        out_specs=[vspec, vspec, anyspec, vspec, vspec, anyspec, vspec, vspec, vspec, anyspec, vspec, anyspec, vspec],
        scratch_shapes=[vm((n_buf, 192, width), F32), dma((n_buf,))],
        compiler_params=pltpu.CompilerParams(vmem_limit_bytes=8 * 2**20),
        name="write",
    )(f2, f1, fq, fo, sall)
    return (lo, gt) + tuple(g.reshape(-1) if g.shape[0] == 1 else g for g in grads)


def solution(mesh):
    rows, whole = P("wide", "blk", None), P()
    return jax.shard_map(
        functools.partial(shards, mesh.shape["wide"]),
        mesh=mesh,
        in_specs=(rows, rows, P("wide", "blk"), P("wide", "blk")) + (whole,) * 13,
        out_specs=(rows, rows) + (whole,) * 13,
        check_vma=False,
    )
```

```python
import functools

import jax
import jax.numpy as jnp
from jax import lax
from jax.experimental import pallas as pl
from jax.experimental.pallas import tpu as pltpu
from jax.sharding import PartitionSpec as P

HEADS = 12
ROW_LEN = 14
EPS = 1e-06
RING = 8
BF = jnp.bfloat16
F32 = jnp.float32
MESH = pl.DeviceIdType.MESH
NT = (((1,), (1,)), ((), ()))
TN = (((0,), (0,)), ((), ()))


def dot(a, b, dims=(((1,), (0,)), ((), ()))):
    return lax.dot_general(a, b, dims, preferred_element_type=F32)


def ring_place(r):
    return jnp.where(r % 2 == 0, r // 2, RING - 1 - r // 2)


def ring_member(q):
    return jnp.where(q < RING // 2, 2 * q, 2 * RING - 1 - 2 * q)


def al(v, m):
    return pl.multiple_of(v, m)


class Stream:
    def __init__(self, way, dev, kind, start, gather, local, final, bufs, other):
        self.way, self.dev, self.kind, self.start, self.gather = way, dev, kind, start, gather
        self.local, self.final, self.bufs, self.other = local, final, bufs, other


START = {"fc2": 0, "fc1": 2, "out": 3, "qkv": 5}
GATHER = {"fc2": 11, "fc1": 9, "out": 12, "qkv": 12}
SMALL = 8
LOOP = 5
AHEAD = 2


def ORDER(two, one, qkv, out):
    return one + qkv + two + out


def layer_kernel(n_wide, factor, *refs):
    (
        tok, cot, counts, flags, g1_h, b1_h, qb_h, vb_h, ob_h, g2_h, b2_h, fb2_h, fb1_h, wqkv_h, wout_h, w1_h, w2_h,
        lo_out, gt_out, f2, f1, fq, fo, sall,
        wqkv, wout, w1, w2, xs, cs, meta, n1, n1t, u1, inv1, qkv, probs, mix, mrg, exs, exr, res, n2, n2t, u2, inv2,
        act, gd, gh, gres, ga, gm, gqkv, mps, mpr, lo_s, gt_s, sg, sy, sv,
        l2, l1, lq, lout, r96, r48, r384, rqn, rqp, y48, yqn, yqp, x96, x384, gsh, gsv,
        vecs, w_sem, v_sem, t_send, t_recv, e_send, e_recv, o_send, o_recv,
        rs_send, rs_recv, yb_send, yb_recv, ya_send, ya_recv, ag_send, ag_recv, yg_send, yg_recv,
        c_send, c_recv, s_send, s_recv, g_send, g_recv,
    ) = refs
    groups = n_wide // RING
    seq, width = xs.shape
    half = width // 2
    ffh = w1.shape[1]
    slots = seq // 4
    w = lax.axis_index("wide")
    b = lax.axis_index("blk")
    y, c = b // 2, b % 2
    group, inner = w // RING, w % RING
    p = ring_place(inner)

    def at_place(q):
        return (group * RING + ring_member(lax.rem(q + RING, RING)), b)

    nxt, prv = at_place(p + 1), at_place(p - 1)
    core = (w, 2 * y + 1 - c)
    ydev = (w, 2 * (1 - y) + c)
    ydiag = (w, 2 * (1 - y) + 1 - c)
    others = [(lax.rem(group + j, groups) * RING + inner, b) for j in range(1, groups)]

    bar = pltpu.get_barrier_semaphore()
    greeted = [core, ydev, ydiag, nxt, prv] + others
    for dev in greeted:
        pl.semaphore_signal(bar, inc=1, device_id=dev, device_id_type=MESH)
    half_c = al(c * half, 128)
    ffh_c = al(c * ffh, 128)
    loads = [
        pltpu.make_async_copy(wqkv_h.at[:, pl.ds(al(j * width + c * half, 128), half)], wqkv.at[:, pl.ds(j * half, half)], w_sem.at[j])
        for j in range(3)
    ] + [
        pltpu.make_async_copy(wout_h.at[pl.ds(half_c, half), :], wout, w_sem.at[3]),
        pltpu.make_async_copy(w1_h.at[:, pl.ds(ffh_c, ffh)], w1, w_sem.at[4]),
        pltpu.make_async_copy(w2_h.at[pl.ds(ffh_c, ffh), :], w2, w_sem.at[5]),
    ]
    small_loads = [
        pltpu.make_async_copy(vec, vecs.at[i], v_sem.at[i])
        for i, vec in enumerate((g1_h, b1_h, qb_h, vb_h, ob_h, g2_h, b2_h, fb2_h))
    ] + [
        pltpu.make_async_copy(fb1_h.at[pl.ds(i * width, width)], vecs.at[8 + i], v_sem.at[8 + i]) for i in range(2 * ffh // width)
    ]
    g1, b1, qb, vb, ob, g2, b2, fb2 = (vecs.at[pl.ds(i, 1), :] for i in range(8))
    for load in small_loads + loads:
        load.start()

    def remote(src, dst, send, recv, dev):
        return pltpu.make_async_remote_copy(
            src_ref=src, dst_ref=dst, send_sem=send, recv_sem=recv, device_id=dev, device_id_type=MESH
        )

    lane64 = lax.broadcasted_iota(jnp.int32, (1, slots), 1)
    zero64 = jnp.zeros((1, slots), F32)
    for img in range(2):
        live = (lane64 < counts[:, pl.ds(img, 1)] * ROW_LEN).astype(F32)
        weight = live * flags[pl.ds(img, 1), :].astype(F32)
        for row, val in ((0, live), (1, weight)):
            low = jnp.concatenate([val, zero64], 1)
            high = jnp.concatenate([zero64, val], 1)
            meta[4 + img, pl.ds(row, 1), :] = jnp.where(c == 0, low, high)
    seg = al(b * slots, slots)
    xs[pl.ds(seg, slots), :] = tok[y]
    cs[pl.ds(seg, slots), :] = cot[y]
    meta[b] = meta[4 + y]

    pl.semaphore_wait(bar, len(greeted))
    first = []
    for i, (dev, img) in enumerate(((core, y), (ydev, 1 - y), (ydiag, 1 - y))):
        first.append([
            remote(meta.at[4 + img], meta.at[b], t_send.at[3 * i], t_recv.at[3 * i], dev),
            remote(tok.at[img], xs.at[pl.ds(seg, slots), :], t_send.at[3 * i + 1], t_recv.at[3 * i + 1], dev),
            remote(cot.at[img], cs.at[pl.ds(seg, slots), :], t_send.at[3 * i + 2], t_recv.at[3 * i + 2], dev),
        ])
    for kind in range(3):
        for trio in first:
            trio[kind].start()
    for kind in range(2):
        for trio in first:
            trio[kind].wait_recv()

    def chunk(q):
        return lax.rem(q + 2 * RING, RING)

    def streams_of(way):
        d = 0 if way == 1 else 1
        dev = nxt if way == 1 else prv
        lo, n = (0, 640) if d == 0 else (640, 512)
        return [
            Stream(
                way, dev, "a", START["fc2"], GATHER["fc2"],
                lambda k, yy: l2.at[pl.ds(al(k * 192 + 96 * d, 16), 96), :],
                lambda k, yy: f2.at[c, pl.ds(al(k * 192 + 96 * d, 16), 96), :],
                r96.at[d], x96.at[d],
            ),
            Stream(
                way, dev, "b", START["fc1"], GATHER["fc1"],
                lambda k, yy: l1.at[pl.ds(al(k * 96 + 48 * d, 16), 48), pl.ds(al(yy * width, 128), width)],
                lambda k, yy: f1.at[c, pl.ds(al(k * 96 + 48 * d, 16), 48), pl.ds(al(yy * width, 128), width)],
                r48.at[d], y48.at[d],
            ),
            Stream(
                way, dev, "b", START["qkv"], GATHER["qkv"],
                lambda k, yy: lq.at[pl.ds(al(k * 96 + 48 * yy, 16), 48), pl.ds(lo, n)],
                lambda k, yy: fq.at[c, pl.ds(al(k * 96 + 48 * yy, 16), 48), pl.ds(lo, n)],
                (rqn, rqp)[d], (yqn, yqp)[d],
            ),
            Stream(
                way, dev, "a", START["out"], GATHER["out"],
                lambda k, yy: lout.at[pl.ds(al(k * 48, 16), 48), pl.ds(half * d, half)],
                lambda k, yy: fo.at[c, pl.ds(al(k * 48, 16), 48), pl.ds(half * d, half)],
                r384.at[d], x384.at[d],
            ),
        ]

    streams = [s for pair in zip(streams_of(1), streams_of(-1)) for s in pair]
    for kind in "ab":
        for i, s in enumerate(s for s in streams if s.kind == kind):
            s.k = i
    for i, s in enumerate(streams):
        s.i = i
    st2, st1, stq, sto = streams[0:2], streams[2:4], streams[4:6], streams[6:8]
    b_streams = st1 + stq
    last = RING - 2

    def rs_chunk(s, step):
        return chunk(p - s.way * (1 + step))

    def y_copy(s, step):
        return remote(s.local(rs_chunk(s, step), 1 - y), s.other.at[step], yb_send.at[s.k], yb_recv.at[s.k, step], ydev)

    def rs_copy(s, src, step):
        return remote(src, s.bufs.at[step], rs_send.at[s.i], rs_recv.at[s.i, step], s.dev)

    def own(s, step):
        total = s.local(rs_chunk(s, step), y)[...].astype(F32)
        if s.kind == "b":
            y_copy(s, step).wait_recv()
            total = total + s.other[step].astype(F32)
        return total

    def rs_first(s):
        if s.kind == "a":
            rs_copy(s, s.local(rs_chunk(s, 0), y), 0).start()
        else:
            s.other[0] = own(s, 0).astype(BF)
            rs_copy(s, s.other.at[0], 0).start()

    def rs_add(s, step):
        total = own(s, step)
        rs_copy(s, s.bufs.at[step - 1], step - 1).wait()
        s.bufs[step - 1] = (total + s.bufs[step - 1].astype(F32)).astype(BF)

    def rs_step(s, step):
        rs_add(s, step)
        rs_copy(s, s.bufs.at[step - 1], step).start()

    def y_ahead(s, step):
        if s.kind == "b":
            y_copy(s, step).start()

    def ya_copy(s):
        return remote(s.bufs.at[last], s.other, ya_send.at[s.k], ya_recv.at[s.k], ydev)

    def rs_end(s):
        rs_add(s, RING - 1)
        if s.kind == "a":
            ya_copy(s).start()
        else:
            s.final(p, y)[...] = s.bufs[last]

    def over_groups(s):
        piece = s.final(p, y)
        slot = gsh.at[s.i, :, pl.ds(0, piece.shape[0]), pl.ds(0, piece.shape[1])]
        slot[group] = piece[...]
        sends = [
            remote(slot.at[group], slot.at[group], g_send.at[s.i, j], g_recv.at[s.i, j], dev) for j, dev in enumerate(others)
        ]
        for send in sends:
            send.start()
        for send in sends:
            send.wait()
        total = slot[0].astype(F32)
        for j in range(1, groups):
            total = total + slot[j].astype(F32)
        piece[...] = total.astype(BF)

    def ag_chunk(s, step):
        return chunk(p - s.way * step)

    def ag_copy(s, step):
        here = s.final(ag_chunk(s, step), y)
        return remote(here, here, ag_send.at[s.i], ag_recv.at[s.i, step], s.dev)

    def yg_copy(s, step):
        here = s.final(ag_chunk(s, step), y)
        return remote(here, here, yg_send.at[s.k], yg_recv.at[s.k, step], ydev)

    def core_copy(s, step, yy):
        here = s.final(ag_chunk(s, step), yy)
        return remote(here, here, c_send.at[s.i // 2], c_recv.at[s.i // 2], core)

    def spread(s, step):
        core_copy(s, step, y).start()
        if s.kind == "b":
            yg_copy(s, step).start()

    def y_arrived(s, step):
        if s.kind == "b":
            yg_copy(s, step).wait_recv()
            core_copy(s, step, 1 - y).start()

    def ag_first(s):
        if s.kind == "a":
            ya_copy(s).wait()
            s.final(p, y)[...] = (s.bufs[last].astype(F32) + s.other[...].astype(F32)).astype(BF)
        if groups > 1:
            over_groups(s)
        ag_copy(s, 0).start()
        spread(s, 0)

    def ag_step(s, step):
        ag_copy(s, step - 1).wait()
        ag_copy(s, step).start()
        spread(s, step)
        y_arrived(s, step - 1)

    def ag_end(s):
        ag_copy(s, last).wait()
        spread(s, RING - 1)
        y_arrived(s, last)

    def s_copy(k, way):
        at = chunk(p - way * k)
        return remote(sg.at[at], sg.at[at], s_send.at[0 if way == 1 else 1], s_recv.at[k if way == 1 else 4 + k], nxt if way == 1 else prv)

    def s_ring(k):
        if k == 0:
            sg[p] = sv[...]
        if k > 0:
            s_copy(k - 1, 1).wait()
        if 0 < k < RING // 2:
            s_copy(k - 1, -1).wait()
        if k < RING // 2:
            s_copy(k, 1).start()
        if k < RING // 2 - 1:
            s_copy(k, -1).start()

    def s_over_y():
        return remote(sy.at[0], sy.at[1], s_send.at[2], s_recv.at[8], ydev)

    def s_over_core():
        return remote(sall.at[c], sall.at[c], s_send.at[3], s_recv.at[9], core)

    def s_sum():
        s_ring(RING // 2)
        total = sg[0]
        for k in range(1, RING):
            total = total + sg[k]
        sy[0] = total
        s_over_y().start()

    def s_last():
        s_over_y().wait()
        total = sy[0] + sy[1]
        if groups > 1:
            gsv[group] = total
            sends = [
                remote(gsv.at[group], gsv.at[group], g_send.at[len(streams), j], g_recv.at[len(streams), j], dev)
                for j, dev in enumerate(others)
            ]
            for send in sends:
                send.start()
            for send in sends:
                send.wait()
            total = gsv[0]
            for j in range(1, groups):
                total = total + gsv[j]
        sall[c] = total
        s_over_core().start()

    def when(cond, fn):
        if isinstance(cond, bool):
            if cond:
                fn()
        else:
            pl.when(cond)(fn)

    def both(*conds):
        if all(isinstance(v, bool) for v in conds):
            return all(conds)
        return functools.reduce(jnp.logical_and, conds)

    def tick(t):
        for s in ORDER(st2, st1, stq, sto):
            step = t - s.start
            when(step == 0, lambda s=s: rs_first(s))
            when(both(step >= 1, step <= last), lambda s=s, step=step: rs_step(s, step))
            when(step == RING - 1, lambda s=s: rs_end(s))
            if s.kind == "b":
                when(both(step >= 0, step < RING - AHEAD), lambda s=s, step=step: y_ahead(s, step + AHEAD))
            step = t - s.gather
            when(step == 0, lambda s=s: ag_first(s))
            when(both(step >= 1, step <= last), lambda s=s, step=step: ag_step(s, step))
            when(step == RING - 1, lambda s=s: ag_end(s))
            if s.kind == "b":
                when(step == RING, lambda s=s: y_arrived(s, RING - 1))
        if not isinstance(t, int):
            for k in range(RING // 2):
                when(t == SMALL + k, lambda k=k: s_ring(k))
            when(t == SMALL + RING // 2, s_sum)
            when(t == SMALL + RING // 2 + 1, s_last)

    blocks = seq // 64

    def rows_of(i):
        return pl.ds(al(i * 64, 64), 64)

    def norm(src, gain, bias, unit_ref, inv_ref, out):
        def body(i, carry):
            r = rows_of(i)
            v = src[r, :].astype(F32)
            cen = v - jnp.mean(v, -1, keepdims=True)
            inv = lax.rsqrt(jnp.mean(cen * cen, -1, keepdims=True) + EPS)
            unit = cen * inv
            unit_ref[r, :] = unit
            inv_ref[r, :] = inv
            out[r, :] = (unit * gain[...] + bias[...]).astype(BF)
            return carry
        lax.fori_loop(0, blocks, body, 0)

    for load in small_loads:
        load.wait()
    norm(xs, g1, b1, u1, inv1, n1)
    loads[0].wait()
    loads[1].wait()
    loads[2].wait()
    qkv[:, pl.ds(0, half)] = (dot(n1[...], wqkv[:, pl.ds(0, half)]) + qb[:, pl.ds(half_c, half)]).astype(BF)
    qkv[:, pl.ds(half, half)] = dot(n1[...], wqkv[:, pl.ds(half, half)]).astype(BF)
    qkv[:, pl.ds(2 * half, half)] = (
        dot(n1[...], wqkv[:, pl.ds(2 * half, half)]) + vb[:, pl.ds(half_c, half)]
    ).astype(BF)

    live_row = jnp.concatenate([meta[0, 0:1, :] + meta[1, 0:1, :], meta[2, 0:1, :] + meta[3, 0:1, :]], 1)
    weight_row = jnp.concatenate([meta[0, 1:2, :] + meta[1, 1:2, :], meta[2, 1:2, :] + meta[3, 1:2, :]], 1)
    key_live = live_row > 0.5
    lane = lax.broadcasted_iota(jnp.int32, (1, 128), 1)
    low_lanes = lane < 64
    head_mask = [low_lanes.astype(BF), (lane >= 64).astype(BF)]
    head_dim = width // HEADS
    scale = head_dim ** -0.5

    def attend(pair, carry):
        off = al(pair * 128, 128)
        qp = qkv[:, pl.ds(off, 128)]
        kp = qkv[:, pl.ds(al(half + off, 128), 128)]
        vp = qkv[:, pl.ds(al(2 * half + off, 128), 128)]
        outs = []
        for hh in range(2):
            s = dot(qp * head_mask[hh], kp, NT) * scale
            s = jnp.where(key_live, s, -1e30)
            e = jnp.exp(s - jnp.max(s, -1, keepdims=True))
            pr = (e / jnp.sum(e, -1, keepdims=True)).astype(BF)
            probs[2 * pair + hh] = pr
            outs.append(dot(pr, vp))
        o = jnp.where(low_lanes, outs[0], outs[1])
        mix[:, pl.ds(off, 128)] = o
        mrg[:, pl.ds(off, 128)] = o.astype(BF)
        return carry

    lax.fori_loop(0, half // 128, attend, 0)

    def swap(i):
        return remote(exs.at[i], exr.at[i], e_send.at[i], e_recv.at[i], core)

    loads[3].wait()
    exs[0] = dot(mrg[...], wout[...]).astype(BF)
    swap(0).start()
    n1t[...] = n1[...].T
    eye = lax.broadcasted_iota(jnp.int32, (seq, seq), 0) == lax.broadcasted_iota(jnp.int32, (seq, seq), 1)
    weight_col = jnp.sum(jnp.where(eye, weight_row, 0.0), -1, keepdims=True)
    for trio in first:
        trio[2].wait_recv()
    cs[...] = (cs[...].astype(F32) * weight_col).astype(BF)
    swap(0).wait_recv()

    def residual(i, carry):
        r = rows_of(i)
        res[r, :] = xs[r, :].astype(F32) + exs[0, r, :].astype(F32) + exr[0, r, :].astype(F32) + ob[...]
        return carry

    lax.fori_loop(0, blocks, residual, 0)
    norm(res, g2, b2, u2, inv2, n2)
    n2t[...] = n2[...].T
    loads[4].wait()
    tile = 256
    root_half = 0.5 ** 0.5
    pdf_scale = (2.0 * jnp.pi) ** -0.5

    def hidden(j, carry):
        cols = pl.ds(al(j * tile, 128), tile)
        h = dot(n2[...], w1[:, cols]) + vecs[pl.ds(8 + 2 * c + j // 3, 1), pl.ds(al((j - 3 * (j // 3)) * tile, 128), tile)]
        cdf = 0.5 * (1.0 + lax.erf(h * root_half))
        act[:, cols] = (h * cdf).astype(BF)
        gd[:, cols] = cdf + h * (jnp.exp(-0.5 * h * h) * pdf_scale)
        return carry

    lax.fori_loop(0, ffh // tile, hidden, 0)
    loads[5].wait()

    def grad_fc2(j, carry):
        cols = pl.ds(al(j * tile, 128), tile)
        l2[cols, :] = (dot(act[:, cols], cs[...], TN) * factor).astype(BF)
        return carry

    lax.fori_loop(0, ffh // tile, grad_fc2, 0)
    tick(0)

    def grad_hidden(j, carry):
        cols = pl.ds(al(j * tile, 128), tile)
        d = dot(cs[...], w2[cols, :], NT) * gd[:, cols]
        low = d.astype(BF)
        gh[:, cols] = low
        row = j // 3
        sv[pl.ds(row, 1), pl.ds(al((j - 3 * row) * tile, 128), tile)] = (
            jnp.sum(low.astype(F32), 0, keepdims=True) * factor
        )
        return carry

    def grad_fc1(j, carry):
        cols = pl.ds(al(j * tile, 128), tile)
        l1[:, cols] = (dot(n2t[...], gh[:, cols]) * factor).astype(BF)
        return carry

    lax.fori_loop(0, ffh // tile, grad_hidden, 0)
    exs[1] = dot(gh[...], w1[...], NT).astype(BF)
    swap(1).start()
    lax.fori_loop(0, ffh // tile, grad_fc1, 0)
    for step in range(AHEAD):
        for s in st1:
            y_ahead(s, step)
    tick(1)
    mps[...] = dot(act[...], w2[...]).astype(BF)

    def seg_rows(s):
        return pl.ds(al(s * slots, slots), slots)

    mlp_sends = [
        remote(mps.at[seg_rows(2 * k + 1 - c)], mpr.at[seg_rows(2 * k + 1 - c)], o_send.at[k], o_recv.at[k], core)
        for k in range(2)
    ]
    for send in mlp_sends:
        send.start()
    swap(1).wait_recv()

    zero_row = jnp.zeros((1, width), F32)

    def norm_back(slot, unit_ref, inv_ref, gain, base):
        def body(i, sums):
            r = rows_of(i)
            g = exs[slot, r, :].astype(F32) + exr[slot, r, :].astype(F32)
            unit = unit_ref[r, :]
            scaled = g * gain[...]
            inner_grad = inv_ref[r, :] * (
                scaled - jnp.mean(scaled, -1, keepdims=True) - unit * jnp.mean(scaled * unit, -1, keepdims=True)
            )
            total = base(r) + inner_grad
            gres[r, :] = total
            low = total.astype(BF)
            ga[r, :] = low
            return (
                sums[0] + jnp.sum(g * unit, 0, keepdims=True),
                sums[1] + jnp.sum(g, 0, keepdims=True),
                sums[2] + jnp.sum(low.astype(F32), 0, keepdims=True),
                sums[3] + jnp.sum(cs[r, :].astype(F32), 0, keepdims=True),
            )
        return lax.fori_loop(0, blocks, body, (zero_row,) * 4)

    def mine(row):
        return jnp.where(c == 0, row[:, :half], row[:, half:]) * factor

    s_gain, s_bias, s_out, s_two = norm_back(1, u2, inv2, g2, lambda r: cs[r, :].astype(F32))
    sv[pl.ds(5, 1), pl.ds(0, half)] = mine(s_gain)
    sv[pl.ds(5, 1), pl.ds(half, half)] = mine(s_bias)
    sv[pl.ds(4, 1), pl.ds(0, half)] = mine(s_out)
    sv[pl.ds(4, 1), pl.ds(half, half)] = mine(s_two)
    sv[pl.ds(6, 2), :] = jnp.zeros((2, width), F32)
    lout[...] = (dot(mrg[...], ga[...], TN) * factor).astype(BF)
    gm[...] = dot(ga[...], wout[...], NT).astype(BF)
    tick(2)

    def attend_back(pair, carry):
        off = al(pair * 128, 128)
        offk = al(half + off, 128)
        offv = al(2 * half + off, 128)
        qp = qkv[:, pl.ds(off, 128)]
        kp = qkv[:, pl.ds(offk, 128)]
        vp = qkv[:, pl.ds(offv, 128)]
        gmp = gm[:, pl.ds(off, 128)]
        op = mix[:, pl.ds(off, 128)]
        dq, dk, dv = [], [], []
        for hh in range(2):
            gmh = gmp * head_mask[hh]
            gp = dot(gmh, vp, NT)
            delta = jnp.sum(gmh.astype(F32) * op, -1, keepdims=True)
            pr = probs[2 * pair + hh]
            ds = (pr.astype(F32) * (gp - delta)).astype(BF)
            dq.append(dot(ds, kp))
            dk.append(dot(ds, qp, TN))
            dv.append(dot(pr, gmp, TN))
        gqkv[:, pl.ds(off, 128)] = (jnp.where(low_lanes, dq[0], dq[1]) * scale).astype(BF)
        gqkv[:, pl.ds(offk, 128)] = (jnp.where(low_lanes, dk[0], dk[1]) * scale).astype(BF)
        gqkv[:, pl.ds(offv, 128)] = jnp.where(low_lanes, dv[0], dv[1]).astype(BF)
        return carry

    lax.fori_loop(0, half // 128, attend_back, 0)
    tick(3)
    for j in range(3):
        cols = pl.ds(j * half, half)
        lq[:, cols] = (dot(n1t[...], gqkv[:, cols]) * factor).astype(BF)
    sv[pl.ds(2, 1), pl.ds(0, half)] = jnp.sum(gqkv[:, pl.ds(0, half)].astype(F32), 0, keepdims=True) * factor
    sv[pl.ds(2, 1), pl.ds(half, half)] = (
        jnp.sum(gqkv[:, pl.ds(2 * half, half)].astype(F32), 0, keepdims=True) * factor
    )
    for step in range(AHEAD):
        for s in stq:
            y_ahead(s, step)
    exs[2] = dot(gqkv[...], wqkv[...], NT).astype(BF)
    swap(2).start()
    tick(4)

    def finish(target, landing, value, sends, sem0):
        for k in range(2):
            val = value(seg_rows(2 * k + c)).astype(BF)
            @pl.when(y == k)
            def _():
                target[y] = val
            @pl.when(y != k)
            def _():
                landing[0] = val
        send = remote(landing.at[0], landing.at[1], o_send.at[sem0], o_recv.at[sem0], ydev)
        send.start()
        return send

    for send in mlp_sends:
        send.wait_recv()
    lo_send = finish(
        lo_out, lo_s,
        lambda r: res[r, :] + mps[r, :].astype(F32) + mpr[r, :].astype(F32) + fb2[...], None, 2,
    )
    swap(2).wait_recv()
    s_gain, s_bias, _, _ = norm_back(2, u1, inv1, g1, lambda r: gres[r, :])
    gt_send = finish(gt_out, gt_s, lambda r: gres[r, :], None, 3)
    sv[pl.ds(3, 1), pl.ds(0, half)] = mine(s_gain)
    sv[pl.ds(3, 1), pl.ds(half, half)] = mine(s_bias)

    lax.fori_loop(LOOP, max(s.gather + (RING if s.kind == "b" else RING - 1) for s in streams) + 1, lambda t, carry: (tick(t), carry)[1], 0)
    s_over_core().wait()

    lo_send.wait()
    lo_out[1 - y] = lo_s[1]
    gt_send.wait()
    gt_out[1 - y] = gt_s[1]

    for trio in first:
        for copy in trio:
            copy.wait_send()
    for i in range(3):
        swap(i).wait_send()
    for send in mlp_sends:
        send.wait_send()

    for s in b_streams:
        whole = s.other
        remote(whole, whole, yb_send.at[s.k], yb_recv.at[s.k, 0], ydev).wait_send()
        remote(whole, whole, yg_send.at[s.k], yg_recv.at[s.k, 0], ydev).wait_send()
    for i, arr in enumerate((f2, f1, fq, fo)):
        remote(arr.at[c], arr.at[c], c_send.at[i], c_recv.at[i], core).wait()


def write_kernel(
    lo, gt, f2, f1, fq, fo, sall,
    o_lo, o_gt, o_ln1g, o_ln1b, o_qkv, o_qb, o_vb, o_out, o_ob, o_ln2g, o_ln2b, o_fc1, o_fb1, o_fc2, o_fb2,
    stage, sems, small_sems,
):
    width = f2.shape[2]
    half = width // 2
    ffh = f2.shape[1]
    n_buf = stage.shape[0]
    jobs = []
    for c in range(2):
        for k in range(ffh // 192):
            jobs.append((f2, (c, 192 * k, 192, 0, width), lambda c=c, k=k: o_fc2.at[pl.ds(c * ffh + 192 * k, 192), :]))
        for k in range(width // 192):
            for h in range(2):
                jobs.append((f1, (c, 192 * k, 192, width * h, width), lambda c=c, k=k, h=h: o_fc1.at[pl.ds(192 * k, 192), pl.ds(c * ffh + width * h, width)]))
            for j in range(3):
                jobs.append((fq, (c, 192 * k, 192, half * j, half), lambda c=c, k=k, j=j: o_qkv.at[pl.ds(192 * k, 192), pl.ds(j * width + c * half, half)]))
        for k in range(half // 192):
            jobs.append((fo, (c, 192 * k, 192, 0, width), lambda c=c, k=k: o_out.at[pl.ds(c * half + 192 * k, 192), :]))
    small = [(lo, o_lo), (gt, o_gt)]
    for c in range(2):
        for row in range(2):
            small.append((sall.at[c, row], o_fb1.at[pl.ds(c * ffh + row * width, width)]))
        for row, first, second in ((2, o_qb, o_vb), (3, o_ln1g, o_ln1b), (4, o_ob, o_fb2), (5, o_ln2g, o_ln2b)):
            small.append((sall.at[c, row, pl.ds(0, half)], first.at[pl.ds(c * half, half)]))
            small.append((sall.at[c, row, pl.ds(half, half)], second.at[pl.ds(c * half, half)]))
    small = [pltpu.make_async_copy(src, target, small_sems.at[i]) for i, (src, target) in enumerate(small)]
    for copy in small:
        copy.start()
    copies = []
    for i, (src, (c, row, rows, col, cols), target) in enumerate(jobs):
        slot = i % n_buf
        if i >= n_buf:
            copies[i - n_buf].wait()
        stage[slot, :, pl.ds(0, cols)] = src[c, pl.ds(row, rows), pl.ds(col, cols)].astype(F32)
        copy = pltpu.make_async_copy(stage.at[slot, :, pl.ds(0, cols)], target(), sems.at[slot])
        copy.start()
        copies.append(copy)
    for copy in small + copies[-n_buf:]:
        copy.wait()


def shards(n_wide, tokens, cotangent, row_counts, mask_flags, ln1_gain, ln1_bias, w_qkv, q_bias, v_bias, w_out, out_bias, ln2_gain, ln2_bias, w_fc1, fc1_bias, w_fc2, fc2_bias):
    images, slots, width = tokens.shape
    ff = w_fc1.shape[1]
    n_blk = lax.axis_size("blk")
    seq, half, ffh = slots * n_blk, width // 2, ff // 2
    groups = n_wide // RING
    factor = float(images * slots * n_wide * n_blk) ** -0.5
    vm, dma = pltpu.VMEM, pltpu.SemaphoreType.DMA
    vspec, anyspec = pl.BlockSpec(memory_space=pltpu.VMEM), pl.BlockSpec(memory_space=pl.ANY)
    n_heads = HEADS // 2
    scratch = [
        vm((width, 3 * half), BF), vm((half, width), BF), vm((width, ffh), BF), vm((ffh, width), BF),
        vm((seq, width), BF), vm((seq, width), BF), vm((6, 8, 128), F32),
        vm((seq, width), BF), vm((width, seq), BF), vm((seq, width), F32), vm((seq, 1), F32),
        vm((seq, 3 * half), BF), vm((n_heads, seq, seq), BF), vm((seq, half), F32), vm((seq, half), BF),
        vm((3, seq, width), BF), vm((3, seq, width), BF), vm((seq, width), F32),
        vm((seq, width), BF), vm((width, seq), BF), vm((seq, width), F32), vm((seq, 1), F32),
        vm((seq, ffh), BF), vm((seq, ffh), F32), vm((seq, ffh), BF), vm((seq, width), F32), vm((seq, width), BF),
        vm((seq, half), BF), vm((seq, 3 * half), BF), vm((seq, width), BF), vm((seq, width), BF),
        vm((2, slots, width), BF), vm((2, slots, width), BF),
        vm((RING, 8, width), F32), vm((2, 8, width), F32), vm((8, width), F32),
        vm((ffh, width), BF), vm((width, ffh), BF), vm((width, 3 * half), BF), vm((half, width), BF),
        vm((2, RING - 1, 96, width), BF), vm((2, RING - 1, 48, width), BF), vm((2, RING - 1, 48, half), BF),
        vm((RING - 1, 48, 640), BF), vm((RING - 1, 48, 512), BF),
        vm((2, RING, 48, width), BF), vm((RING, 48, 640), BF), vm((RING, 48, 512), BF),
        vm((2, 96, width), BF), vm((2, 48, half), BF),
        vm((8, groups, 96, width) if groups > 1 else (1, 1, 16, 128), BF),
        vm((groups, 8, width) if groups > 1 else (1, 8, 128), F32),
        vm((16, width), F32), dma((6,)), dma((16,)), dma((9,)), dma((9,)), dma((3,)), dma((3,)), dma((4,)), dma((4,)),
        dma((8,)), dma((8, RING - 1)), dma((4,)), dma((4, RING)), dma((4,)), dma((4,)),
        dma((8,)), dma((8, RING - 1)), dma((4,)), dma((4, RING)),
        dma((4,)), dma((4,)), dma((4,)), dma((10,)),
        dma((9, max(groups - 1, 1))), dma((9, max(groups - 1, 1))),
    ]
    outs = [
        vm(tokens.shape, BF), vm(tokens.shape, BF),
        vm((2, ffh, width), BF), vm((2, width, ffh), BF), vm((2, width, 3 * half), BF), vm((2, half, width), BF),
        vm((2, 8, width), F32),
    ]
    lo, gt, f2, f1, fq, fo, sall = pl.pallas_call(
        functools.partial(layer_kernel, n_wide, factor),
        out_shape=outs,
        in_specs=[vspec] * 4 + [anyspec] * 13,
        out_specs=[vspec] * 7,
        scratch_shapes=scratch,
        compiler_params=pltpu.CompilerParams(collective_id=0, has_side_effects=True, vmem_limit_bytes=46 * 2**20),
        name="layer",
    )(
        tokens, cotangent, row_counts.T, mask_flags, ln1_gain, ln1_bias, q_bias, v_bias, out_bias,
        ln2_gain, ln2_bias, fc2_bias, fc1_bias, w_qkv, w_out, w_fc1, w_fc2,
    )
    vec = jax.ShapeDtypeStruct((width,), F32)
    mat = lambda *shape: jax.ShapeDtypeStruct(shape, F32)
    n_buf = 6
    return pl.pallas_call(
        write_kernel,
        out_shape=[
            jax.ShapeDtypeStruct(tokens.shape, BF), jax.ShapeDtypeStruct(tokens.shape, BF),
            vec, vec, mat(width, 3 * width), vec, vec, mat(width, width), vec, vec, vec, mat(width, ff), mat(ff), mat(ff, width), vec,
        ],
        in_specs=[vspec] * 7,
        out_specs=[anyspec] * 15,
        scratch_shapes=[vm((n_buf, 192, width), F32), dma((n_buf,)), dma((24,))],
        compiler_params=pltpu.CompilerParams(vmem_limit_bytes=8 * 2**20),
        name="write",
    )(lo, gt, f2, f1, fq, fo, sall)


def solution(mesh):
    rows, whole = P("wide", "blk", None), P()
    return jax.shard_map(
        functools.partial(shards, mesh.shape["wide"]),
        mesh=mesh,
        in_specs=(rows, rows, P("wide", "blk"), P("wide", "blk")) + (whole,) * 13,
        out_specs=(rows, rows) + (whole,) * 13,
        check_vma=False,
    )
```

```python
import functools

import jax
import jax.numpy as jnp
from jax import lax
from jax.experimental import pallas as pl
from jax.experimental.pallas import tpu as pltpu
from jax.sharding import PartitionSpec as P

HEADS = 12
ROW_LEN = 14
EPS = 1e-06
RING = 8
BF = jnp.bfloat16
F32 = jnp.float32
MESH = pl.DeviceIdType.MESH
NT = (((1,), (1,)), ((), ()))
TN = (((0,), (0,)), ((), ()))


def dot(a, b, dims=(((1,), (0,)), ((), ()))):
    return lax.dot_general(a, b, dims, preferred_element_type=F32)


def ring_place(r):
    return jnp.where(r % 2 == 0, r // 2, RING - 1 - r // 2)


def ring_member(q):
    return jnp.where(q < RING // 2, 2 * q, 2 * RING - 1 - 2 * q)


def al(v, m):
    return pl.multiple_of(v, m)


class Stream:
    def __init__(self, way, dev, local, final, bufs, other):
        self.way, self.dev, self.local, self.final = way, dev, local, final
        self.bufs, self.other = bufs, other


class Pair:
    def __init__(self, i, kind, k, name, array, whole, streams):
        self.i, self.kind, self.k, self.array, self.whole, self.streams = i, kind, k, array, whole, streams
        self.start, self.gather = START[name], GATHER[name]


START = {"fc2a": 2, "fc2b": 0, "fc1": 2, "out": 4, "qkv": 4}
GATHER = {"fc2a": 12, "fc2b": 9, "fc1": 11, "out": 12, "qkv": 11}
SMALL = 8
LOOP = 5
AHEAD = 2
ORDER = (2, 1, 0, 3, 4)


def layer_kernel(n_wide, factor, *refs):
    (
        tok, cot, counts_h, flags_h, g1_h, b1_h, qb_h, vb_h, ob_h, g2_h, b2_h, fb2_h, fb1_h, wqkv_h, wout_h, w1_h, w2_h,
        lo_out, gt_out, f2, f1, fq, fo, sall,
        wqkv, wout, w1, w2, xs, cs, meta, n1, n1t, u1, inv1, qkv, probs, mix, mrg, exs, exr, res, n2, n2t, u2, inv2,
        act, gd, gh, gres, ga, gm, gqkv, mps, mpr, lo_s, gt_s, sg, sy, sv,
        l2, l1, lq, lout, r48, r384, rqn, rqp, y48, yqn, yqp, x48, x384, gsh, gsv,
        vecs, counts, flags, w_sem, v_sem, t_send, t_recv, e_send, e_recv, o_send, o_recv,
        rs_send, rs_recv, yb_send, yb_recv, ya_send, ya_recv, ag_send, ag_recv, yg_send, yg_recv,
        c_send, c_recv, s_send, s_recv, g_send, g_recv,
    ) = refs
    groups = n_wide // RING
    seq, width = xs.shape
    half = width // 2
    ffh = w1.shape[1]
    slots = seq // 4
    w = lax.axis_index("wide")
    b = lax.axis_index("blk")
    y, c = b // 2, b % 2
    group, inner = w // RING, w % RING
    p = ring_place(inner)

    def at_place(q):
        return (group * RING + ring_member(lax.rem(q + RING, RING)), b)

    nxt, prv = at_place(p + 1), at_place(p - 1)
    core = (w, 2 * y + 1 - c)
    ydev = (w, 2 * (1 - y) + c)
    others = [(lax.rem(group + j, groups) * RING + inner, b) for j in range(1, groups)]

    bar = pltpu.get_barrier_semaphore()
    greeted = [core, ydev, nxt, prv] + others
    for dev in greeted:
        pl.semaphore_signal(bar, inc=1, device_id=dev, device_id_type=MESH)
    half_c = al(c * half, 128)
    ffh_c = al(c * ffh, 128)
    seg = al(b * slots, slots)
    own_rows = [
        pltpu.make_async_copy(tok.at[y], xs.at[pl.ds(seg, slots), :], v_sem.at[12]),
        pltpu.make_async_copy(cot.at[y], cs.at[pl.ds(seg, slots), :], v_sem.at[13]),
    ]
    marks = [
        pltpu.make_async_copy(counts_h, counts, v_sem.at[14]),
        pltpu.make_async_copy(flags_h, flags, v_sem.at[15]),
    ]
    for load in marks + own_rows:
        load.start()
    loads = [
        pltpu.make_async_copy(wqkv_h.at[:, pl.ds(al(j * width + c * half, 128), half)], wqkv.at[:, pl.ds(j * half, half)], w_sem.at[j])
        for j in range(3)
    ] + [
        pltpu.make_async_copy(wout_h.at[pl.ds(half_c, half), :], wout, w_sem.at[3]),
        pltpu.make_async_copy(w1_h.at[:, pl.ds(ffh_c, ffh)], w1, w_sem.at[4]),
        pltpu.make_async_copy(w2_h.at[pl.ds(ffh_c, ffh), :], w2, w_sem.at[5]),
    ]
    small_loads = [
        pltpu.make_async_copy(vec, vecs.at[i], v_sem.at[i])
        for i, vec in enumerate((g1_h, b1_h, qb_h, vb_h, ob_h, g2_h, b2_h, fb2_h))
    ] + [
        pltpu.make_async_copy(fb1_h.at[pl.ds(i * width, width)], vecs.at[8 + i], v_sem.at[8 + i]) for i in range(2 * ffh // width)
    ]
    g1, b1, qb, vb, ob, g2, b2, fb2 = (vecs.at[pl.ds(i, 1), :] for i in range(8))
    for load in small_loads + loads:
        load.start()

    def remote(src, dst, send, recv, dev):
        return pltpu.make_async_remote_copy(
            src_ref=src, dst_ref=dst, send_sem=send, recv_sem=recv, device_id=dev, device_id_type=MESH
        )

    pl.semaphore_wait(bar, len(greeted))
    def entry(i, k, img, dev):
        src = (meta.at[4 + img], tok.at[img], cot.at[img])[k]
        dst = (meta.at[b], xs.at[pl.ds(seg, slots), :], cs.at[pl.ds(seg, slots), :])[k]
        return remote(src, dst, t_send.at[3 * i + k], t_recv.at[3 * i + k], dev)

    def onward(k):
        rows = pl.ds(al((2 * (1 - y) + c) * slots, slots), slots)
        here = (meta.at[2 * (1 - y) + c], xs.at[rows, :], cs.at[rows, :])[k]
        return remote(here, here, t_send.at[6 + k], t_recv.at[6 + k], core)

    first = [[entry(0, k, y, core) for k in range(3)], [entry(1, k, 1 - y, ydev) for k in range(3)], [onward(k) for k in range(3)]]
    for trio in first[:2]:
        trio[1].start()
    for load in marks:
        load.wait()
    lane64 = lax.broadcasted_iota(jnp.int32, (1, slots), 1)
    zero64 = jnp.zeros((1, slots), F32)
    for img in range(2):
        live = (lane64 < counts[:, pl.ds(img, 1)] * ROW_LEN).astype(F32)
        weight = live * flags[pl.ds(img, 1), :].astype(F32)
        for row, val in ((0, live), (1, weight)):
            low = jnp.concatenate([val, zero64], 1)
            high = jnp.concatenate([zero64, val], 1)
            meta[4 + img, pl.ds(row, 1), :] = jnp.where(c == 0, low, high)
    meta[b] = meta[4 + y]
    for k in (0, 2):
        for trio in first[:2]:
            trio[k].start()

    def chunk(q):
        return lax.rem(q + 2 * RING, RING)

    def fc2_streams(j):
        return [
            Stream(
                way, dev,
                lambda k, yy, d=d: l2.at[pl.ds(al(k * 192 + 96 * d + 48 * j, 16), 48), :],
                lambda k, yy, d=d: f2.at[c, k, pl.ds(96 * d + 48 * j, 48), :],
                r48.at[2 * j + d], x48.at[2 * j + d],
            )
            for d, (way, dev) in enumerate(ways)
        ]

    ways = ((1, nxt), (-1, prv))
    core_ways = tuple(
        (way * (1 - 2 * c), (jnp.where(c == 0, here[0], there[0]), b))
        for way, here, there in ((1, nxt, prv), (-1, prv, nxt))
    )
    split = ((0, 640), (640, 512))
    pairs = [
        Pair(0, "a", 0, "fc2a", 0, l2.at[pl.ds(0, 96), :], fc2_streams(0)),
        Pair(1, "a", 1, "fc2b", 0, l2.at[pl.ds(0, 96), :], fc2_streams(1)),
        Pair(2, "b", 0, "fc1", 1, l2.at[pl.ds(0, 96), :], [
            Stream(
                way, dev,
                lambda k, yy, d=d: l1.at[pl.ds(al(k * 96 + 48 * d, 16), 48), pl.ds(al(yy * width, 128), width)],
                lambda k, yy, d=d: f1.at[c, k, pl.ds(48 * d, 48), pl.ds(al(yy * width, 128), width)],
                r48.at[4 + d], y48.at[d],
            )
            for d, (way, dev) in enumerate(ways)
        ]),
        Pair(3, "b", 1, "qkv", 2, lq.at[pl.ds(0, 48), :], [
            Stream(
                way, dev,
                lambda k, yy, at=split[d]: lq.at[pl.ds(al(k * 96 + 48 * yy, 16), 48), pl.ds(*at)],
                lambda k, yy, at=split[d]: fq.at[c, k, pl.ds(al(48 * yy, 16), 48), pl.ds(*at)],
                (rqn, rqp)[d], (yqn, yqp)[d],
            )
            for d, (way, dev) in enumerate(core_ways)
        ]),
        Pair(4, "a", 2, "out", 3, l2.at[pl.ds(0, 48), :], [
            Stream(
                way, dev,
                lambda k, yy, d=d: lout.at[pl.ds(al(k * 48, 16), 48), pl.ds(half * d, half)],
                lambda k, yy, d=d: fo.at[c, k, :, pl.ds(half * d, half)],
                r384.at[d], x384.at[d],
            )
            for d, (way, dev) in enumerate(ways)
        ]),
    ]
    fc1_pair, qkv_pair = pairs[2], pairs[3]
    b_pairs = [fc1_pair, qkv_pair]
    last = RING - 2

    def rs_chunk(s, step):
        return chunk(p - s.way * (1 + step))

    def arrived(a, sem):
        remote(a.whole, a.whole, sem, sem, core).wait_recv()

    def left(a, sem):
        remote(a.whole, a.whole, sem, sem, core).wait_send()

    def y_ahead(a, step):
        for s in a.streams:
            remote(
                s.local(rs_chunk(s, step), 1 - y), s.other.at[step], yb_send.at[a.k], yb_recv.at[a.k, step], ydev
            ).start()

    def own(a, s, step):
        total = s.local(rs_chunk(s, step), y)[...].astype(F32)
        if a.kind == "b":
            total = total + s.other[step].astype(F32)
        return total

    def rs_send_on(a, s, src, step):
        remote(src, s.bufs.at[step], rs_send.at[a.i], rs_recv.at[a.i, step], s.dev).start()

    def rs_first(a):
        if a.kind == "b":
            arrived(a, yb_recv.at[a.k, 0])
        for s in a.streams:
            if a.kind == "a":
                rs_send_on(a, s, s.local(rs_chunk(s, 0), y), 0)
            else:
                s.other[0] = own(a, s, 0).astype(BF)
                rs_send_on(a, s, s.other.at[0], 0)

    def rs_arrived(a, step):
        if a.kind == "b":
            arrived(a, yb_recv.at[a.k, step])
        arrived(a, rs_recv.at[a.i, step - 1])
        left(a, rs_send.at[a.i])

    def rs_step(a, step):
        rs_arrived(a, step)
        for s in a.streams:
            s.bufs[step - 1] = (own(a, s, step) + s.bufs[step - 1].astype(F32)).astype(BF)
            rs_send_on(a, s, s.bufs.at[step - 1], step)

    def rs_end(a):
        rs_arrived(a, RING - 1)
        for s in a.streams:
            total = (own(a, s, RING - 1) + s.bufs[last].astype(F32)).astype(BF)
            if a.kind == "a":
                s.bufs[last] = total
                remote(s.bufs.at[last], s.other, ya_send.at[a.k], ya_recv.at[a.k], ydev).start()
            else:
                s.final(p, y)[...] = total

    def over_groups(a, d):
        s, i = a.streams[d], 2 * a.i + d
        piece = s.final(p, y)
        slot = gsh.at[i, :, pl.ds(0, piece.shape[0]), pl.ds(0, piece.shape[1])]
        slot[group] = piece[...]
        sends = [
            remote(slot.at[group], slot.at[group], g_send.at[i, j], g_recv.at[i, j], dev) for j, dev in enumerate(others)
        ]
        for send in sends:
            send.start()
        for send in sends:
            send.wait()
        total = slot[0].astype(F32)
        for j in range(1, groups):
            total = total + slot[j].astype(F32)
        piece[...] = total.astype(BF)

    def ag_send_on(a, step):
        for s in a.streams:
            here = s.final(chunk(p - s.way * step), y)
            remote(here, here, ag_send.at[a.i], ag_recv.at[a.i, step], s.dev).start()

    def spread(a, step):
        for s in a.streams:
            here = s.final(chunk(p - s.way * step), y)
            if a.kind == "b":
                remote(here, here, yg_send.at[a.k], yg_recv.at[a.k, step], ydev).start()
            remote(here, here, c_send.at[a.array], c_recv.at[a.array], core).start()

    def y_arrived(a, step):
        if a.kind == "b":
            arrived(a, yg_recv.at[a.k, step])
            for s in a.streams:
                here = s.final(chunk(p - s.way * step), 1 - y)
                remote(here, here, c_send.at[a.array], c_recv.at[a.array], core).start()

    def ag_first(a):
        if a.kind == "a":
            arrived(a, ya_recv.at[a.k])
            left(a, ya_send.at[a.k])
            for s in a.streams:
                s.final(p, y)[...] = (s.bufs[last].astype(F32) + s.other[...].astype(F32)).astype(BF)
        if groups > 1:
            for d in range(2):
                over_groups(a, d)
        ag_send_on(a, 0)
        spread(a, 0)

    def ag_step(a, step):
        arrived(a, ag_recv.at[a.i, step - 1])
        left(a, ag_send.at[a.i])
        ag_send_on(a, step)
        spread(a, step)
        y_arrived(a, step - 1)

    def ag_end(a):
        arrived(a, ag_recv.at[a.i, last])
        left(a, ag_send.at[a.i])
        spread(a, RING - 1)
        y_arrived(a, last)

    y_bytes = [f1.at[c, :, pl.ds(0, 48), :], fq.at[c, :, pl.ds(0, 48), :]]

    def s_copy(k, way):
        at = chunk(p - way * k)
        return remote(sg.at[at], sg.at[at], s_send.at[0 if way == 1 else 1], s_recv.at[k if way == 1 else 4 + k], nxt if way == 1 else prv)

    def s_ring(k):
        if k == 0:
            sg[p] = sv[...]
        if k > 0:
            s_copy(k - 1, 1).wait()
        if 0 < k < RING // 2:
            s_copy(k - 1, -1).wait()
        if k < RING // 2:
            s_copy(k, 1).start()
        if k < RING // 2 - 1:
            s_copy(k, -1).start()

    def s_over_y():
        return remote(sy.at[0], sy.at[1], s_send.at[2], s_recv.at[8], ydev)

    def s_over_core():
        return remote(sall.at[c], sall.at[c], s_send.at[3], s_recv.at[9], core)

    def s_sum():
        s_ring(RING // 2)
        total = sg[0]
        for k in range(1, RING):
            total = total + sg[k]
        sy[0] = total
        s_over_y().start()

    def s_last():
        s_over_y().wait()
        total = sy[0] + sy[1]
        if groups > 1:
            gsv[group] = total
            sends = [
                remote(gsv.at[group], gsv.at[group], g_send.at[10, j], g_recv.at[10, j], dev)
                for j, dev in enumerate(others)
            ]
            for send in sends:
                send.start()
            for send in sends:
                send.wait()
            total = gsv[0]
            for j in range(1, groups):
                total = total + gsv[j]
        sall[c] = total
        s_over_core().start()

    def when(cond, fn):
        if isinstance(cond, bool):
            if cond:
                fn()
        else:
            pl.when(cond)(fn)

    def both(*conds):
        if all(isinstance(v, bool) for v in conds):
            return all(conds)
        return functools.reduce(jnp.logical_and, conds)

    def tick(t):
        for i in ORDER:
            a = pairs[i]
            step = t - a.start
            when(step == 0, lambda a=a: rs_first(a))
            when(both(step >= 1, step <= last), lambda a=a, step=step: rs_step(a, step))
            when(step == RING - 1, lambda a=a: rs_end(a))
            if a.kind == "b":
                when(both(step >= 0, step < RING - AHEAD), lambda a=a, step=step: y_ahead(a, step + AHEAD))
            step = t - a.gather
            when(step == 0, lambda a=a: ag_first(a))
            when(both(step >= 1, step <= last), lambda a=a, step=step: ag_step(a, step))
            when(step == RING - 1, lambda a=a: ag_end(a))
            if a.kind == "b":
                when(step == RING, lambda a=a: y_arrived(a, RING - 1))
        if not isinstance(t, int):
            for k in range(RING // 2):
                when(t == SMALL + k, lambda k=k: s_ring(k))
            when(t == SMALL + RING // 2, s_sum)
            when(t == SMALL + RING // 2 + 1, s_last)

    blocks = seq // 64

    def rows_of(i):
        return pl.ds(al(i * 64, 64), 64)

    def norm(src, gain, bias, unit_ref, inv_ref, out, start=0, count=blocks):
        def body(i, carry):
            r = rows_of(start + i)
            v = src[r, :].astype(F32)
            cen = v - jnp.mean(v, -1, keepdims=True)
            inv = lax.rsqrt(jnp.mean(cen * cen, -1, keepdims=True) + EPS)
            unit = cen * inv
            unit_ref[r, :] = unit
            inv_ref[r, :] = inv
            out[r, :] = (unit * gain[...] + bias[...]).astype(BF)
            return carry
        lax.fori_loop(0, count, body, 0)

    def project(yy):
        norm(xs, g1, b1, u1, inv1, n1, 2 * yy, 2)
        r = pl.ds(al(yy * 2 * slots, 2 * slots), 2 * slots)
        rows = n1[r, :]
        qkv[r, pl.ds(0, half)] = (dot(rows, wqkv[:, pl.ds(0, half)]) + qb[:, pl.ds(half_c, half)]).astype(BF)
        qkv[r, pl.ds(half, half)] = dot(rows, wqkv[:, pl.ds(half, half)]).astype(BF)
        qkv[r, pl.ds(2 * half, half)] = (
            dot(rows, wqkv[:, pl.ds(2 * half, half)]) + vb[:, pl.ds(half_c, half)]
        ).astype(BF)

    for load in small_loads + loads[:3]:
        load.wait()
    own_rows[0].wait()
    first[0][1].wait_recv()
    project(y)
    first[1][1].wait_recv()
    first[2][1].start()
    first[1][0].wait_recv()
    first[2][0].start()
    first[2][1].wait_recv()
    project(1 - y)
    first[1][2].wait_recv()
    first[2][2].start()
    first[0][0].wait_recv()
    first[2][0].wait_recv()

    live_row = jnp.concatenate([meta[0, 0:1, :] + meta[1, 0:1, :], meta[2, 0:1, :] + meta[3, 0:1, :]], 1)
    weight_row = jnp.concatenate([meta[0, 1:2, :] + meta[1, 1:2, :], meta[2, 1:2, :] + meta[3, 1:2, :]], 1)
    dead = jnp.where(live_row > 0.5, 0.0, -1e30)
    lane = lax.broadcasted_iota(jnp.int32, (1, 128), 1)
    low_lanes = lane < 64
    head_mask = [low_lanes.astype(BF), (lane >= 64).astype(BF)]
    head_dim = width // HEADS
    scale = head_dim ** -0.5

    def attend(pair, carry):
        off = al(pair * 128, 128)
        qp = qkv[:, pl.ds(off, 128)]
        kp = qkv[:, pl.ds(al(half + off, 128), 128)]
        vp = qkv[:, pl.ds(al(2 * half + off, 128), 128)]
        outs = []
        for hh in range(2):
            s = dot(qp * head_mask[hh], kp, NT) * scale
            s = s + dead
            e = jnp.exp(s - jnp.max(s, -1, keepdims=True))
            pr = (e * (1.0 / jnp.sum(e, -1, keepdims=True))).astype(BF)
            probs[2 * pair + hh] = pr
            outs.append(dot(pr, vp))
        o = jnp.where(low_lanes, outs[0], outs[1])
        mix[:, pl.ds(off, 128)] = o
        mrg[:, pl.ds(off, 128)] = o.astype(BF)
        return carry

    lax.fori_loop(0, half // 128, attend, 0)

    def swap(i):
        return remote(exs.at[i], exr.at[i], e_send.at[i], e_recv.at[i], core)

    loads[3].wait()
    exs[0] = dot(mrg[...], wout[...]).astype(BF)
    swap(0).start()
    n1t[...] = n1[...].T
    eye = lax.broadcasted_iota(jnp.int32, (seq, seq), 0) == lax.broadcasted_iota(jnp.int32, (seq, seq), 1)
    weight_col = jnp.sum(jnp.where(eye, weight_row, 0.0), -1, keepdims=True)
    own_rows[1].wait()
    first[0][2].wait_recv()
    first[2][2].wait()
    cs[...] = (cs[...].astype(F32) * weight_col).astype(BF)
    swap(0).wait_recv()

    def residual(i, carry):
        r = rows_of(i)
        res[r, :] = xs[r, :].astype(F32) + exs[0, r, :].astype(F32) + exr[0, r, :].astype(F32) + ob[...]
        return carry

    lax.fori_loop(0, blocks, residual, 0)
    norm(res, g2, b2, u2, inv2, n2)
    n2t[...] = n2[...].T
    loads[4].wait()
    tile = 256
    root_half = 0.5 ** 0.5
    pdf_scale = (2.0 * jnp.pi) ** -0.5

    def hidden(j, carry):
        cols = pl.ds(al(j * tile, 128), tile)
        h = dot(n2[...], w1[:, cols]) + vecs[pl.ds(8 + 2 * c + j // 3, 1), pl.ds(al((j - 3 * (j // 3)) * tile, 128), tile)]
        cdf = 0.5 * (1.0 + lax.erf(h * root_half))
        act[:, cols] = (h * cdf).astype(BF)
        gd[:, cols] = cdf + h * (jnp.exp(-0.5 * h * h) * pdf_scale)
        return carry

    lax.fori_loop(0, ffh // tile, hidden, 0)
    loads[5].wait()

    def grad_fc2(j, carry):
        cols = pl.ds(al(j * tile, 128), tile)
        l2[cols, :] = (dot(act[:, cols], cs[...], TN) * factor).astype(BF)
        return carry

    lax.fori_loop(0, ffh // tile, grad_fc2, 0)
    tick(0)

    def grad_hidden(j, carry):
        cols = pl.ds(al(j * tile, 128), tile)
        d = dot(cs[...], w2[cols, :], NT) * gd[:, cols]
        low = d.astype(BF)
        gh[:, cols] = low
        row = j // 3
        sv[pl.ds(row, 1), pl.ds(al((j - 3 * row) * tile, 128), tile)] = (
            jnp.sum(low.astype(F32), 0, keepdims=True) * factor
        )
        return carry

    def grad_fc1(j, carry):
        cols = pl.ds(al(j * tile, 128), tile)
        l1[:, cols] = (dot(n2t[...], gh[:, cols]) * factor).astype(BF)
        return carry

    lax.fori_loop(0, ffh // tile, grad_hidden, 0)
    exs[1] = dot(gh[...], w1[...], NT).astype(BF)
    swap(1).start()
    lax.fori_loop(0, ffh // tile, grad_fc1, 0)
    for step in range(AHEAD):
        y_ahead(fc1_pair, step)
    tick(1)
    mps[...] = dot(act[...], w2[...]).astype(BF)

    def seg_rows(s):
        return pl.ds(al(s * slots, slots), slots)

    mlp_sends = [
        remote(mps.at[seg_rows(2 * k + 1 - c)], mpr.at[seg_rows(2 * k + 1 - c)], o_send.at[k], o_recv.at[k], core)
        for k in range(2)
    ]
    for send in mlp_sends:
        send.start()
    swap(1).wait_recv()

    zero_row = jnp.zeros((1, width), F32)

    def norm_back(slot, unit_ref, inv_ref, gain, base):
        def body(i, sums):
            r = rows_of(i)
            g = exs[slot, r, :].astype(F32) + exr[slot, r, :].astype(F32)
            unit = unit_ref[r, :]
            scaled = g * gain[...]
            inner_grad = inv_ref[r, :] * (
                scaled - jnp.mean(scaled, -1, keepdims=True) - unit * jnp.mean(scaled * unit, -1, keepdims=True)
            )
            total = base(r) + inner_grad
            gres[r, :] = total
            low = total.astype(BF)
            ga[r, :] = low
            return (
                sums[0] + jnp.sum(g * unit, 0, keepdims=True),
                sums[1] + jnp.sum(g, 0, keepdims=True),
                sums[2] + jnp.sum(low.astype(F32), 0, keepdims=True),
                sums[3] + jnp.sum(cs[r, :].astype(F32), 0, keepdims=True),
            )
        return lax.fori_loop(0, blocks, body, (zero_row,) * 4)

    def mine(row):
        return jnp.where(c == 0, row[:, :half], row[:, half:]) * factor

    s_gain, s_bias, s_out, s_two = norm_back(1, u2, inv2, g2, lambda r: cs[r, :].astype(F32))
    sv[pl.ds(5, 1), pl.ds(0, half)] = mine(s_gain)
    sv[pl.ds(5, 1), pl.ds(half, half)] = mine(s_bias)
    sv[pl.ds(4, 1), pl.ds(0, half)] = mine(s_out)
    sv[pl.ds(4, 1), pl.ds(half, half)] = mine(s_two)
    sv[pl.ds(6, 2), :] = jnp.zeros((2, width), F32)
    lout[...] = (dot(mrg[...], ga[...], TN) * factor).astype(BF)
    gm[...] = dot(ga[...], wout[...], NT).astype(BF)
    tick(2)

    def attend_back(pair, carry):
        off = al(pair * 128, 128)
        offk = al(half + off, 128)
        offv = al(2 * half + off, 128)
        qp = qkv[:, pl.ds(off, 128)]
        kp = qkv[:, pl.ds(offk, 128)]
        vp = qkv[:, pl.ds(offv, 128)]
        gmp = gm[:, pl.ds(off, 128)]
        op = mix[:, pl.ds(off, 128)]
        dq, dk, dv = [], [], []
        for hh in range(2):
            gmh = gmp * head_mask[hh]
            gp = dot(gmh, vp, NT)
            delta = jnp.sum(gmh.astype(F32) * op, -1, keepdims=True)
            pr = probs[2 * pair + hh]
            ds = (pr.astype(F32) * (gp - delta)).astype(BF)
            dq.append(dot(ds, kp))
            dk.append(dot(ds, qp, TN))
            dv.append(dot(pr, gmp, TN))
        gqkv[:, pl.ds(off, 128)] = (jnp.where(low_lanes, dq[0], dq[1]) * scale).astype(BF)
        gqkv[:, pl.ds(offk, 128)] = (jnp.where(low_lanes, dk[0], dk[1]) * scale).astype(BF)
        gqkv[:, pl.ds(offv, 128)] = jnp.where(low_lanes, dv[0], dv[1]).astype(BF)
        return carry

    lax.fori_loop(0, half // 128, attend_back, 0)
    tick(3)
    for j in range(3):
        cols = pl.ds(j * half, half)
        lq[:, cols] = (dot(n1t[...], gqkv[:, cols]) * factor).astype(BF)
    sv[pl.ds(2, 1), pl.ds(0, half)] = jnp.sum(gqkv[:, pl.ds(0, half)].astype(F32), 0, keepdims=True) * factor
    sv[pl.ds(2, 1), pl.ds(half, half)] = (
        jnp.sum(gqkv[:, pl.ds(2 * half, half)].astype(F32), 0, keepdims=True) * factor
    )
    for step in range(AHEAD):
        y_ahead(qkv_pair, step)
    exs[2] = dot(gqkv[...], wqkv[...], NT).astype(BF)
    swap(2).start()
    tick(4)

    def finish(target, landing, value, sends, sem0):
        for k in range(2):
            val = value(seg_rows(2 * k + c)).astype(BF)
            @pl.when(y == k)
            def _():
                target[y] = val
            @pl.when(y != k)
            def _():
                landing[0] = val
        send = remote(landing.at[0], landing.at[1], o_send.at[sem0], o_recv.at[sem0], ydev)
        send.start()
        return send

    for send in mlp_sends:
        send.wait_recv()
    lo_send = finish(
        lo_out, lo_s,
        lambda r: res[r, :] + mps[r, :].astype(F32) + mpr[r, :].astype(F32) + fb2[...], None, 2,
    )
    swap(2).wait_recv()
    s_gain, s_bias, _, _ = norm_back(2, u1, inv1, g1, lambda r: gres[r, :])
    gt_send = finish(gt_out, gt_s, lambda r: gres[r, :], None, 3)
    sv[pl.ds(3, 1), pl.ds(0, half)] = mine(s_gain)
    sv[pl.ds(3, 1), pl.ds(half, half)] = mine(s_bias)

    lax.fori_loop(LOOP, max(a.gather + (RING if a.kind == "b" else RING - 1) for a in pairs) + 1, lambda t, carry: (tick(t), carry)[1], 0)
    s_over_core().wait()

    lo_send.wait()
    lo_out[1 - y] = lo_s[1]
    gt_send.wait()
    gt_out[1 - y] = gt_s[1]

    for copy in first[0] + first[1] + first[2][:2]:
        copy.wait_send()
    for i in range(3):
        swap(i).wait_send()
    for send in mlp_sends:
        send.wait_send()

    for a in b_pairs:
        remote(y_bytes[a.k], y_bytes[a.k], yb_send.at[a.k], yb_recv.at[a.k, 0], ydev).wait_send()
        remote(y_bytes[a.k], y_bytes[a.k], yg_send.at[a.k], yg_recv.at[a.k, 0], ydev).wait_send()
    for i, arr in enumerate((f2, f1, fq, fo)):
        remote(arr.at[c], arr.at[c], c_send.at[i], c_recv.at[i], core).wait()


def write_kernel(
    lo, gt, f2, f1, fq, fo, sall,
    o_lo, o_gt, o_ln1g, o_ln1b, o_qkv, o_qb, o_vb, o_out, o_ob, o_ln2g, o_ln2b, o_fc1, o_fb1, o_fc2, o_fb2,
    stage, sems, small_sems,
):
    width = f2.shape[3]
    half = width // 2
    ffh = f2.shape[1] * f2.shape[2]
    n_buf = stage.shape[0]
    jobs = []
    for c in range(2):
        for k in range(RING):
            jobs.append((f2, c, [k], 0, width, o_fc2.at[pl.ds(c * ffh + 192 * k, 192), :]))
        for k in range(0, RING, 2):
            for h in range(2):
                jobs.append((f1, c, [k, k + 1], width * h, width, o_fc1.at[pl.ds(96 * k, 192), pl.ds(c * ffh + width * h, width)]))
            for j in range(3):
                jobs.append((fq, c, [k, k + 1], half * j, half, o_qkv.at[pl.ds(96 * k, 192), pl.ds(j * width + c * half, half)]))
        for k in range(0, RING, 4):
            jobs.append((fo, c, [k, k + 1, k + 2, k + 3], 0, width, o_out.at[pl.ds(c * half + 48 * k, 192), :]))
    small = [(lo, o_lo), (gt, o_gt)]
    for c in range(2):
        for row in range(2):
            small.append((sall.at[c, row], o_fb1.at[pl.ds(c * ffh + row * width, width)]))
        for row, first, second in ((2, o_qb, o_vb), (3, o_ln1g, o_ln1b), (4, o_ob, o_fb2), (5, o_ln2g, o_ln2b)):
            small.append((sall.at[c, row, pl.ds(0, half)], first.at[pl.ds(c * half, half)]))
            small.append((sall.at[c, row, pl.ds(half, half)], second.at[pl.ds(c * half, half)]))
    small = [pltpu.make_async_copy(src, target, small_sems.at[i]) for i, (src, target) in enumerate(small)]
    for copy in small:
        copy.start()
    copies = []
    for i, (src, c, chunks, col, cols, target) in enumerate(jobs):
        slot = i % n_buf
        if i >= n_buf:
            copies[i - n_buf].wait()
        rows = 192 // len(chunks)
        for at, k in enumerate(chunks):
            stage[slot, pl.ds(at * rows, rows), pl.ds(0, cols)] = src[c, k, :, pl.ds(col, cols)].astype(F32)
        copy = pltpu.make_async_copy(stage.at[slot, :, pl.ds(0, cols)], target, sems.at[slot])
        copy.start()
        copies.append(copy)
    for copy in small + copies[-n_buf:]:
        copy.wait()


def shards(n_wide, tokens, cotangent, row_counts, mask_flags, ln1_gain, ln1_bias, w_qkv, q_bias, v_bias, w_out, out_bias, ln2_gain, ln2_bias, w_fc1, fc1_bias, w_fc2, fc2_bias):
    images, slots, width = tokens.shape
    ff = w_fc1.shape[1]
    n_blk = lax.axis_size("blk")
    seq, half, ffh = slots * n_blk, width // 2, ff // 2
    groups = n_wide // RING
    factor = float(images * slots * n_wide * n_blk) ** -0.5
    vm, dma = pltpu.VMEM, pltpu.SemaphoreType.DMA
    vspec, anyspec = pl.BlockSpec(memory_space=pltpu.VMEM), pl.BlockSpec(memory_space=pl.ANY)
    n_heads = HEADS // 2
    scratch = [
        vm((width, 3 * half), BF), vm((half, width), BF), vm((width, ffh), BF), vm((ffh, width), BF),
        vm((seq, width), BF), vm((seq, width), BF), vm((6, 8, 128), F32),
        vm((seq, width), BF), vm((width, seq), BF), vm((seq, width), F32), vm((seq, 1), F32),
        vm((seq, 3 * half), BF), vm((n_heads, seq, seq), BF), vm((seq, half), F32), vm((seq, half), BF),
        vm((3, seq, width), BF), vm((3, seq, width), BF), vm((seq, width), F32),
        vm((seq, width), BF), vm((width, seq), BF), vm((seq, width), F32), vm((seq, 1), F32),
        vm((seq, ffh), BF), vm((seq, ffh), F32), vm((seq, ffh), BF), vm((seq, width), F32), vm((seq, width), BF),
        vm((seq, half), BF), vm((seq, 3 * half), BF), vm((seq, width), BF), vm((seq, width), BF),
        vm((2, slots, width), BF), vm((2, slots, width), BF),
        vm((RING, 8, width), F32), vm((2, 8, width), F32), vm((8, width), F32),
        vm((ffh, width), BF), vm((width, ffh), BF), vm((width, 3 * half), BF), vm((half, width), BF),
        vm((6, RING - 1, 48, width), BF), vm((2, RING - 1, 48, half), BF),
        vm((RING - 1, 48, 640), BF), vm((RING - 1, 48, 512), BF),
        vm((2, RING, 48, width), BF), vm((RING, 48, 640), BF), vm((RING, 48, 512), BF),
        vm((4, 48, width), BF), vm((2, 48, half), BF),
        vm((10, groups, 48, width) if groups > 1 else (1, 1, 16, 128), BF),
        vm((groups, 8, width) if groups > 1 else (1, 8, 128), F32),
        vm((16, width), F32), vm((1, 2), jnp.int32), vm((2, slots), jnp.int32), dma((6,)), dma((16,)), dma((9,)), dma((9,)), dma((3,)), dma((3,)), dma((4,)), dma((4,)),
        dma((5,)), dma((5, RING - 1)), dma((2,)), dma((2, RING)), dma((3,)), dma((3,)),
        dma((5,)), dma((5, RING - 1)), dma((2,)), dma((2, RING)),
        dma((4,)), dma((4,)), dma((4,)), dma((10,)),
        dma((11 if groups > 1 else 1, max(groups - 1, 1))), dma((11 if groups > 1 else 1, max(groups - 1, 1))),
    ]
    outs = [
        vm(tokens.shape, BF), vm(tokens.shape, BF),
        vm((2, RING, ffh // RING, width), BF), vm((2, RING, width // RING, ffh), BF),
        vm((2, RING, width // RING, 3 * half), BF), vm((2, RING, half // RING, width), BF),
        vm((2, 8, width), F32),
    ]
    lo, gt, f2, f1, fq, fo, sall = pl.pallas_call(
        functools.partial(layer_kernel, n_wide, factor),
        out_shape=outs,
        in_specs=[anyspec] * 17,
        out_specs=[vspec] * 7,
        scratch_shapes=scratch,
        compiler_params=pltpu.CompilerParams(collective_id=0, has_side_effects=True, vmem_limit_bytes=46 * 2**20),
        name="layer",
    )(
        tokens, cotangent, row_counts.T, mask_flags, ln1_gain, ln1_bias, q_bias, v_bias, out_bias,
        ln2_gain, ln2_bias, fc2_bias, fc1_bias, w_qkv, w_out, w_fc1, w_fc2,
    )
    vec = jax.ShapeDtypeStruct((width,), F32)
    mat = lambda *shape: jax.ShapeDtypeStruct(shape, F32)
    n_buf = 6
    return pl.pallas_call(
        write_kernel,
        out_shape=[
            jax.ShapeDtypeStruct(tokens.shape, BF), jax.ShapeDtypeStruct(tokens.shape, BF),
            vec, vec, mat(width, 3 * width), vec, vec, mat(width, width), vec, vec, vec, mat(width, ff), mat(ff), mat(ff, width), vec,
        ],
        in_specs=[vspec] * 7,
        out_specs=[anyspec] * 15,
        scratch_shapes=[vm((n_buf, 192, width), F32), dma((n_buf,)), dma((24,))],
        compiler_params=pltpu.CompilerParams(vmem_limit_bytes=8 * 2**20),
        name="write",
    )(lo, gt, f2, f1, fq, fo, sall)


def solution(mesh):
    rows, whole = P("wide", "blk", None), P()
    return jax.shard_map(
        functools.partial(shards, mesh.shape["wide"]),
        mesh=mesh,
        in_specs=(rows, rows, P("wide", "blk"), P("wide", "blk")) + (whole,) * 13,
        out_specs=(rows, rows) + (whole,) * 13,
        check_vma=False,
    )
```

```python
import functools

import jax
import jax.numpy as jnp
from jax import lax
from jax.experimental import pallas as pl
from jax.experimental.pallas import tpu as pltpu
from jax.sharding import PartitionSpec as P

HEADS = 12
ROW_LEN = 14
EPS = 1e-06
RING = 8
BF = jnp.bfloat16
F32 = jnp.float32
MESH = pl.DeviceIdType.MESH
NT = (((1,), (1,)), ((), ()))
TN = (((0,), (0,)), ((), ()))


def dot(a, b, dims=(((1,), (0,)), ((), ()))):
    return lax.dot_general(a, b, dims, preferred_element_type=F32)


def ring_place(r):
    return jnp.where(r % 2 == 0, r // 2, RING - 1 - r // 2)


def ring_member(q):
    return jnp.where(q < RING // 2, 2 * q, 2 * RING - 1 - 2 * q)


def al(v, m):
    return pl.multiple_of(v, m)


class Stream:
    def __init__(self, way, dev, local, final, bufs, other):
        self.way, self.dev, self.local, self.final = way, dev, local, final
        self.bufs, self.other = bufs, other


class Pair:
    def __init__(self, i, kind, k, name, array, whole, streams):
        self.i, self.kind, self.k, self.array, self.whole, self.streams = i, kind, k, array, whole, streams
        self.start, self.gather = START[name], GATHER[name]


START = {"fc2a": 1, "fc2b": 0, "fc1": 2, "out": 5, "qkv": 5}
GATHER = {"fc2a": 12, "fc2b": 9, "fc1": 11, "out": 13, "qkv": 12}
SMALL = 8
LOOP = 5
AHEAD = 2
ORDER = (1, 4, 3, 2, 0)


def layer_kernel(n_wide, factor, *refs):
    (
        tok, cot, counts_h, flags_h, g1_h, b1_h, qb_h, vb_h, ob_h, g2_h, b2_h, fb2_h, fb1_h, wqkv_h, wout_h, w1_h, w2_h,
        lo_out, gt_out, f2, f1, fq, fo, sall,
        wqkv, wout, w1, w2, xs, cs, meta, n1, n1t, u1, inv1, qkv, probs, mix, mrg, exs, exr, res, n2, n2t, u2, inv2,
        act, gd, gh, gres, ga, gm, gqkv, mps, mpr, lo_s, gt_s, sg, sy, sv,
        l2, l1, lq, lout, r48, r384, rqn, rqp, y48, yqn, yqp, x48, x384, gsh, gsv,
        vecs, counts, flags, w_sem, v_sem, t_send, t_recv, e_send, e_recv, o_send, o_recv,
        rs_send, rs_recv, yb_send, yb_recv, ya_send, ya_recv, ag_send, ag_recv, yg_send, yg_recv,
        c_send, c_recv, s_send, s_recv, g_send, g_recv,
    ) = refs
    groups = n_wide // RING
    seq, width = xs.shape
    half = width // 2
    ffh = w1.shape[1]
    slots = seq // 4
    w = lax.axis_index("wide")
    b = lax.axis_index("blk")
    y, c = b // 2, b % 2
    group, inner = w // RING, w % RING
    p = ring_place(inner)

    def at_place(q):
        return (group * RING + ring_member(lax.rem(q + RING, RING)), b)

    nxt, prv = at_place(p + 1), at_place(p - 1)
    core = (w, 2 * y + 1 - c)
    ydev = (w, 2 * (1 - y) + c)
    others = [(lax.rem(group + j, groups) * RING + inner, b) for j in range(1, groups)]

    bar = pltpu.get_barrier_semaphore()
    greeted = [core, ydev, nxt, prv] + others
    for dev in greeted:
        pl.semaphore_signal(bar, inc=1, device_id=dev, device_id_type=MESH)
    half_c = al(c * half, 128)
    ffh_c = al(c * ffh, 128)
    seg = al(b * slots, slots)
    own_rows = [
        pltpu.make_async_copy(tok.at[y], xs.at[pl.ds(seg, slots), :], v_sem.at[12]),
        pltpu.make_async_copy(cot.at[y], cs.at[pl.ds(seg, slots), :], v_sem.at[13]),
    ]
    marks = [
        pltpu.make_async_copy(counts_h, counts, v_sem.at[14]),
        pltpu.make_async_copy(flags_h, flags, v_sem.at[15]),
    ]
    for load in marks + own_rows:
        load.start()
    loads = [
        pltpu.make_async_copy(wqkv_h.at[:, pl.ds(al(j * width + c * half, 128), half)], wqkv.at[:, pl.ds(j * half, half)], w_sem.at[j])
        for j in range(3)
    ] + [
        pltpu.make_async_copy(wout_h.at[pl.ds(half_c, half), :], wout, w_sem.at[3]),
        pltpu.make_async_copy(w1_h.at[:, pl.ds(ffh_c, ffh)], w1, w_sem.at[4]),
        pltpu.make_async_copy(w2_h.at[pl.ds(ffh_c, ffh), :], w2, w_sem.at[5]),
    ]
    small_loads = [
        pltpu.make_async_copy(vec, vecs.at[i], v_sem.at[i])
        for i, vec in enumerate((g1_h, b1_h, qb_h, vb_h, ob_h, g2_h, b2_h, fb2_h))
    ] + [
        pltpu.make_async_copy(fb1_h.at[pl.ds(i * width, width)], vecs.at[8 + i], v_sem.at[8 + i]) for i in range(2 * ffh // width)
    ]
    g1, b1, qb, vb, ob, g2, b2, fb2 = (vecs.at[pl.ds(i, 1), :] for i in range(8))
    for load in small_loads + loads:
        load.start()

    def remote(src, dst, send, recv, dev):
        return pltpu.make_async_remote_copy(
            src_ref=src, dst_ref=dst, send_sem=send, recv_sem=recv, device_id=dev, device_id_type=MESH
        )

    pl.semaphore_wait(bar, len(greeted))
    def entry(i, k, img, dev):
        src = (meta.at[4 + img], tok.at[img], cot.at[img])[k]
        dst = (meta.at[b], xs.at[pl.ds(seg, slots), :], cs.at[pl.ds(seg, slots), :])[k]
        return remote(src, dst, t_send.at[3 * i + k], t_recv.at[3 * i + k], dev)

    def onward(k):
        rows = pl.ds(al((2 * (1 - y) + c) * slots, slots), slots)
        here = (meta.at[2 * (1 - y) + c], xs.at[rows, :], cs.at[rows, :])[k]
        return remote(here, here, t_send.at[6 + k], t_recv.at[6 + k], core)

    first = [[entry(0, k, y, core) for k in range(3)], [entry(1, k, 1 - y, ydev) for k in range(3)], [onward(k) for k in range(3)]]
    for trio in first[:2]:
        trio[1].start()
    for load in marks:
        load.wait()
    lane64 = lax.broadcasted_iota(jnp.int32, (1, slots), 1)
    zero64 = jnp.zeros((1, slots), F32)
    for img in range(2):
        live = (lane64 < counts[:, pl.ds(img, 1)] * ROW_LEN).astype(F32)
        weight = live * flags[pl.ds(img, 1), :].astype(F32)
        for row, val in ((0, live), (1, weight)):
            low = jnp.concatenate([val, zero64], 1)
            high = jnp.concatenate([zero64, val], 1)
            meta[4 + img, pl.ds(row, 1), :] = jnp.where(c == 0, low, high)
    meta[b] = meta[4 + y]
    for k in (0, 2):
        for trio in first[:2]:
            trio[k].start()

    def chunk(q):
        return lax.rem(q + 2 * RING, RING)

    def fc2_streams(j):
        return [
            Stream(
                way, dev,
                lambda k, yy, d=d: l2.at[pl.ds(al(k * 192 + 96 * d + 48 * j, 16), 48), :],
                lambda k, yy, d=d: f2.at[c, k, pl.ds(96 * d + 48 * j, 48), :],
                r48.at[2 * j + d], x48.at[2 * j + d],
            )
            for d, (way, dev) in enumerate(ways)
        ]

    ways = ((1, nxt), (-1, prv))
    core_ways = tuple(
        (way * (1 - 2 * c), (jnp.where(c == 0, here[0], there[0]), b))
        for way, here, there in ((1, nxt, prv), (-1, prv, nxt))
    )
    split = ((0, 640), (640, 512))
    pairs = [
        Pair(0, "a", 0, "fc2a", 0, l2.at[pl.ds(0, 96), :], fc2_streams(0)),
        Pair(1, "a", 1, "fc2b", 0, l2.at[pl.ds(0, 96), :], fc2_streams(1)),
        Pair(2, "b", 0, "fc1", 1, l2.at[pl.ds(0, 96), :], [
            Stream(
                way, dev,
                lambda k, yy, d=d: l1.at[pl.ds(al(k * 96 + 48 * d, 16), 48), pl.ds(al(yy * width, 128), width)],
                lambda k, yy, d=d: f1.at[c, k, pl.ds(48 * d, 48), pl.ds(al(yy * width, 128), width)],
                r48.at[4 + d], y48.at[d],
            )
            for d, (way, dev) in enumerate(ways)
        ]),
        Pair(3, "b", 1, "qkv", 2, lq.at[pl.ds(0, 48), :], [
            Stream(
                way, dev,
                lambda k, yy, at=split[d]: lq.at[pl.ds(al(k * 96 + 48 * yy, 16), 48), pl.ds(*at)],
                lambda k, yy, at=split[d]: fq.at[c, k, pl.ds(al(48 * yy, 16), 48), pl.ds(*at)],
                (rqn, rqp)[d], (yqn, yqp)[d],
            )
            for d, (way, dev) in enumerate(core_ways)
        ]),
        Pair(4, "a", 2, "out", 3, l2.at[pl.ds(0, 48), :], [
            Stream(
                way, dev,
                lambda k, yy, d=d: lout.at[pl.ds(al(k * 48, 16), 48), pl.ds(half * d, half)],
                lambda k, yy, d=d: fo.at[c, k, :, pl.ds(half * d, half)],
                r384.at[d], x384.at[d],
            )
            for d, (way, dev) in enumerate(ways)
        ]),
    ]
    fc1_pair, qkv_pair = pairs[2], pairs[3]
    b_pairs = [fc1_pair, qkv_pair]
    last = RING - 2

    def rs_chunk(s, step):
        return chunk(p - s.way * (1 + step))

    def arrived(a, sem):
        remote(a.whole, a.whole, sem, sem, core).wait_recv()

    def left(a, sem):
        remote(a.whole, a.whole, sem, sem, core).wait_send()

    def y_ahead(a, step):
        for s in a.streams:
            remote(
                s.local(rs_chunk(s, step), 1 - y), s.other.at[step], yb_send.at[a.k], yb_recv.at[a.k, step], ydev
            ).start()

    def own(a, s, step):
        total = s.local(rs_chunk(s, step), y)[...].astype(F32)
        if a.kind == "b":
            total = total + s.other[step].astype(F32)
        return total

    def rs_send_on(a, s, src, step):
        remote(src, s.bufs.at[step], rs_send.at[a.i], rs_recv.at[a.i, step], s.dev).start()

    def rs_first(a):
        if a.kind == "b":
            arrived(a, yb_recv.at[a.k, 0])
        for s in a.streams:
            if a.kind == "a":
                rs_send_on(a, s, s.local(rs_chunk(s, 0), y), 0)
            else:
                s.other[0] = own(a, s, 0).astype(BF)
                rs_send_on(a, s, s.other.at[0], 0)

    def rs_arrived(a, step):
        if a.kind == "b":
            arrived(a, yb_recv.at[a.k, step])
        arrived(a, rs_recv.at[a.i, step - 1])
        left(a, rs_send.at[a.i])

    def rs_step(a, step):
        rs_arrived(a, step)
        for s in a.streams:
            s.bufs[step - 1] = (own(a, s, step) + s.bufs[step - 1].astype(F32)).astype(BF)
            rs_send_on(a, s, s.bufs.at[step - 1], step)

    def rs_end(a):
        rs_arrived(a, RING - 1)
        for s in a.streams:
            total = (own(a, s, RING - 1) + s.bufs[last].astype(F32)).astype(BF)
            if a.kind == "a":
                s.bufs[last] = total
                remote(s.bufs.at[last], s.other, ya_send.at[a.k], ya_recv.at[a.k], ydev).start()
            else:
                s.final(p, y)[...] = total

    def over_groups(a, d):
        s, i = a.streams[d], 2 * a.i + d
        piece = s.final(p, y)
        slot = gsh.at[i, :, pl.ds(0, piece.shape[0]), pl.ds(0, piece.shape[1])]
        slot[group] = piece[...]
        sends = [
            remote(slot.at[group], slot.at[group], g_send.at[i, j], g_recv.at[i, j], dev) for j, dev in enumerate(others)
        ]
        for send in sends:
            send.start()
        for send in sends:
            send.wait()
        total = slot[0].astype(F32)
        for j in range(1, groups):
            total = total + slot[j].astype(F32)
        piece[...] = total.astype(BF)

    def ag_send_on(a, step):
        for s in a.streams:
            here = s.final(chunk(p - s.way * step), y)
            remote(here, here, ag_send.at[a.i], ag_recv.at[a.i, step], s.dev).start()

    def spread(a, step):
        for s in a.streams:
            here = s.final(chunk(p - s.way * step), y)
            if a.kind == "b":
                remote(here, here, yg_send.at[a.k], yg_recv.at[a.k, step], ydev).start()
            remote(here, here, c_send.at[a.array], c_recv.at[a.array], core).start()

    def y_arrived(a, step):
        if a.kind == "b":
            arrived(a, yg_recv.at[a.k, step])
            for s in a.streams:
                here = s.final(chunk(p - s.way * step), 1 - y)
                remote(here, here, c_send.at[a.array], c_recv.at[a.array], core).start()

    def ag_first(a):
        if a.kind == "a":
            arrived(a, ya_recv.at[a.k])
            left(a, ya_send.at[a.k])
            for s in a.streams:
                s.final(p, y)[...] = (s.bufs[last].astype(F32) + s.other[...].astype(F32)).astype(BF)
        if groups > 1:
            for d in range(2):
                over_groups(a, d)
        ag_send_on(a, 0)
        spread(a, 0)

    def ag_step(a, step):
        arrived(a, ag_recv.at[a.i, step - 1])
        left(a, ag_send.at[a.i])
        ag_send_on(a, step)
        spread(a, step)
        y_arrived(a, step - 1)

    def ag_end(a):
        arrived(a, ag_recv.at[a.i, last])
        left(a, ag_send.at[a.i])
        spread(a, RING - 1)
        y_arrived(a, last)

    y_bytes = [f1.at[c, :, pl.ds(0, 48), :], fq.at[c, :, pl.ds(0, 48), :]]

    def s_copy(k, way):
        at = chunk(p - way * k)
        return remote(sg.at[at], sg.at[at], s_send.at[0 if way == 1 else 1], s_recv.at[k if way == 1 else 4 + k], nxt if way == 1 else prv)

    def s_ring(k):
        if k == 0:
            sg[p] = sv[...]
        if k > 0:
            s_copy(k - 1, 1).wait()
        if 0 < k < RING // 2:
            s_copy(k - 1, -1).wait()
        if k < RING // 2:
            s_copy(k, 1).start()
        if k < RING // 2 - 1:
            s_copy(k, -1).start()

    def s_over_y():
        return remote(sy.at[0], sy.at[1], s_send.at[2], s_recv.at[8], ydev)

    def s_over_core():
        return remote(sall.at[c], sall.at[c], s_send.at[3], s_recv.at[9], core)

    def s_sum():
        s_ring(RING // 2)
        total = sg[0]
        for k in range(1, RING):
            total = total + sg[k]
        sy[0] = total
        s_over_y().start()

    def s_last():
        s_over_y().wait()
        total = sy[0] + sy[1]
        if groups > 1:
            gsv[group] = total
            sends = [
                remote(gsv.at[group], gsv.at[group], g_send.at[10, j], g_recv.at[10, j], dev)
                for j, dev in enumerate(others)
            ]
            for send in sends:
                send.start()
            for send in sends:
                send.wait()
            total = gsv[0]
            for j in range(1, groups):
                total = total + gsv[j]
        sall[c] = total
        s_over_core().start()

    def when(cond, fn):
        if isinstance(cond, bool):
            if cond:
                fn()
        else:
            pl.when(cond)(fn)

    def both(*conds):
        if all(isinstance(v, bool) for v in conds):
            return all(conds)
        return functools.reduce(jnp.logical_and, conds)

    def tick(t):
        for i in ORDER:
            a = pairs[i]
            step = t - a.start
            when(step == 0, lambda a=a: rs_first(a))
            when(both(step >= 1, step <= last), lambda a=a, step=step: rs_step(a, step))
            when(step == RING - 1, lambda a=a: rs_end(a))
            if a.kind == "b":
                when(both(step >= 0, step < RING - AHEAD), lambda a=a, step=step: y_ahead(a, step + AHEAD))
            step = t - a.gather
            when(step == 0, lambda a=a: ag_first(a))
            when(both(step >= 1, step <= last), lambda a=a, step=step: ag_step(a, step))
            when(step == RING - 1, lambda a=a: ag_end(a))
            if a.kind == "b":
                when(step == RING, lambda a=a: y_arrived(a, RING - 1))
        if not isinstance(t, int):
            for k in range(RING // 2):
                when(t == SMALL + k, lambda k=k: s_ring(k))
            when(t == SMALL + RING // 2, s_sum)
            when(t == SMALL + RING // 2 + 1, s_last)

    blocks = seq // 64

    def rows_of(i):
        return pl.ds(al(i * 64, 64), 64)

    def norm(src, gain, bias, unit_ref, inv_ref, out, start=0, count=blocks):
        def body(i, carry):
            r = rows_of(start + i)
            v = src[r, :].astype(F32)
            cen = v - jnp.mean(v, -1, keepdims=True)
            inv = lax.rsqrt(jnp.mean(cen * cen, -1, keepdims=True) + EPS)
            unit = cen * inv
            unit_ref[r, :] = unit
            inv_ref[r, :] = inv
            out[r, :] = (unit * gain[...] + bias[...]).astype(BF)
            return carry
        lax.fori_loop(0, count, body, 0, unroll=2)

    def project(yy):
        norm(xs, g1, b1, u1, inv1, n1, 2 * yy, 2)
        r = pl.ds(al(yy * 2 * slots, 2 * slots), 2 * slots)
        rows = n1[r, :]
        qkv[r, pl.ds(0, half)] = (dot(rows, wqkv[:, pl.ds(0, half)]) + qb[:, pl.ds(half_c, half)]).astype(BF)
        qkv[r, pl.ds(half, half)] = dot(rows, wqkv[:, pl.ds(half, half)]).astype(BF)
        qkv[r, pl.ds(2 * half, half)] = (
            dot(rows, wqkv[:, pl.ds(2 * half, half)]) + vb[:, pl.ds(half_c, half)]
        ).astype(BF)

    for load in small_loads + loads[:3]:
        load.wait()
    own_rows[0].wait()
    first[0][1].wait_recv()
    project(y)
    first[1][1].wait_recv()
    first[2][1].start()
    first[1][0].wait_recv()
    first[2][0].start()
    first[2][1].wait_recv()
    project(1 - y)
    first[1][2].wait_recv()
    first[2][2].start()
    first[0][0].wait_recv()
    first[2][0].wait_recv()

    live_row = jnp.concatenate([meta[0, 0:1, :] + meta[1, 0:1, :], meta[2, 0:1, :] + meta[3, 0:1, :]], 1)
    weight_row = jnp.concatenate([meta[0, 1:2, :] + meta[1, 1:2, :], meta[2, 1:2, :] + meta[3, 1:2, :]], 1)
    dead = jnp.where(live_row > 0.5, 0.0, -1e30)
    lane = lax.broadcasted_iota(jnp.int32, (1, 128), 1)
    low_lanes = lane < 64
    head_mask = [low_lanes.astype(BF), (lane >= 64).astype(BF)]
    head_dim = width // HEADS
    scale = head_dim ** -0.5

    def attend(pair, carry):
        off = al(pair * 128, 128)
        qp = qkv[:, pl.ds(off, 128)]
        kp = qkv[:, pl.ds(al(half + off, 128), 128)]
        vp = qkv[:, pl.ds(al(2 * half + off, 128), 128)]
        outs = []
        for hh in range(2):
            s = dot(qp * head_mask[hh], kp, NT) * scale
            s = s + dead
            e = jnp.exp(s - jnp.max(s, -1, keepdims=True))
            pr = (e * (1.0 / jnp.sum(e, -1, keepdims=True))).astype(BF)
            probs[2 * pair + hh] = pr
            outs.append(dot(pr, vp))
        o = jnp.where(low_lanes, outs[0], outs[1])
        mix[:, pl.ds(off, 128)] = o
        mrg[:, pl.ds(off, 128)] = o.astype(BF)
        return carry

    lax.fori_loop(0, half // 128, attend, 0, unroll=3)

    def swap(i):
        return remote(exs.at[i], exr.at[i], e_send.at[i], e_recv.at[i], core)

    loads[3].wait()
    exs[0] = dot(mrg[...], wout[...]).astype(BF)
    swap(0).start()
    n1t[...] = n1[...].T
    eye = lax.broadcasted_iota(jnp.int32, (seq, seq), 0) == lax.broadcasted_iota(jnp.int32, (seq, seq), 1)
    weight_col = jnp.sum(jnp.where(eye, weight_row, 0.0), -1, keepdims=True)
    own_rows[1].wait()
    first[0][2].wait_recv()
    first[2][2].wait()
    cs[...] = (cs[...].astype(F32) * weight_col).astype(BF)
    swap(0).wait_recv()

    def residual(i, carry):
        r = rows_of(i)
        res[r, :] = xs[r, :].astype(F32) + exs[0, r, :].astype(F32) + exr[0, r, :].astype(F32) + ob[...]
        return carry

    lax.fori_loop(0, blocks, residual, 0, unroll=2)
    norm(res, g2, b2, u2, inv2, n2)
    n2t[...] = n2[...].T
    loads[4].wait()
    tile = 256
    root_half = 0.5 ** 0.5
    pdf_scale = (2.0 * jnp.pi) ** -0.5

    def hidden(j, carry):
        cols = pl.ds(al(j * tile, 128), tile)
        h = dot(n2[...], w1[:, cols]) + vecs[pl.ds(8 + 2 * c + j // 3, 1), pl.ds(al((j - 3 * (j // 3)) * tile, 128), tile)]
        cdf = 0.5 * (1.0 + lax.erf(h * root_half))
        act[:, cols] = (h * cdf).astype(BF)
        gd[:, cols] = cdf + h * (jnp.exp(-0.5 * h * h) * pdf_scale)
        return carry

    lax.fori_loop(0, ffh // tile, hidden, 0, unroll=3)
    loads[5].wait()

    def grad_fc2(j, carry):
        cols = pl.ds(al(j * tile, 128), tile)
        l2[cols, :] = (dot(act[:, cols], cs[...], TN) * factor).astype(BF)
        return carry

    lax.fori_loop(0, ffh // tile, grad_fc2, 0, unroll=3)
    tick(0)

    def grad_hidden(j, carry):
        cols = pl.ds(al(j * tile, 128), tile)
        d = dot(cs[...], w2[cols, :], NT) * gd[:, cols]
        low = d.astype(BF)
        gh[:, cols] = low
        row = j // 3
        sv[pl.ds(row, 1), pl.ds(al((j - 3 * row) * tile, 128), tile)] = (
            jnp.sum(low.astype(F32), 0, keepdims=True) * factor
        )
        return carry

    def grad_fc1(j, carry):
        cols = pl.ds(al(j * tile, 128), tile)
        l1[:, cols] = (dot(n2t[...], gh[:, cols]) * factor).astype(BF)
        return carry

    lax.fori_loop(0, ffh // tile, grad_hidden, 0, unroll=3)
    exs[1] = dot(gh[...], w1[...], NT).astype(BF)
    swap(1).start()
    lax.fori_loop(0, ffh // tile, grad_fc1, 0, unroll=3)
    for step in range(AHEAD):
        y_ahead(fc1_pair, step)
    tick(1)
    mps[...] = dot(act[...], w2[...]).astype(BF)

    def seg_rows(s):
        return pl.ds(al(s * slots, slots), slots)

    mlp_sends = [
        remote(mps.at[seg_rows(2 * k + 1 - c)], mpr.at[seg_rows(2 * k + 1 - c)], o_send.at[k], o_recv.at[k], core)
        for k in range(2)
    ]
    for send in mlp_sends:
        send.start()
    swap(1).wait_recv()

    zero_row = jnp.zeros((1, width), F32)

    def norm_back(slot, unit_ref, inv_ref, gain, base):
        def body(i, sums):
            r = rows_of(i)
            g = exs[slot, r, :].astype(F32) + exr[slot, r, :].astype(F32)
            unit = unit_ref[r, :]
            scaled = g * gain[...]
            inner_grad = inv_ref[r, :] * (
                scaled - jnp.mean(scaled, -1, keepdims=True) - unit * jnp.mean(scaled * unit, -1, keepdims=True)
            )
            total = base(r) + inner_grad
            gres[r, :] = total
            low = total.astype(BF)
            ga[r, :] = low
            return (
                sums[0] + jnp.sum(g * unit, 0, keepdims=True),
                sums[1] + jnp.sum(g, 0, keepdims=True),
                sums[2] + jnp.sum(low.astype(F32), 0, keepdims=True),
                sums[3] + jnp.sum(cs[r, :].astype(F32), 0, keepdims=True),
            )
        return lax.fori_loop(0, blocks, body, (zero_row,) * 4, unroll=2)

    def mine(row):
        return jnp.where(c == 0, row[:, :half], row[:, half:]) * factor

    s_gain, s_bias, s_out, s_two = norm_back(1, u2, inv2, g2, lambda r: cs[r, :].astype(F32))
    sv[pl.ds(5, 1), pl.ds(0, half)] = mine(s_gain)
    sv[pl.ds(5, 1), pl.ds(half, half)] = mine(s_bias)
    sv[pl.ds(4, 1), pl.ds(0, half)] = mine(s_out)
    sv[pl.ds(4, 1), pl.ds(half, half)] = mine(s_two)
    sv[pl.ds(6, 2), :] = jnp.zeros((2, width), F32)
    lout[...] = (dot(mrg[...], ga[...], TN) * factor).astype(BF)
    gm[...] = dot(ga[...], wout[...], NT).astype(BF)
    tick(2)

    def attend_back(pair, carry):
        off = al(pair * 128, 128)
        offk = al(half + off, 128)
        offv = al(2 * half + off, 128)
        qp = qkv[:, pl.ds(off, 128)]
        kp = qkv[:, pl.ds(offk, 128)]
        vp = qkv[:, pl.ds(offv, 128)]
        gmp = gm[:, pl.ds(off, 128)]
        op = mix[:, pl.ds(off, 128)]
        dq, dk, dv = [], [], []
        for hh in range(2):
            gmh = gmp * head_mask[hh]
            gp = dot(gmh, vp, NT)
            delta = jnp.sum(gmh.astype(F32) * op, -1, keepdims=True)
            pr = probs[2 * pair + hh]
            ds = (pr.astype(F32) * (gp - delta)).astype(BF)
            dq.append(dot(ds, kp))
            dk.append(dot(ds, qp, TN))
            dv.append(dot(pr, gmp, TN))
        gqkv[:, pl.ds(off, 128)] = (jnp.where(low_lanes, dq[0], dq[1]) * scale).astype(BF)
        gqkv[:, pl.ds(offk, 128)] = (jnp.where(low_lanes, dk[0], dk[1]) * scale).astype(BF)
        gqkv[:, pl.ds(offv, 128)] = jnp.where(low_lanes, dv[0], dv[1]).astype(BF)
        return carry

    lax.fori_loop(0, half // 128, attend_back, 0, unroll=3)
    tick(3)
    for j in range(3):
        cols = pl.ds(j * half, half)
        lq[:, cols] = (dot(n1t[...], gqkv[:, cols]) * factor).astype(BF)
    sv[pl.ds(2, 1), pl.ds(0, half)] = jnp.sum(gqkv[:, pl.ds(0, half)].astype(F32), 0, keepdims=True) * factor
    sv[pl.ds(2, 1), pl.ds(half, half)] = (
        jnp.sum(gqkv[:, pl.ds(2 * half, half)].astype(F32), 0, keepdims=True) * factor
    )
    for step in range(AHEAD):
        y_ahead(qkv_pair, step)
    exs[2] = dot(gqkv[...], wqkv[...], NT).astype(BF)
    swap(2).start()
    tick(4)

    def finish(target, landing, value, sends, sem0):
        for k in range(2):
            val = value(seg_rows(2 * k + c)).astype(BF)
            @pl.when(y == k)
            def _():
                target[y] = val
            @pl.when(y != k)
            def _():
                landing[0] = val
        send = remote(landing.at[0], landing.at[1], o_send.at[sem0], o_recv.at[sem0], ydev)
        send.start()
        return send

    for send in mlp_sends:
        send.wait_recv()
    lo_send = finish(
        lo_out, lo_s,
        lambda r: res[r, :] + mps[r, :].astype(F32) + mpr[r, :].astype(F32) + fb2[...], None, 2,
    )
    swap(2).wait_recv()
    s_gain, s_bias, _, _ = norm_back(2, u1, inv1, g1, lambda r: gres[r, :])
    gt_send = finish(gt_out, gt_s, lambda r: gres[r, :], None, 3)
    sv[pl.ds(3, 1), pl.ds(0, half)] = mine(s_gain)
    sv[pl.ds(3, 1), pl.ds(half, half)] = mine(s_bias)

    lax.fori_loop(LOOP, max(a.gather + (RING if a.kind == "b" else RING - 1) for a in pairs) + 1, lambda t, carry: (tick(t), carry)[1], 0)
    s_over_core().wait()

    lo_send.wait()
    lo_out[1 - y] = lo_s[1]
    gt_send.wait()
    gt_out[1 - y] = gt_s[1]

    for copy in first[0] + first[1] + first[2][:2]:
        copy.wait_send()
    for i in range(3):
        swap(i).wait_send()
    for send in mlp_sends:
        send.wait_send()

    for a in b_pairs:
        remote(y_bytes[a.k], y_bytes[a.k], yb_send.at[a.k], yb_recv.at[a.k, 0], ydev).wait_send()
        remote(y_bytes[a.k], y_bytes[a.k], yg_send.at[a.k], yg_recv.at[a.k, 0], ydev).wait_send()
    for i, arr in enumerate((f2, f1, fq, fo)):
        remote(arr.at[c], arr.at[c], c_send.at[i], c_recv.at[i], core).wait()


def write_kernel(
    lo, gt, f2, f1, fq, fo, sall,
    o_lo, o_gt, o_ln1g, o_ln1b, o_qkv, o_qb, o_vb, o_out, o_ob, o_ln2g, o_ln2b, o_fc1, o_fb1, o_fc2, o_fb2,
    stage, sems, small_sems,
):
    width = f2.shape[3]
    half = width // 2
    ffh = f2.shape[1] * f2.shape[2]
    n_buf = stage.shape[0]
    jobs = []
    for c in range(2):
        for k in range(RING):
            jobs.append((f2, c, [k], 0, width, o_fc2.at[pl.ds(c * ffh + 192 * k, 192), :]))
        for k in range(0, RING, 2):
            for h in range(2):
                jobs.append((f1, c, [k, k + 1], width * h, width, o_fc1.at[pl.ds(96 * k, 192), pl.ds(c * ffh + width * h, width)]))
            for j in range(3):
                jobs.append((fq, c, [k, k + 1], half * j, half, o_qkv.at[pl.ds(96 * k, 192), pl.ds(j * width + c * half, half)]))
        for k in range(0, RING, 4):
            jobs.append((fo, c, [k, k + 1, k + 2, k + 3], 0, width, o_out.at[pl.ds(c * half + 48 * k, 192), :]))
    small = [(lo, o_lo), (gt, o_gt)]
    for c in range(2):
        for row in range(2):
            small.append((sall.at[c, row], o_fb1.at[pl.ds(c * ffh + row * width, width)]))
        for row, first, second in ((2, o_qb, o_vb), (3, o_ln1g, o_ln1b), (4, o_ob, o_fb2), (5, o_ln2g, o_ln2b)):
            small.append((sall.at[c, row, pl.ds(0, half)], first.at[pl.ds(c * half, half)]))
            small.append((sall.at[c, row, pl.ds(half, half)], second.at[pl.ds(c * half, half)]))
    small = [pltpu.make_async_copy(src, target, small_sems.at[i]) for i, (src, target) in enumerate(small)]
    for copy in small:
        copy.start()
    copies = []
    for i, (src, c, chunks, col, cols, target) in enumerate(jobs):
        slot = i % n_buf
        if i >= n_buf:
            copies[i - n_buf].wait()
        rows = 192 // len(chunks)
        for at, k in enumerate(chunks):
            stage[slot, pl.ds(at * rows, rows), pl.ds(0, cols)] = src[c, k, :, pl.ds(col, cols)].astype(F32)
        copy = pltpu.make_async_copy(stage.at[slot, :, pl.ds(0, cols)], target, sems.at[slot])
        copy.start()
        copies.append(copy)
    for copy in small + copies[-n_buf:]:
        copy.wait()


def shards(n_wide, tokens, cotangent, row_counts, mask_flags, ln1_gain, ln1_bias, w_qkv, q_bias, v_bias, w_out, out_bias, ln2_gain, ln2_bias, w_fc1, fc1_bias, w_fc2, fc2_bias):
    images, slots, width = tokens.shape
    ff = w_fc1.shape[1]
    n_blk = lax.axis_size("blk")
    seq, half, ffh = slots * n_blk, width // 2, ff // 2
    groups = n_wide // RING
    factor = float(images * slots * n_wide * n_blk) ** -0.5
    vm, dma = pltpu.VMEM, pltpu.SemaphoreType.DMA
    vspec, anyspec = pl.BlockSpec(memory_space=pltpu.VMEM), pl.BlockSpec(memory_space=pl.ANY)
    n_heads = HEADS // 2
    scratch = [
        vm((width, 3 * half), BF), vm((half, width), BF), vm((width, ffh), BF), vm((ffh, width), BF),
        vm((seq, width), BF), vm((seq, width), BF), vm((6, 8, 128), F32),
        vm((seq, width), BF), vm((width, seq), BF), vm((seq, width), F32), vm((seq, 1), F32),
        vm((seq, 3 * half), BF), vm((n_heads, seq, seq), BF), vm((seq, half), F32), vm((seq, half), BF),
        vm((3, seq, width), BF), vm((3, seq, width), BF), vm((seq, width), F32),
        vm((seq, width), BF), vm((width, seq), BF), vm((seq, width), F32), vm((seq, 1), F32),
        vm((seq, ffh), BF), vm((seq, ffh), F32), vm((seq, ffh), BF), vm((seq, width), F32), vm((seq, width), BF),
        vm((seq, half), BF), vm((seq, 3 * half), BF), vm((seq, width), BF), vm((seq, width), BF),
        vm((2, slots, width), BF), vm((2, slots, width), BF),
        vm((RING, 8, width), F32), vm((2, 8, width), F32), vm((8, width), F32),
        vm((ffh, width), BF), vm((width, ffh), BF), vm((width, 3 * half), BF), vm((half, width), BF),
        vm((6, RING - 1, 48, width), BF), vm((2, RING - 1, 48, half), BF),
        vm((RING - 1, 48, 640), BF), vm((RING - 1, 48, 512), BF),
        vm((2, RING, 48, width), BF), vm((RING, 48, 640), BF), vm((RING, 48, 512), BF),
        vm((4, 48, width), BF), vm((2, 48, half), BF),
        vm((10, groups, 48, width) if groups > 1 else (1, 1, 16, 128), BF),
        vm((groups, 8, width) if groups > 1 else (1, 8, 128), F32),
        vm((16, width), F32), vm((1, 2), jnp.int32), vm((2, slots), jnp.int32), dma((6,)), dma((16,)), dma((9,)), dma((9,)), dma((3,)), dma((3,)), dma((4,)), dma((4,)),
        dma((5,)), dma((5, RING - 1)), dma((2,)), dma((2, RING)), dma((3,)), dma((3,)),
        dma((5,)), dma((5, RING - 1)), dma((2,)), dma((2, RING)),
        dma((4,)), dma((4,)), dma((4,)), dma((10,)),
        dma((11 if groups > 1 else 1, max(groups - 1, 1))), dma((11 if groups > 1 else 1, max(groups - 1, 1))),
    ]
    outs = [
        vm(tokens.shape, BF), vm(tokens.shape, BF),
        vm((2, RING, ffh // RING, width), BF), vm((2, RING, width // RING, ffh), BF),
        vm((2, RING, width // RING, 3 * half), BF), vm((2, RING, half // RING, width), BF),
        vm((2, 8, width), F32),
    ]
    lo, gt, f2, f1, fq, fo, sall = pl.pallas_call(
        functools.partial(layer_kernel, n_wide, factor),
        out_shape=outs,
        in_specs=[anyspec] * 17,
        out_specs=[vspec] * 7,
        scratch_shapes=scratch,
        compiler_params=pltpu.CompilerParams(collective_id=0, has_side_effects=True, vmem_limit_bytes=46 * 2**20),
        name="layer",
    )(
        tokens, cotangent, row_counts.T, mask_flags, ln1_gain, ln1_bias, q_bias, v_bias, out_bias,
        ln2_gain, ln2_bias, fc2_bias, fc1_bias, w_qkv, w_out, w_fc1, w_fc2,
    )
    vec = jax.ShapeDtypeStruct((width,), F32)
    mat = lambda *shape: jax.ShapeDtypeStruct(shape, F32)
    n_buf = 6
    return pl.pallas_call(
        write_kernel,
        out_shape=[
            jax.ShapeDtypeStruct(tokens.shape, BF), jax.ShapeDtypeStruct(tokens.shape, BF),
            vec, vec, mat(width, 3 * width), vec, vec, mat(width, width), vec, vec, vec, mat(width, ff), mat(ff), mat(ff, width), vec,
        ],
        in_specs=[vspec] * 7,
        out_specs=[anyspec] * 15,
        scratch_shapes=[vm((n_buf, 192, width), F32), dma((n_buf,)), dma((24,))],
        compiler_params=pltpu.CompilerParams(vmem_limit_bytes=8 * 2**20),
        name="write",
    )(lo, gt, f2, f1, fq, fo, sall)


def solution(mesh):
    rows, whole = P("wide", "blk", None), P()
    return jax.shard_map(
        functools.partial(shards, mesh.shape["wide"]),
        mesh=mesh,
        in_specs=(rows, rows, P("wide", "blk"), P("wide", "blk")) + (whole,) * 13,
        out_specs=(rows, rows) + (whole,) * 13,
        check_vma=False,
    )
```

```python
import functools

import jax
import jax.numpy as jnp
from jax import lax
from jax.experimental import pallas as pl
from jax.experimental.pallas import tpu as pltpu
from jax.sharding import PartitionSpec as P

HEADS = 12
ROW_LEN = 14
EPS = 1e-06
RING = 8
BF = jnp.bfloat16
F32 = jnp.float32
MESH = pl.DeviceIdType.MESH
NT = (((1,), (1,)), ((), ()))
TN = (((0,), (0,)), ((), ()))


def dot(a, b, dims=(((1,), (0,)), ((), ()))):
    return lax.dot_general(a, b, dims, preferred_element_type=F32)


def ring_place(r):
    return jnp.where(r % 2 == 0, r // 2, RING - 1 - r // 2)


def ring_member(q):
    return jnp.where(q < RING // 2, 2 * q, 2 * RING - 1 - 2 * q)


def al(v, m):
    return pl.multiple_of(v, m)


class Stream:
    def __init__(self, way, dev, local, final, bufs, other):
        self.way, self.dev, self.local, self.final = way, dev, local, final
        self.bufs, self.other = bufs, other


class Pair:
    def __init__(self, i, kind, k, name, array, whole, streams):
        self.i, self.kind, self.k, self.array, self.whole, self.streams = i, kind, k, array, whole, streams
        self.start, self.gather = START[name], GATHER[name]


START = {"fc2a": 1, "fc2b": 0, "fc1": 2, "out": 5, "qkv": 5}
GATHER = {"fc2a": 12, "fc2b": 9, "fc1": 11, "out": 13, "qkv": 12}
SMALL = 8
LOOP = 5
AHEAD = 2
ORDER = (1, 4, 3, 2, 0)


def layer_kernel(n_wide, factor, *refs):
    (
        tok, cot, counts_h, flags_h, g1_h, b1_h, qb_h, vb_h, ob_h, g2_h, b2_h, fb2_h, fb1_h, wqkv_h, wout_h, w1_h, w2_h,
        lo_out, gt_out, f2, f1, fq, fo, sall,
        wqkv, wout, w1, w2, xs, cs, meta, n1, n1t, u1, inv1, qkv, probs, mix, mrg, exs, exr, res, n2, n2t, u2, inv2,
        act, gd, gh, gres, ga, gm, gqkv, mps, mpr, lo_s, gt_s, sg, sy, sv,
        l2, l1, lq, lout, r48, r384, rqn, rqp, y48, yqn, yqp, x48, x384, gsh, gsv,
        vecs, counts, flags, w_sem, v_sem, t_send, t_recv, e_send, e_recv, o_send, o_recv,
        rs_send, rs_recv, yb_send, yb_recv, ya_send, ya_recv, ag_send, ag_recv, yg_send, yg_recv,
        c_send, c_recv, s_send, s_recv, g_send, g_recv,
    ) = refs
    groups = n_wide // RING
    seq, width = xs.shape
    half = width // 2
    ffh = w1.shape[1]
    slots = seq // 4
    w = lax.axis_index("wide")
    b = lax.axis_index("blk")
    y, c = b // 2, b % 2
    group, inner = w // RING, w % RING
    p = ring_place(inner)

    def at_place(q):
        return (group * RING + ring_member(lax.rem(q + RING, RING)), b)

    nxt, prv = at_place(p + 1), at_place(p - 1)
    core = (w, 2 * y + 1 - c)
    ydev = (w, 2 * (1 - y) + c)
    others = [(lax.rem(group + j, groups) * RING + inner, b) for j in range(1, groups)]

    bar = pltpu.get_barrier_semaphore()
    greeted = [core, ydev, nxt, prv] + others
    for dev in greeted:
        pl.semaphore_signal(bar, inc=1, device_id=dev, device_id_type=MESH)
    half_c = al(c * half, 128)
    ffh_c = al(c * ffh, 128)
    seg = al(b * slots, slots)
    own_rows = [
        pltpu.make_async_copy(tok.at[y], xs.at[pl.ds(seg, slots), :], v_sem.at[12]),
        pltpu.make_async_copy(cot.at[y], cs.at[pl.ds(seg, slots), :], v_sem.at[13]),
    ]
    marks = [
        pltpu.make_async_copy(counts_h, counts, v_sem.at[14]),
        pltpu.make_async_copy(flags_h, flags, v_sem.at[15]),
    ]
    for load in marks + own_rows:
        load.start()
    loads = [
        pltpu.make_async_copy(wqkv_h.at[:, pl.ds(al(j * width + c * half, 128), half)], wqkv.at[:, pl.ds(j * half, half)], w_sem.at[j])
        for j in range(3)
    ] + [
        pltpu.make_async_copy(wout_h.at[pl.ds(half_c, half), :], wout, w_sem.at[3]),
        pltpu.make_async_copy(w1_h.at[:, pl.ds(ffh_c, ffh)], w1, w_sem.at[4]),
        pltpu.make_async_copy(w2_h.at[pl.ds(ffh_c, ffh), :], w2, w_sem.at[5]),
    ]
    small_loads = [
        pltpu.make_async_copy(vec, vecs.at[i], v_sem.at[i])
        for i, vec in enumerate((g1_h, b1_h, qb_h, vb_h, ob_h, g2_h, b2_h, fb2_h))
    ] + [
        pltpu.make_async_copy(fb1_h.at[pl.ds(i * width, width)], vecs.at[8 + i], v_sem.at[8 + i]) for i in range(2 * ffh // width)
    ]
    g1, b1, qb, vb, ob, g2, b2, fb2 = (vecs.at[pl.ds(i, 1), :] for i in range(8))
    for load in small_loads + loads:
        load.start()

    def remote(src, dst, send, recv, dev):
        return pltpu.make_async_remote_copy(
            src_ref=src, dst_ref=dst, send_sem=send, recv_sem=recv, device_id=dev, device_id_type=MESH
        )

    pl.semaphore_wait(bar, len(greeted))
    def entry(i, k, img, dev):
        src = (meta.at[4 + img], tok.at[img], cot.at[img])[k]
        dst = (meta.at[b], xs.at[pl.ds(seg, slots), :], cs.at[pl.ds(seg, slots), :])[k]
        return remote(src, dst, t_send.at[3 * i + k], t_recv.at[3 * i + k], dev)

    def onward(k):
        rows = pl.ds(al((2 * (1 - y) + c) * slots, slots), slots)
        here = (meta.at[2 * (1 - y) + c], xs.at[rows, :], cs.at[rows, :])[k]
        return remote(here, here, t_send.at[6 + k], t_recv.at[6 + k], core)

    first = [[entry(0, k, y, core) for k in range(3)], [entry(1, k, 1 - y, ydev) for k in range(3)], [onward(k) for k in range(3)]]
    for trio in first[:2]:
        trio[1].start()
    for load in marks:
        load.wait()
    lane64 = lax.broadcasted_iota(jnp.int32, (1, slots), 1)
    zero64 = jnp.zeros((1, slots), F32)
    for img in range(2):
        live = (lane64 < counts[:, pl.ds(img, 1)] * ROW_LEN).astype(F32)
        weight = live * flags[pl.ds(img, 1), :].astype(F32)
        for row, val in ((0, live), (1, weight)):
            low = jnp.concatenate([val, zero64], 1)
            high = jnp.concatenate([zero64, val], 1)
            meta[4 + img, pl.ds(row, 1), :] = jnp.where(c == 0, low, high)
    meta[b] = meta[4 + y]
    for k in (0, 2):
        for trio in first[:2]:
            trio[k].start()

    def chunk(q):
        return lax.rem(q + 2 * RING, RING)

    def fc2_streams(j):
        return [
            Stream(
                way, dev,
                lambda k, yy, d=d: l2.at[pl.ds(al(k * 192 + 96 * d + 48 * j, 16), 48), :],
                lambda k, yy, d=d: f2.at[c, k, pl.ds(96 * d + 48 * j, 48), :],
                r48.at[2 * j + d], x48.at[2 * j + d],
            )
            for d, (way, dev) in enumerate(ways)
        ]

    ways = ((1, nxt), (-1, prv))
    core_ways = tuple(
        (way * (1 - 2 * c), (jnp.where(c == 0, here[0], there[0]), b))
        for way, here, there in ((1, nxt, prv), (-1, prv, nxt))
    )
    split = ((0, 640), (640, 512))
    pairs = [
        Pair(0, "a", 0, "fc2a", 0, l2.at[pl.ds(0, 96), :], fc2_streams(0)),
        Pair(1, "a", 1, "fc2b", 0, l2.at[pl.ds(0, 96), :], fc2_streams(1)),
        Pair(2, "b", 0, "fc1", 1, l2.at[pl.ds(0, 96), :], [
            Stream(
                way, dev,
                lambda k, yy, d=d: l1.at[pl.ds(al(k * 96 + 48 * d, 16), 48), pl.ds(al(yy * width, 128), width)],
                lambda k, yy, d=d: f1.at[c, k, pl.ds(48 * d, 48), pl.ds(al(yy * width, 128), width)],
                r48.at[4 + d], y48.at[d],
            )
            for d, (way, dev) in enumerate(ways)
        ]),
        Pair(3, "b", 1, "qkv", 2, lq.at[pl.ds(0, 48), :], [
            Stream(
                way, dev,
                lambda k, yy, at=split[d]: lq.at[pl.ds(al(k * 96 + 48 * yy, 16), 48), pl.ds(*at)],
                lambda k, yy, at=split[d]: fq.at[c, k, pl.ds(al(48 * yy, 16), 48), pl.ds(*at)],
                (rqn, rqp)[d], (yqn, yqp)[d],
            )
            for d, (way, dev) in enumerate(core_ways)
        ]),
        Pair(4, "a", 2, "out", 3, l2.at[pl.ds(0, 48), :], [
            Stream(
                way, dev,
                lambda k, yy, d=d: lout.at[pl.ds(al(k * 48, 16), 48), pl.ds(half * d, half)],
                lambda k, yy, d=d: fo.at[c, k, :, pl.ds(half * d, half)],
                r384.at[d], x384.at[d],
            )
            for d, (way, dev) in enumerate(ways)
        ]),
    ]
    fc1_pair, qkv_pair = pairs[2], pairs[3]
    b_pairs = [fc1_pair, qkv_pair]
    last = RING - 2

    def rs_chunk(s, step):
        return chunk(p - s.way * (1 + step))

    def arrived(a, sem):
        remote(a.whole, a.whole, sem, sem, core).wait_recv()

    def left(a, sem):
        remote(a.whole, a.whole, sem, sem, core).wait_send()

    def y_ahead(a, step):
        for s in a.streams:
            remote(
                s.local(rs_chunk(s, step), 1 - y), s.other.at[step], yb_send.at[a.k], yb_recv.at[a.k, step], ydev
            ).start()

    def own(a, s, step):
        total = s.local(rs_chunk(s, step), y)[...].astype(F32)
        if a.kind == "b":
            total = total + s.other[step].astype(F32)
        return total

    def rs_send_on(a, s, src, step):
        remote(src, s.bufs.at[step], rs_send.at[a.i], rs_recv.at[a.i, step], s.dev).start()

    def rs_first(a):
        if a.kind == "b":
            arrived(a, yb_recv.at[a.k, 0])
        for s in a.streams:
            if a.kind == "a":
                rs_send_on(a, s, s.local(rs_chunk(s, 0), y), 0)
            else:
                s.other[0] = own(a, s, 0).astype(BF)
                rs_send_on(a, s, s.other.at[0], 0)

    def rs_arrived(a, step):
        if a.kind == "b":
            arrived(a, yb_recv.at[a.k, step])
        arrived(a, rs_recv.at[a.i, step - 1])
        left(a, rs_send.at[a.i])

    def rs_step(a, step):
        rs_arrived(a, step)
        for s in a.streams:
            s.bufs[step - 1] = (own(a, s, step) + s.bufs[step - 1].astype(F32)).astype(BF)
            rs_send_on(a, s, s.bufs.at[step - 1], step)

    def rs_end(a):
        rs_arrived(a, RING - 1)
        for s in a.streams:
            total = (own(a, s, RING - 1) + s.bufs[last].astype(F32)).astype(BF)
            if a.kind == "a":
                s.bufs[last] = total
                remote(s.bufs.at[last], s.other, ya_send.at[a.k], ya_recv.at[a.k], ydev).start()
            else:
                s.final(p, y)[...] = total

    def over_groups(a, d):
        s, i = a.streams[d], 2 * a.i + d
        piece = s.final(p, y)
        slot = gsh.at[i, :, pl.ds(0, piece.shape[0]), pl.ds(0, piece.shape[1])]
        slot[group] = piece[...]
        sends = [
            remote(slot.at[group], slot.at[group], g_send.at[i, j], g_recv.at[i, j], dev) for j, dev in enumerate(others)
        ]
        for send in sends:
            send.start()
        for send in sends:
            send.wait()
        total = slot[0].astype(F32)
        for j in range(1, groups):
            total = total + slot[j].astype(F32)
        piece[...] = total.astype(BF)

    def ag_send_on(a, step):
        for s in a.streams:
            here = s.final(chunk(p - s.way * step), y)
            remote(here, here, ag_send.at[a.i], ag_recv.at[a.i, step], s.dev).start()

    def spread(a, step):
        for s in a.streams:
            here = s.final(chunk(p - s.way * step), y)
            if a.kind == "b":
                remote(here, here, yg_send.at[a.k], yg_recv.at[a.k, step], ydev).start()
            remote(here, here, c_send.at[a.array], c_recv.at[a.array], core).start()

    def y_arrived(a, step):
        if a.kind == "b":
            arrived(a, yg_recv.at[a.k, step])
            for s in a.streams:
                here = s.final(chunk(p - s.way * step), 1 - y)
                remote(here, here, c_send.at[a.array], c_recv.at[a.array], core).start()

    def ag_first(a):
        if a.kind == "a":
            arrived(a, ya_recv.at[a.k])
            left(a, ya_send.at[a.k])
            for s in a.streams:
                s.final(p, y)[...] = (s.bufs[last].astype(F32) + s.other[...].astype(F32)).astype(BF)
        if groups > 1:
            for d in range(2):
                over_groups(a, d)
        ag_send_on(a, 0)
        spread(a, 0)

    def ag_step(a, step):
        arrived(a, ag_recv.at[a.i, step - 1])
        left(a, ag_send.at[a.i])
        ag_send_on(a, step)
        spread(a, step)
        y_arrived(a, step - 1)

    def ag_end(a):
        arrived(a, ag_recv.at[a.i, last])
        left(a, ag_send.at[a.i])
        spread(a, RING - 1)
        y_arrived(a, last)

    y_bytes = [f1.at[c, :, pl.ds(0, 48), :], fq.at[c, :, pl.ds(0, 48), :]]

    def s_copy(k, way):
        at = chunk(p - way * k)
        return remote(sg.at[at], sg.at[at], s_send.at[0 if way == 1 else 1], s_recv.at[k if way == 1 else 4 + k], nxt if way == 1 else prv)

    def s_ring(k):
        if k == 0:
            sg[p] = sv[...]
        if k > 0:
            s_copy(k - 1, 1).wait()
        if 0 < k < RING // 2:
            s_copy(k - 1, -1).wait()
        if k < RING // 2:
            s_copy(k, 1).start()
        if k < RING // 2 - 1:
            s_copy(k, -1).start()

    def s_over_y():
        return remote(sy.at[0], sy.at[1], s_send.at[2], s_recv.at[8], ydev)

    def s_over_core():
        return remote(sall.at[c], sall.at[c], s_send.at[3], s_recv.at[9], core)

    def s_sum():
        s_ring(RING // 2)
        total = sg[0]
        for k in range(1, RING):
            total = total + sg[k]
        sy[0] = total
        s_over_y().start()

    def s_last():
        s_over_y().wait()
        total = sy[0] + sy[1]
        if groups > 1:
            gsv[group] = total
            sends = [
                remote(gsv.at[group], gsv.at[group], g_send.at[10, j], g_recv.at[10, j], dev)
                for j, dev in enumerate(others)
            ]
            for send in sends:
                send.start()
            for send in sends:
                send.wait()
            total = gsv[0]
            for j in range(1, groups):
                total = total + gsv[j]
        sall[c] = total
        s_over_core().start()

    def when(cond, fn):
        if isinstance(cond, bool):
            if cond:
                fn()
        else:
            pl.when(cond)(fn)

    def both(*conds):
        if all(isinstance(v, bool) for v in conds):
            return all(conds)
        return functools.reduce(jnp.logical_and, conds)

    def tick(t):
        for i in ORDER:
            a = pairs[i]
            step = t - a.start
            when(step == 0, lambda a=a: rs_first(a))
            when(both(step >= 1, step <= last), lambda a=a, step=step: rs_step(a, step))
            when(step == RING - 1, lambda a=a: rs_end(a))
            if a.kind == "b":
                when(both(step >= 0, step < RING - AHEAD), lambda a=a, step=step: y_ahead(a, step + AHEAD))
            step = t - a.gather
            when(step == 0, lambda a=a: ag_first(a))
            when(both(step >= 1, step <= last), lambda a=a, step=step: ag_step(a, step))
            when(step == RING - 1, lambda a=a: ag_end(a))
            if a.kind == "b":
                when(step == RING, lambda a=a: y_arrived(a, RING - 1))
        if not isinstance(t, int):
            for k in range(RING // 2):
                when(t == SMALL + k, lambda k=k: s_ring(k))
            when(t == SMALL + RING // 2, s_sum)
            when(t == SMALL + RING // 2 + 1, s_last)

    blocks = seq // 64

    def rows_of(i):
        return pl.ds(al(i * 64, 64), 64)

    def norm(src, gain, bias, unit_ref, inv_ref, out, start=0, count=blocks):
        def body(i, carry):
            r = rows_of(start + i)
            v = src[r, :].astype(F32)
            cen = v - jnp.mean(v, -1, keepdims=True)
            inv = lax.rsqrt(jnp.mean(cen * cen, -1, keepdims=True) + EPS)
            unit = cen * inv
            unit_ref[r, :] = unit
            inv_ref[r, :] = inv
            out[r, :] = (unit * gain[...] + bias[...]).astype(BF)
            return carry
        lax.fori_loop(0, count, body, 0, unroll=2)

    def project(yy):
        norm(xs, g1, b1, u1, inv1, n1, 2 * yy, 2)
        r = pl.ds(al(yy * 2 * slots, 2 * slots), 2 * slots)
        rows = n1[r, :]
        qkv[r, pl.ds(0, half)] = (dot(rows, wqkv[:, pl.ds(0, half)]) + qb[:, pl.ds(half_c, half)]).astype(BF)
        qkv[r, pl.ds(half, half)] = dot(rows, wqkv[:, pl.ds(half, half)]).astype(BF)
        qkv[r, pl.ds(2 * half, half)] = (
            dot(rows, wqkv[:, pl.ds(2 * half, half)]) + vb[:, pl.ds(half_c, half)]
        ).astype(BF)

    for load in small_loads + loads[:3]:
        load.wait()
    own_rows[0].wait()
    first[0][1].wait_recv()
    project(y)
    first[1][1].wait_recv()
    first[2][1].start()
    first[1][0].wait_recv()
    first[2][0].start()
    first[2][1].wait_recv()
    project(1 - y)
    first[1][2].wait_recv()
    first[2][2].start()
    first[0][0].wait_recv()
    first[2][0].wait_recv()

    live_row = jnp.concatenate([meta[0, 0:1, :] + meta[1, 0:1, :], meta[2, 0:1, :] + meta[3, 0:1, :]], 1)
    weight_row = jnp.concatenate([meta[0, 1:2, :] + meta[1, 1:2, :], meta[2, 1:2, :] + meta[3, 1:2, :]], 1)
    dead = jnp.where(live_row > 0.5, 0.0, -1e30)
    lane = lax.broadcasted_iota(jnp.int32, (1, 128), 1)
    low_lanes = lane < 64
    head_mask = [low_lanes.astype(BF), (lane >= 64).astype(BF)]
    head_dim = width // HEADS
    scale = head_dim ** -0.5

    def attend(pair, carry):
        off = al(pair * 128, 128)
        qp = qkv[:, pl.ds(off, 128)]
        kp = qkv[:, pl.ds(al(half + off, 128), 128)]
        vp = qkv[:, pl.ds(al(2 * half + off, 128), 128)]
        outs = []
        for hh in range(2):
            s = dot(qp * head_mask[hh], kp, NT) * scale
            s = s + dead
            e = jnp.exp(s - jnp.max(s, -1, keepdims=True))
            pr = (e * (1.0 / jnp.sum(e, -1, keepdims=True))).astype(BF)
            probs[2 * pair + hh] = pr
            outs.append(dot(pr, vp))
        o = jnp.where(low_lanes, outs[0], outs[1])
        mix[:, pl.ds(off, 128)] = o
        mrg[:, pl.ds(off, 128)] = o.astype(BF)
        return carry

    lax.fori_loop(0, half // 128, attend, 0, unroll=3)

    def swap(i):
        return remote(exs.at[i], exr.at[i], e_send.at[i], e_recv.at[i], core)

    loads[3].wait()
    def swap_rows(k):
        r = pl.ds(k * (seq // 2), seq // 2)
        return remote(exs.at[0, r, :], exr.at[0, r, :], e_send.at[3 * k], e_recv.at[3 * k], core)

    for k in range(2):
        r = pl.ds(k * (seq // 2), seq // 2)
        exs[0, r, :] = dot(mrg[r, :], wout[...]).astype(BF)
        swap_rows(k).start()
    n1t[...] = n1[...].T
    eye = lax.broadcasted_iota(jnp.int32, (seq, seq), 0) == lax.broadcasted_iota(jnp.int32, (seq, seq), 1)
    weight_col = jnp.sum(jnp.where(eye, weight_row, 0.0), -1, keepdims=True)
    own_rows[1].wait()
    first[0][2].wait_recv()
    first[2][2].wait()
    cs[...] = (cs[...].astype(F32) * weight_col).astype(BF)

    def residual(i, carry):
        r = rows_of(i)
        res[r, :] = xs[r, :].astype(F32) + exs[0, r, :].astype(F32) + exr[0, r, :].astype(F32) + ob[...]
        return carry

    for k in range(2):
        swap_rows(k).wait_recv()
        lax.fori_loop(2 * k, 2 * k + 2, residual, 0, unroll=2)
        norm(res, g2, b2, u2, inv2, n2, 2 * k, 2)
    n2t[...] = n2[...].T
    loads[4].wait()
    tile = 256
    root_half = 0.5 ** 0.5
    pdf_scale = (2.0 * jnp.pi) ** -0.5

    def hidden(j, carry):
        cols = pl.ds(al(j * tile, 128), tile)
        h = dot(n2[...], w1[:, cols]) + vecs[pl.ds(8 + 2 * c + j // 3, 1), pl.ds(al((j - 3 * (j // 3)) * tile, 128), tile)]
        cdf = 0.5 * (1.0 + lax.erf(h * root_half))
        act[:, cols] = (h * cdf).astype(BF)
        gd[:, cols] = cdf + h * (jnp.exp(-0.5 * h * h) * pdf_scale)
        return carry

    lax.fori_loop(0, ffh // tile, hidden, 0, unroll=3)
    loads[5].wait()

    def grad_fc2(j, carry):
        cols = pl.ds(al(j * tile, 128), tile)
        l2[cols, :] = (dot(act[:, cols], cs[...], TN) * factor).astype(BF)
        return carry

    lax.fori_loop(0, ffh // tile, grad_fc2, 0, unroll=3)
    tick(0)

    def grad_hidden(j, carry):
        cols = pl.ds(al(j * tile, 128), tile)
        d = dot(cs[...], w2[cols, :], NT) * gd[:, cols]
        low = d.astype(BF)
        gh[:, cols] = low
        row = j // 3
        sv[pl.ds(row, 1), pl.ds(al((j - 3 * row) * tile, 128), tile)] = (
            jnp.sum(low.astype(F32), 0, keepdims=True) * factor
        )
        return carry

    def grad_fc1(j, carry):
        cols = pl.ds(al(j * tile, 128), tile)
        l1[:, cols] = (dot(n2t[...], gh[:, cols]) * factor).astype(BF)
        return carry

    lax.fori_loop(0, ffh // tile, grad_hidden, 0, unroll=3)
    exs[1] = dot(gh[...], w1[...], NT).astype(BF)
    swap(1).start()
    lax.fori_loop(0, ffh // tile, grad_fc1, 0, unroll=3)
    for step in range(AHEAD):
        y_ahead(fc1_pair, step)
    tick(1)
    mps[...] = dot(act[...], w2[...]).astype(BF)

    def seg_rows(s):
        return pl.ds(al(s * slots, slots), slots)

    mlp_sends = [
        remote(mps.at[seg_rows(2 * k + 1 - c)], mpr.at[seg_rows(2 * k + 1 - c)], o_send.at[k], o_recv.at[k], core)
        for k in range(2)
    ]
    for send in mlp_sends:
        send.start()
    swap(1).wait_recv()

    zero_row = jnp.zeros((1, width), F32)

    def norm_back(slot, unit_ref, inv_ref, gain, base):
        def body(i, sums):
            r = rows_of(i)
            g = exs[slot, r, :].astype(F32) + exr[slot, r, :].astype(F32)
            unit = unit_ref[r, :]
            scaled = g * gain[...]
            inner_grad = inv_ref[r, :] * (
                scaled - jnp.mean(scaled, -1, keepdims=True) - unit * jnp.mean(scaled * unit, -1, keepdims=True)
            )
            total = base(r) + inner_grad
            gres[r, :] = total
            low = total.astype(BF)
            ga[r, :] = low
            return (
                sums[0] + jnp.sum(g * unit, 0, keepdims=True),
                sums[1] + jnp.sum(g, 0, keepdims=True),
                sums[2] + jnp.sum(low.astype(F32), 0, keepdims=True),
                sums[3] + jnp.sum(cs[r, :].astype(F32), 0, keepdims=True),
            )
        return lax.fori_loop(0, blocks, body, (zero_row,) * 4, unroll=2)

    def mine(row):
        return jnp.where(c == 0, row[:, :half], row[:, half:]) * factor

    s_gain, s_bias, s_out, s_two = norm_back(1, u2, inv2, g2, lambda r: cs[r, :].astype(F32))
    sv[pl.ds(5, 1), pl.ds(0, half)] = mine(s_gain)
    sv[pl.ds(5, 1), pl.ds(half, half)] = mine(s_bias)
    sv[pl.ds(4, 1), pl.ds(0, half)] = mine(s_out)
    sv[pl.ds(4, 1), pl.ds(half, half)] = mine(s_two)
    sv[pl.ds(6, 2), :] = jnp.zeros((2, width), F32)
    lout[...] = (dot(mrg[...], ga[...], TN) * factor).astype(BF)
    gm[...] = dot(ga[...], wout[...], NT).astype(BF)
    tick(2)

    def attend_back(pair, carry):
        off = al(pair * 128, 128)
        offk = al(half + off, 128)
        offv = al(2 * half + off, 128)
        qp = qkv[:, pl.ds(off, 128)]
        kp = qkv[:, pl.ds(offk, 128)]
        vp = qkv[:, pl.ds(offv, 128)]
        gmp = gm[:, pl.ds(off, 128)]
        op = mix[:, pl.ds(off, 128)]
        dq, dk, dv = [], [], []
        for hh in range(2):
            gmh = gmp * head_mask[hh]
            gp = dot(gmh, vp, NT)
            delta = jnp.sum(gmh.astype(F32) * op, -1, keepdims=True)
            pr = probs[2 * pair + hh]
            ds = (pr.astype(F32) * (gp - delta)).astype(BF)
            dq.append(dot(ds, kp))
            dk.append(dot(ds, qp, TN))
            dv.append(dot(pr, gmp, TN))
        gqkv[:, pl.ds(off, 128)] = (jnp.where(low_lanes, dq[0], dq[1]) * scale).astype(BF)
        gqkv[:, pl.ds(offk, 128)] = (jnp.where(low_lanes, dk[0], dk[1]) * scale).astype(BF)
        gqkv[:, pl.ds(offv, 128)] = jnp.where(low_lanes, dv[0], dv[1]).astype(BF)
        return carry

    lax.fori_loop(0, half // 128, attend_back, 0, unroll=3)
    tick(3)
    for j in range(3):
        cols = pl.ds(j * half, half)
        lq[:, cols] = (dot(n1t[...], gqkv[:, cols]) * factor).astype(BF)
    sv[pl.ds(2, 1), pl.ds(0, half)] = jnp.sum(gqkv[:, pl.ds(0, half)].astype(F32), 0, keepdims=True) * factor
    sv[pl.ds(2, 1), pl.ds(half, half)] = (
        jnp.sum(gqkv[:, pl.ds(2 * half, half)].astype(F32), 0, keepdims=True) * factor
    )
    for step in range(AHEAD):
        y_ahead(qkv_pair, step)
    exs[2] = dot(gqkv[...], wqkv[...], NT).astype(BF)
    swap(2).start()
    tick(4)

    def finish(target, landing, value, sends, sem0):
        for k in range(2):
            val = value(seg_rows(2 * k + c)).astype(BF)
            @pl.when(y == k)
            def _():
                target[y] = val
            @pl.when(y != k)
            def _():
                landing[0] = val
        send = remote(landing.at[0], landing.at[1], o_send.at[sem0], o_recv.at[sem0], ydev)
        send.start()
        return send

    for send in mlp_sends:
        send.wait_recv()
    lo_send = finish(
        lo_out, lo_s,
        lambda r: res[r, :] + mps[r, :].astype(F32) + mpr[r, :].astype(F32) + fb2[...], None, 2,
    )
    swap(2).wait_recv()
    s_gain, s_bias, _, _ = norm_back(2, u1, inv1, g1, lambda r: gres[r, :])
    gt_send = finish(gt_out, gt_s, lambda r: gres[r, :], None, 3)
    sv[pl.ds(3, 1), pl.ds(0, half)] = mine(s_gain)
    sv[pl.ds(3, 1), pl.ds(half, half)] = mine(s_bias)

    lax.fori_loop(LOOP, max(a.gather + (RING if a.kind == "b" else RING - 1) for a in pairs) + 1, lambda t, carry: (tick(t), carry)[1], 0)
    s_over_core().wait()

    lo_send.wait()
    lo_out[1 - y] = lo_s[1]
    gt_send.wait()
    gt_out[1 - y] = gt_s[1]

    for copy in first[0] + first[1] + first[2][:2]:
        copy.wait_send()
    for copy in (swap_rows(0), swap_rows(1), swap(1), swap(2)):
        copy.wait_send()
    for send in mlp_sends:
        send.wait_send()

    for a in b_pairs:
        remote(y_bytes[a.k], y_bytes[a.k], yb_send.at[a.k], yb_recv.at[a.k, 0], ydev).wait_send()
        remote(y_bytes[a.k], y_bytes[a.k], yg_send.at[a.k], yg_recv.at[a.k, 0], ydev).wait_send()
    for i, arr in enumerate((f2, f1, fq, fo)):
        remote(arr.at[c], arr.at[c], c_send.at[i], c_recv.at[i], core).wait()


def write_kernel(
    lo, gt, f2, f1, fq, fo, sall,
    o_lo, o_gt, o_ln1g, o_ln1b, o_qkv, o_qb, o_vb, o_out, o_ob, o_ln2g, o_ln2b, o_fc1, o_fb1, o_fc2, o_fb2,
    stage, sems, small_sems,
):
    width = f2.shape[3]
    half = width // 2
    ffh = f2.shape[1] * f2.shape[2]
    n_buf = stage.shape[0]
    jobs = []
    for c in range(2):
        for k in range(RING):
            jobs.append((f2, c, [k], 0, width, o_fc2.at[pl.ds(c * ffh + 192 * k, 192), :]))
        for k in range(0, RING, 2):
            for h in range(2):
                jobs.append((f1, c, [k, k + 1], width * h, width, o_fc1.at[pl.ds(96 * k, 192), pl.ds(c * ffh + width * h, width)]))
            for j in range(3):
                jobs.append((fq, c, [k, k + 1], half * j, half, o_qkv.at[pl.ds(96 * k, 192), pl.ds(j * width + c * half, half)]))
        for k in range(0, RING, 4):
            jobs.append((fo, c, [k, k + 1, k + 2, k + 3], 0, width, o_out.at[pl.ds(c * half + 48 * k, 192), :]))
    small = [(lo, o_lo), (gt, o_gt)]
    for c in range(2):
        for row in range(2):
            small.append((sall.at[c, row], o_fb1.at[pl.ds(c * ffh + row * width, width)]))
        for row, first, second in ((2, o_qb, o_vb), (3, o_ln1g, o_ln1b), (4, o_ob, o_fb2), (5, o_ln2g, o_ln2b)):
            small.append((sall.at[c, row, pl.ds(0, half)], first.at[pl.ds(c * half, half)]))
            small.append((sall.at[c, row, pl.ds(half, half)], second.at[pl.ds(c * half, half)]))
    small = [pltpu.make_async_copy(src, target, small_sems.at[i]) for i, (src, target) in enumerate(small)]
    for copy in small:
        copy.start()
    copies = []
    for i, (src, c, chunks, col, cols, target) in enumerate(jobs):
        slot = i % n_buf
        if i >= n_buf:
            copies[i - n_buf].wait()
        rows = 192 // len(chunks)
        for at, k in enumerate(chunks):
            stage[slot, pl.ds(at * rows, rows), pl.ds(0, cols)] = src[c, k, :, pl.ds(col, cols)].astype(F32)
        copy = pltpu.make_async_copy(stage.at[slot, :, pl.ds(0, cols)], target, sems.at[slot])
        copy.start()
        copies.append(copy)
    for copy in small + copies[-n_buf:]:
        copy.wait()


def shards(n_wide, tokens, cotangent, row_counts, mask_flags, ln1_gain, ln1_bias, w_qkv, q_bias, v_bias, w_out, out_bias, ln2_gain, ln2_bias, w_fc1, fc1_bias, w_fc2, fc2_bias):
    images, slots, width = tokens.shape
    ff = w_fc1.shape[1]
    n_blk = lax.axis_size("blk")
    seq, half, ffh = slots * n_blk, width // 2, ff // 2
    groups = n_wide // RING
    factor = float(images * slots * n_wide * n_blk) ** -0.5
    vm, dma = pltpu.VMEM, pltpu.SemaphoreType.DMA
    vspec, anyspec = pl.BlockSpec(memory_space=pltpu.VMEM), pl.BlockSpec(memory_space=pl.ANY)
    n_heads = HEADS // 2
    scratch = [
        vm((width, 3 * half), BF), vm((half, width), BF), vm((width, ffh), BF), vm((ffh, width), BF),
        vm((seq, width), BF), vm((seq, width), BF), vm((6, 8, 128), F32),
        vm((seq, width), BF), vm((width, seq), BF), vm((seq, width), F32), vm((seq, 1), F32),
        vm((seq, 3 * half), BF), vm((n_heads, seq, seq), BF), vm((seq, half), F32), vm((seq, half), BF),
        vm((3, seq, width), BF), vm((3, seq, width), BF), vm((seq, width), F32),
        vm((seq, width), BF), vm((width, seq), BF), vm((seq, width), F32), vm((seq, 1), F32),
        vm((seq, ffh), BF), vm((seq, ffh), F32), vm((seq, ffh), BF), vm((seq, width), F32), vm((seq, width), BF),
        vm((seq, half), BF), vm((seq, 3 * half), BF), vm((seq, width), BF), vm((seq, width), BF),
        vm((2, slots, width), BF), vm((2, slots, width), BF),
        vm((RING, 8, width), F32), vm((2, 8, width), F32), vm((8, width), F32),
        vm((ffh, width), BF), vm((width, ffh), BF), vm((width, 3 * half), BF), vm((half, width), BF),
        vm((6, RING - 1, 48, width), BF), vm((2, RING - 1, 48, half), BF),
        vm((RING - 1, 48, 640), BF), vm((RING - 1, 48, 512), BF),
        vm((2, RING, 48, width), BF), vm((RING, 48, 640), BF), vm((RING, 48, 512), BF),
        vm((4, 48, width), BF), vm((2, 48, half), BF),
        vm((10, groups, 48, width) if groups > 1 else (1, 1, 16, 128), BF),
        vm((groups, 8, width) if groups > 1 else (1, 8, 128), F32),
        vm((16, width), F32), vm((1, 2), jnp.int32), vm((2, slots), jnp.int32), dma((6,)), dma((16,)), dma((9,)), dma((9,)), dma((4,)), dma((4,)), dma((4,)), dma((4,)),
        dma((5,)), dma((5, RING - 1)), dma((2,)), dma((2, RING)), dma((3,)), dma((3,)),
        dma((5,)), dma((5, RING - 1)), dma((2,)), dma((2, RING)),
        dma((4,)), dma((4,)), dma((4,)), dma((10,)),
        dma((11 if groups > 1 else 1, max(groups - 1, 1))), dma((11 if groups > 1 else 1, max(groups - 1, 1))),
    ]
    outs = [
        vm(tokens.shape, BF), vm(tokens.shape, BF),
        vm((2, RING, ffh // RING, width), BF), vm((2, RING, width // RING, ffh), BF),
        vm((2, RING, width // RING, 3 * half), BF), vm((2, RING, half // RING, width), BF),
        vm((2, 8, width), F32),
    ]
    lo, gt, f2, f1, fq, fo, sall = pl.pallas_call(
        functools.partial(layer_kernel, n_wide, factor),
        out_shape=outs,
        in_specs=[anyspec] * 17,
        out_specs=[vspec] * 7,
        scratch_shapes=scratch,
        compiler_params=pltpu.CompilerParams(collective_id=0, has_side_effects=True, vmem_limit_bytes=46 * 2**20),
        name="layer",
    )(
        tokens, cotangent, row_counts.T, mask_flags, ln1_gain, ln1_bias, q_bias, v_bias, out_bias,
        ln2_gain, ln2_bias, fc2_bias, fc1_bias, w_qkv, w_out, w_fc1, w_fc2,
    )
    vec = jax.ShapeDtypeStruct((width,), F32)
    mat = lambda *shape: jax.ShapeDtypeStruct(shape, F32)
    n_buf = 6
    return pl.pallas_call(
        write_kernel,
        out_shape=[
            jax.ShapeDtypeStruct(tokens.shape, BF), jax.ShapeDtypeStruct(tokens.shape, BF),
            vec, vec, mat(width, 3 * width), vec, vec, mat(width, width), vec, vec, vec, mat(width, ff), mat(ff), mat(ff, width), vec,
        ],
        in_specs=[vspec] * 7,
        out_specs=[anyspec] * 15,
        scratch_shapes=[vm((n_buf, 192, width), F32), dma((n_buf,)), dma((24,))],
        compiler_params=pltpu.CompilerParams(vmem_limit_bytes=8 * 2**20),
        name="write",
    )(lo, gt, f2, f1, fq, fo, sall)


def solution(mesh):
    rows, whole = P("wide", "blk", None), P()
    return jax.shard_map(
        functools.partial(shards, mesh.shape["wide"]),
        mesh=mesh,
        in_specs=(rows, rows, P("wide", "blk"), P("wide", "blk")) + (whole,) * 13,
        out_specs=(rows, rows) + (whole,) * 13,
        check_vma=False,
    )
```

```python
import functools

import jax
import jax.numpy as jnp
from jax import lax
from jax.experimental import pallas as pl
from jax.experimental.pallas import tpu as pltpu
from jax.sharding import PartitionSpec as P

HEADS = 12
ROW_LEN = 14
EPS = 1e-06
RING = 8
BF = jnp.bfloat16
F32 = jnp.float32
MESH = pl.DeviceIdType.MESH
NT = (((1,), (1,)), ((), ()))
TN = (((0,), (0,)), ((), ()))


def dot(a, b, dims=(((1,), (0,)), ((), ()))):
    return lax.dot_general(a, b, dims, preferred_element_type=F32)


def ring_place(r):
    return jnp.where(r % 2 == 0, r // 2, RING - 1 - r // 2)


def ring_member(q):
    return jnp.where(q < RING // 2, 2 * q, 2 * RING - 1 - 2 * q)


def al(v, m):
    return pl.multiple_of(v, m)


class Stream:
    def __init__(self, way, dev, local, final, bufs, other):
        self.way, self.dev, self.local, self.final = way, dev, local, final
        self.bufs, self.other = bufs, other


class Pair:
    def __init__(self, i, kind, k, name, array, whole, streams):
        self.i, self.kind, self.k, self.array, self.whole, self.streams = i, kind, k, array, whole, streams
        self.start, self.gather = START[name], GATHER[name]


START = {"fc2a": 1, "fc2b": 0, "fc1": 2, "out": 5, "qkv": 5}
GATHER = {"fc2a": 12, "fc2b": 9, "fc1": 11, "out": 13, "qkv": 12}
SMALL = 8
LOOP = 5
AHEAD = 2
ORDER = (1, 4, 3, 2, 0)


def layer_kernel(n_wide, factor, *refs):
    (
        tok, cot, counts_h, flags_h, g1_h, b1_h, qb_h, vb_h, ob_h, g2_h, b2_h, fb2_h, fb1_h, wqkv_h, wout_h, w1_h, w2_h,
        lo_out, gt_out, f2, f1, fq, fo, sall,
        wqkv, wout, w1, w2, xs, cs, meta, n1, n1t, u1, inv1, qkv, probs, mix, mrg, exs, exr, res, n2, n2t, u2, inv2,
        act, gd, gh, gres, ga, gm, gqkv, mps, mpr, lo_s, gt_s, sg, sy, sv,
        l2, l1, lq, lout, r48, r384, rqn, rqp, y48, yqn, yqp, x48, x384, gsh, gsv,
        vecs, counts, flags, w_sem, v_sem, t_send, t_recv, e_send, e_recv, o_send, o_recv,
        rs_send, rs_recv, yb_send, yb_recv, ya_send, ya_recv, ag_send, ag_recv, yg_send, yg_recv,
        c_send, c_recv, s_send, s_recv, g_send, g_recv,
    ) = refs
    groups = n_wide // RING
    seq, width = xs.shape
    half = width // 2
    ffh = w1.shape[1]
    slots = seq // 4
    w = lax.axis_index("wide")
    b = lax.axis_index("blk")
    y, c = b // 2, b % 2
    group, inner = w // RING, w % RING
    p = ring_place(inner)

    def at_place(q):
        return (group * RING + ring_member(lax.rem(q + RING, RING)), b)

    nxt, prv = at_place(p + 1), at_place(p - 1)
    core = (w, 2 * y + 1 - c)
    ydev = (w, 2 * (1 - y) + c)
    others = [(lax.rem(group + j, groups) * RING + inner, b) for j in range(1, groups)]

    bar = pltpu.get_barrier_semaphore()
    greeted = [core, ydev, nxt, prv] + others
    for dev in greeted:
        pl.semaphore_signal(bar, inc=1, device_id=dev, device_id_type=MESH)
    half_c = al(c * half, 128)
    ffh_c = al(c * ffh, 128)
    seg = al(b * slots, slots)
    own_rows = [
        pltpu.make_async_copy(tok.at[y], xs.at[pl.ds(seg, slots), :], v_sem.at[12]),
        pltpu.make_async_copy(cot.at[y], cs.at[pl.ds(seg, slots), :], v_sem.at[13]),
    ]
    marks = [
        pltpu.make_async_copy(counts_h, counts, v_sem.at[14]),
        pltpu.make_async_copy(flags_h, flags, v_sem.at[15]),
    ]
    for load in marks + own_rows:
        load.start()
    loads = [
        pltpu.make_async_copy(wqkv_h.at[:, pl.ds(al(j * width + c * half, 128), half)], wqkv.at[:, pl.ds(j * half, half)], w_sem.at[j])
        for j in range(3)
    ] + [
        pltpu.make_async_copy(wout_h.at[pl.ds(half_c, half), :], wout, w_sem.at[3]),
        pltpu.make_async_copy(w1_h.at[:, pl.ds(ffh_c, ffh)], w1, w_sem.at[4]),
        pltpu.make_async_copy(w2_h.at[pl.ds(ffh_c, ffh), :], w2, w_sem.at[5]),
    ]
    small_loads = [
        pltpu.make_async_copy(vec, vecs.at[i], v_sem.at[i])
        for i, vec in enumerate((g1_h, b1_h, qb_h, vb_h, ob_h, g2_h, b2_h, fb2_h))
    ] + [
        pltpu.make_async_copy(fb1_h.at[pl.ds(i * width, width)], vecs.at[8 + i], v_sem.at[8 + i]) for i in range(2 * ffh // width)
    ]
    g1, b1, qb, vb, ob, g2, b2, fb2 = (vecs.at[pl.ds(i, 1), :] for i in range(8))
    for load in small_loads + loads[:3]:
        load.start()

    def remote(src, dst, send, recv, dev):
        return pltpu.make_async_remote_copy(
            src_ref=src, dst_ref=dst, send_sem=send, recv_sem=recv, device_id=dev, device_id_type=MESH
        )

    pl.semaphore_wait(bar, len(greeted))
    def entry(i, k, img, dev):
        src = (meta.at[4 + img], tok.at[img], cot.at[img])[k]
        dst = (meta.at[b], xs.at[pl.ds(seg, slots), :], cs.at[pl.ds(seg, slots), :])[k]
        return remote(src, dst, t_send.at[3 * i + k], t_recv.at[3 * i + k], dev)

    def onward(k):
        rows = pl.ds(al((2 * (1 - y) + c) * slots, slots), slots)
        here = (meta.at[2 * (1 - y) + c], xs.at[rows, :], cs.at[rows, :])[k]
        return remote(here, here, t_send.at[6 + k], t_recv.at[6 + k], core)

    first = [[entry(0, k, y, core) for k in range(3)], [entry(1, k, 1 - y, ydev) for k in range(3)], [onward(k) for k in range(3)]]
    for trio in first[:2]:
        trio[1].start()
    for load in loads[3:]:
        load.start()
    for load in marks:
        load.wait()
    lane64 = lax.broadcasted_iota(jnp.int32, (1, slots), 1)
    zero64 = jnp.zeros((1, slots), F32)
    for img in range(2):
        live = (lane64 < counts[:, pl.ds(img, 1)] * ROW_LEN).astype(F32)
        weight = live * flags[pl.ds(img, 1), :].astype(F32)
        for row, val in ((0, live), (1, weight)):
            low = jnp.concatenate([val, zero64], 1)
            high = jnp.concatenate([zero64, val], 1)
            meta[4 + img, pl.ds(row, 1), :] = jnp.where(c == 0, low, high)
    meta[b] = meta[4 + y]
    for k in (0, 2):
        for trio in first[:2]:
            trio[k].start()

    def chunk(q):
        return lax.rem(q + 2 * RING, RING)

    def fc2_streams(j):
        return [
            Stream(
                way, dev,
                lambda k, yy, d=d: l2.at[pl.ds(al(k * 192 + 96 * d + 48 * j, 16), 48), :],
                lambda k, yy, d=d: f2.at[c, k, pl.ds(96 * d + 48 * j, 48), :],
                r48.at[2 * j + d], x48.at[2 * j + d],
            )
            for d, (way, dev) in enumerate(ways)
        ]

    ways = ((1, nxt), (-1, prv))
    core_ways = tuple(
        (way * (1 - 2 * c), (jnp.where(c == 0, here[0], there[0]), b))
        for way, here, there in ((1, nxt, prv), (-1, prv, nxt))
    )
    split = ((0, 640), (640, 512))
    pairs = [
        Pair(0, "a", 0, "fc2a", 0, l2.at[pl.ds(0, 96), :], fc2_streams(0)),
        Pair(1, "a", 1, "fc2b", 0, l2.at[pl.ds(0, 96), :], fc2_streams(1)),
        Pair(2, "b", 0, "fc1", 1, l2.at[pl.ds(0, 96), :], [
            Stream(
                way, dev,
                lambda k, yy, d=d: l1.at[pl.ds(al(k * 96 + 48 * d, 16), 48), pl.ds(al(yy * width, 128), width)],
                lambda k, yy, d=d: f1.at[c, k, pl.ds(48 * d, 48), pl.ds(al(yy * width, 128), width)],
                r48.at[4 + d], y48.at[d],
            )
            for d, (way, dev) in enumerate(ways)
        ]),
        Pair(3, "b", 1, "qkv", 2, lq.at[pl.ds(0, 48), :], [
            Stream(
                way, dev,
                lambda k, yy, at=split[d]: lq.at[pl.ds(al(k * 96 + 48 * yy, 16), 48), pl.ds(*at)],
                lambda k, yy, at=split[d]: fq.at[c, k, pl.ds(al(48 * yy, 16), 48), pl.ds(*at)],
                (rqn, rqp)[d], (yqn, yqp)[d],
            )
            for d, (way, dev) in enumerate(core_ways)
        ]),
        Pair(4, "a", 2, "out", 3, l2.at[pl.ds(0, 48), :], [
            Stream(
                way, dev,
                lambda k, yy, d=d: lout.at[pl.ds(al(k * 48, 16), 48), pl.ds(half * d, half)],
                lambda k, yy, d=d: fo.at[c, k, :, pl.ds(half * d, half)],
                r384.at[d], x384.at[d],
            )
            for d, (way, dev) in enumerate(ways)
        ]),
    ]
    fc1_pair, qkv_pair = pairs[2], pairs[3]
    b_pairs = [fc1_pair, qkv_pair]
    last = RING - 2

    def rs_chunk(s, step):
        return chunk(p - s.way * (1 + step))

    def arrived(a, sem):
        remote(a.whole, a.whole, sem, sem, core).wait_recv()

    def left(a, sem):
        remote(a.whole, a.whole, sem, sem, core).wait_send()

    def y_ahead(a, step):
        for s in a.streams:
            remote(
                s.local(rs_chunk(s, step), 1 - y), s.other.at[step], yb_send.at[a.k], yb_recv.at[a.k, step], ydev
            ).start()

    def own(a, s, step):
        total = s.local(rs_chunk(s, step), y)[...].astype(F32)
        if a.kind == "b":
            total = total + s.other[step].astype(F32)
        return total

    def rs_send_on(a, s, src, step):
        remote(src, s.bufs.at[step], rs_send.at[a.i], rs_recv.at[a.i, step], s.dev).start()

    def rs_first(a):
        if a.kind == "b":
            arrived(a, yb_recv.at[a.k, 0])
        for s in a.streams:
            if a.kind == "a":
                rs_send_on(a, s, s.local(rs_chunk(s, 0), y), 0)
            else:
                s.other[0] = own(a, s, 0).astype(BF)
                rs_send_on(a, s, s.other.at[0], 0)

    def rs_arrived(a, step):
        if a.kind == "b":
            arrived(a, yb_recv.at[a.k, step])
        arrived(a, rs_recv.at[a.i, step - 1])
        left(a, rs_send.at[a.i])

    def rs_step(a, step):
        rs_arrived(a, step)
        for s in a.streams:
            s.bufs[step - 1] = (own(a, s, step) + s.bufs[step - 1].astype(F32)).astype(BF)
            rs_send_on(a, s, s.bufs.at[step - 1], step)

    def rs_end(a):
        rs_arrived(a, RING - 1)
        for s in a.streams:
            total = (own(a, s, RING - 1) + s.bufs[last].astype(F32)).astype(BF)
            if a.kind == "a":
                s.bufs[last] = total
                remote(s.bufs.at[last], s.other, ya_send.at[a.k], ya_recv.at[a.k], ydev).start()
            else:
                s.final(p, y)[...] = total

    def over_groups(a, d):
        s, i = a.streams[d], 2 * a.i + d
        piece = s.final(p, y)
        slot = gsh.at[i, :, pl.ds(0, piece.shape[0]), pl.ds(0, piece.shape[1])]
        slot[group] = piece[...]
        sends = [
            remote(slot.at[group], slot.at[group], g_send.at[i, j], g_recv.at[i, j], dev) for j, dev in enumerate(others)
        ]
        for send in sends:
            send.start()
        for send in sends:
            send.wait()
        total = slot[0].astype(F32)
        for j in range(1, groups):
            total = total + slot[j].astype(F32)
        piece[...] = total.astype(BF)

    def ag_send_on(a, step):
        for s in a.streams:
            here = s.final(chunk(p - s.way * step), y)
            remote(here, here, ag_send.at[a.i], ag_recv.at[a.i, step], s.dev).start()

    def spread(a, step):
        for s in a.streams:
            here = s.final(chunk(p - s.way * step), y)
            if a.kind == "b":
                remote(here, here, yg_send.at[a.k], yg_recv.at[a.k, step], ydev).start()
            remote(here, here, c_send.at[a.array], c_recv.at[a.array], core).start()

    def y_arrived(a, step):
        if a.kind == "b":
            arrived(a, yg_recv.at[a.k, step])
            for s in a.streams:
                here = s.final(chunk(p - s.way * step), 1 - y)
                remote(here, here, c_send.at[a.array], c_recv.at[a.array], core).start()

    def ag_first(a):
        if a.kind == "a":
            arrived(a, ya_recv.at[a.k])
            left(a, ya_send.at[a.k])
            for s in a.streams:
                s.final(p, y)[...] = (s.bufs[last].astype(F32) + s.other[...].astype(F32)).astype(BF)
        if groups > 1:
            for d in range(2):
                over_groups(a, d)
        ag_send_on(a, 0)
        spread(a, 0)

    def ag_step(a, step):
        arrived(a, ag_recv.at[a.i, step - 1])
        left(a, ag_send.at[a.i])
        ag_send_on(a, step)
        spread(a, step)
        y_arrived(a, step - 1)

    def ag_end(a):
        arrived(a, ag_recv.at[a.i, last])
        left(a, ag_send.at[a.i])
        spread(a, RING - 1)
        y_arrived(a, last)

    y_bytes = [f1.at[c, :, pl.ds(0, 48), :], fq.at[c, :, pl.ds(0, 48), :]]

    def s_copy(k, way):
        at = chunk(p - way * k)
        return remote(sg.at[at], sg.at[at], s_send.at[0 if way == 1 else 1], s_recv.at[k if way == 1 else 4 + k], nxt if way == 1 else prv)

    def s_ring(k):
        if k == 0:
            sg[p] = sv[...]
        if k > 0:
            s_copy(k - 1, 1).wait()
        if 0 < k < RING // 2:
            s_copy(k - 1, -1).wait()
        if k < RING // 2:
            s_copy(k, 1).start()
        if k < RING // 2 - 1:
            s_copy(k, -1).start()

    def s_over_y():
        return remote(sy.at[0], sy.at[1], s_send.at[2], s_recv.at[8], ydev)

    def s_over_core():
        return remote(sall.at[c], sall.at[c], s_send.at[3], s_recv.at[9], core)

    def s_sum():
        s_ring(RING // 2)
        total = sg[0]
        for k in range(1, RING):
            total = total + sg[k]
        sy[0] = total
        s_over_y().start()

    def s_last():
        s_over_y().wait()
        total = sy[0] + sy[1]
        if groups > 1:
            gsv[group] = total
            sends = [
                remote(gsv.at[group], gsv.at[group], g_send.at[10, j], g_recv.at[10, j], dev)
                for j, dev in enumerate(others)
            ]
            for send in sends:
                send.start()
            for send in sends:
                send.wait()
            total = gsv[0]
            for j in range(1, groups):
                total = total + gsv[j]
        sall[c] = total
        s_over_core().start()

    def when(cond, fn):
        if isinstance(cond, bool):
            if cond:
                fn()
        else:
            pl.when(cond)(fn)

    def both(*conds):
        if all(isinstance(v, bool) for v in conds):
            return all(conds)
        return functools.reduce(jnp.logical_and, conds)

    def tick(t):
        for i in ORDER:
            a = pairs[i]
            step = t - a.start
            when(step == 0, lambda a=a: rs_first(a))
            when(both(step >= 1, step <= last), lambda a=a, step=step: rs_step(a, step))
            when(step == RING - 1, lambda a=a: rs_end(a))
            if a.kind == "b":
                when(both(step >= 0, step < RING - AHEAD), lambda a=a, step=step: y_ahead(a, step + AHEAD))
            step = t - a.gather
            when(step == 0, lambda a=a: ag_first(a))
            when(both(step >= 1, step <= last), lambda a=a, step=step: ag_step(a, step))
            when(step == RING - 1, lambda a=a: ag_end(a))
            if a.kind == "b":
                when(step == RING, lambda a=a: y_arrived(a, RING - 1))
        if not isinstance(t, int):
            for k in range(RING // 2):
                when(t == SMALL + k, lambda k=k: s_ring(k))
            when(t == SMALL + RING // 2, s_sum)
            when(t == SMALL + RING // 2 + 1, s_last)

    blocks = seq // 64

    def rows_of(i):
        return pl.ds(al(i * 64, 64), 64)

    def norm(src, gain, bias, unit_ref, inv_ref, out, start=0, count=blocks):
        def body(i, carry):
            r = rows_of(start + i)
            v = src[r, :].astype(F32)
            cen = v - jnp.mean(v, -1, keepdims=True)
            inv = lax.rsqrt(jnp.mean(cen * cen, -1, keepdims=True) + EPS)
            unit = cen * inv
            unit_ref[r, :] = unit
            inv_ref[r, :] = inv
            out[r, :] = (unit * gain[...] + bias[...]).astype(BF)
            return carry
        lax.fori_loop(0, count, body, 0, unroll=2)

    def project(yy):
        norm(xs, g1, b1, u1, inv1, n1, 2 * yy, 2)
        r = pl.ds(al(yy * 2 * slots, 2 * slots), 2 * slots)
        rows = n1[r, :]
        qkv[r, pl.ds(0, half)] = (dot(rows, wqkv[:, pl.ds(0, half)]) + qb[:, pl.ds(half_c, half)]).astype(BF)
        qkv[r, pl.ds(half, half)] = dot(rows, wqkv[:, pl.ds(half, half)]).astype(BF)
        qkv[r, pl.ds(2 * half, half)] = (
            dot(rows, wqkv[:, pl.ds(2 * half, half)]) + vb[:, pl.ds(half_c, half)]
        ).astype(BF)

    for load in small_loads + loads[:3]:
        load.wait()
    own_rows[0].wait()
    first[0][1].wait_recv()
    project(y)
    first[1][1].wait_recv()
    first[2][1].start()
    first[1][0].wait_recv()
    first[2][0].start()
    first[2][1].wait_recv()
    project(1 - y)
    first[1][2].wait_recv()
    first[2][2].start()
    first[0][0].wait_recv()
    first[2][0].wait_recv()

    live_row = jnp.concatenate([meta[0, 0:1, :] + meta[1, 0:1, :], meta[2, 0:1, :] + meta[3, 0:1, :]], 1)
    weight_row = jnp.concatenate([meta[0, 1:2, :] + meta[1, 1:2, :], meta[2, 1:2, :] + meta[3, 1:2, :]], 1)
    dead = jnp.where(live_row > 0.5, 0.0, -1e30)
    lane = lax.broadcasted_iota(jnp.int32, (1, 128), 1)
    low_lanes = lane < 64
    head_mask = [low_lanes.astype(BF), (lane >= 64).astype(BF)]
    head_dim = width // HEADS
    scale = head_dim ** -0.5

    def attend(pair, carry):
        off = al(pair * 128, 128)
        qp = qkv[:, pl.ds(off, 128)]
        kp = qkv[:, pl.ds(al(half + off, 128), 128)]
        vp = qkv[:, pl.ds(al(2 * half + off, 128), 128)]
        outs = []
        for hh in range(2):
            s = dot(qp * head_mask[hh], kp, NT) * scale
            s = s + dead
            e = jnp.exp(s - jnp.max(s, -1, keepdims=True))
            pr = (e * (1.0 / jnp.sum(e, -1, keepdims=True))).astype(BF)
            probs[2 * pair + hh] = pr
            outs.append(dot(pr, vp))
        o = jnp.where(low_lanes, outs[0], outs[1])
        mix[:, pl.ds(off, 128)] = o
        mrg[:, pl.ds(off, 128)] = o.astype(BF)
        return carry

    lax.fori_loop(0, half // 128, attend, 0, unroll=3)

    def swap(i):
        return remote(exs.at[i], exr.at[i], e_send.at[i], e_recv.at[i], core)

    loads[3].wait()
    def swap_rows(k):
        r = pl.ds(k * (seq // 2), seq // 2)
        return remote(exs.at[0, r, :], exr.at[0, r, :], e_send.at[3 * k], e_recv.at[3 * k], core)

    for k in range(2):
        r = pl.ds(k * (seq // 2), seq // 2)
        exs[0, r, :] = dot(mrg[r, :], wout[...]).astype(BF)
        swap_rows(k).start()
    n1t[...] = n1[...].T
    eye = lax.broadcasted_iota(jnp.int32, (seq, seq), 0) == lax.broadcasted_iota(jnp.int32, (seq, seq), 1)
    weight_col = jnp.sum(jnp.where(eye, weight_row, 0.0), -1, keepdims=True)
    own_rows[1].wait()
    first[0][2].wait_recv()
    first[2][2].wait()
    cs[...] = (cs[...].astype(F32) * weight_col).astype(BF)

    def residual(i, carry):
        r = rows_of(i)
        res[r, :] = xs[r, :].astype(F32) + exs[0, r, :].astype(F32) + exr[0, r, :].astype(F32) + ob[...]
        return carry

    for k in range(2):
        swap_rows(k).wait_recv()
        lax.fori_loop(2 * k, 2 * k + 2, residual, 0, unroll=2)
        norm(res, g2, b2, u2, inv2, n2, 2 * k, 2)
    n2t[...] = n2[...].T
    loads[4].wait()
    tile = 256
    root_half = 0.5 ** 0.5
    pdf_scale = (2.0 * jnp.pi) ** -0.5

    def hidden(j, carry):
        cols = pl.ds(al(j * tile, 128), tile)
        h = dot(n2[...], w1[:, cols]) + vecs[pl.ds(8 + 2 * c + j // 3, 1), pl.ds(al((j - 3 * (j // 3)) * tile, 128), tile)]
        cdf = 0.5 * (1.0 + lax.erf(h * root_half))
        act[:, cols] = (h * cdf).astype(BF)
        gd[:, cols] = cdf + h * (jnp.exp(-0.5 * h * h) * pdf_scale)
        return carry

    lax.fori_loop(0, ffh // tile, hidden, 0, unroll=3)
    loads[5].wait()

    def grad_fc2(j, carry):
        cols = pl.ds(al(j * tile, 128), tile)
        l2[cols, :] = (dot(act[:, cols], cs[...], TN) * factor).astype(BF)
        return carry

    lax.fori_loop(0, ffh // tile, grad_fc2, 0, unroll=3)
    tick(0)

    def grad_hidden(j, carry):
        cols = pl.ds(al(j * tile, 128), tile)
        d = dot(cs[...], w2[cols, :], NT) * gd[:, cols]
        low = d.astype(BF)
        gh[:, cols] = low
        row = j // 3
        sv[pl.ds(row, 1), pl.ds(al((j - 3 * row) * tile, 128), tile)] = (
            jnp.sum(low.astype(F32), 0, keepdims=True) * factor
        )
        return carry

    def grad_fc1(j, carry):
        cols = pl.ds(al(j * tile, 128), tile)
        l1[:, cols] = (dot(n2t[...], gh[:, cols]) * factor).astype(BF)
        return carry

    lax.fori_loop(0, ffh // tile, grad_hidden, 0, unroll=3)
    exs[1] = dot(gh[...], w1[...], NT).astype(BF)
    swap(1).start()
    lax.fori_loop(0, ffh // tile, grad_fc1, 0, unroll=3)
    for step in range(AHEAD):
        y_ahead(fc1_pair, step)
    tick(1)
    mps[...] = dot(act[...], w2[...]).astype(BF)

    def seg_rows(s):
        return pl.ds(al(s * slots, slots), slots)

    mlp_sends = [
        remote(mps.at[seg_rows(2 * k + 1 - c)], mpr.at[seg_rows(2 * k + 1 - c)], o_send.at[k], o_recv.at[k], core)
        for k in range(2)
    ]
    for send in mlp_sends:
        send.start()
    swap(1).wait_recv()

    zero_row = jnp.zeros((1, width), F32)

    def norm_back(slot, unit_ref, inv_ref, gain, base):
        def body(i, sums):
            r = rows_of(i)
            g = exs[slot, r, :].astype(F32) + exr[slot, r, :].astype(F32)
            unit = unit_ref[r, :]
            scaled = g * gain[...]
            inner_grad = inv_ref[r, :] * (
                scaled - jnp.mean(scaled, -1, keepdims=True) - unit * jnp.mean(scaled * unit, -1, keepdims=True)
            )
            total = base(r) + inner_grad
            gres[r, :] = total
            low = total.astype(BF)
            ga[r, :] = low
            return (
                sums[0] + jnp.sum(g * unit, 0, keepdims=True),
                sums[1] + jnp.sum(g, 0, keepdims=True),
                sums[2] + jnp.sum(low.astype(F32), 0, keepdims=True),
                sums[3] + jnp.sum(cs[r, :].astype(F32), 0, keepdims=True),
            )
        return lax.fori_loop(0, blocks, body, (zero_row,) * 4, unroll=2)

    def mine(row):
        return jnp.where(c == 0, row[:, :half], row[:, half:]) * factor

    s_gain, s_bias, s_out, s_two = norm_back(1, u2, inv2, g2, lambda r: cs[r, :].astype(F32))
    sv[pl.ds(5, 1), pl.ds(0, half)] = mine(s_gain)
    sv[pl.ds(5, 1), pl.ds(half, half)] = mine(s_bias)
    sv[pl.ds(4, 1), pl.ds(0, half)] = mine(s_out)
    sv[pl.ds(4, 1), pl.ds(half, half)] = mine(s_two)
    sv[pl.ds(6, 2), :] = jnp.zeros((2, width), F32)
    lout[...] = (dot(mrg[...], ga[...], TN) * factor).astype(BF)
    gm[...] = dot(ga[...], wout[...], NT).astype(BF)
    tick(2)

    def attend_back(pair, carry):
        off = al(pair * 128, 128)
        offk = al(half + off, 128)
        offv = al(2 * half + off, 128)
        qp = qkv[:, pl.ds(off, 128)]
        kp = qkv[:, pl.ds(offk, 128)]
        vp = qkv[:, pl.ds(offv, 128)]
        gmp = gm[:, pl.ds(off, 128)]
        op = mix[:, pl.ds(off, 128)]
        dq, dk, dv = [], [], []
        for hh in range(2):
            gmh = gmp * head_mask[hh]
            gp = dot(gmh, vp, NT)
            delta = jnp.sum(gmh.astype(F32) * op, -1, keepdims=True)
            pr = probs[2 * pair + hh]
            ds = (pr.astype(F32) * (gp - delta)).astype(BF)
            dq.append(dot(ds, kp))
            dk.append(dot(ds, qp, TN))
            dv.append(dot(pr, gmp, TN))
        gqkv[:, pl.ds(off, 128)] = (jnp.where(low_lanes, dq[0], dq[1]) * scale).astype(BF)
        gqkv[:, pl.ds(offk, 128)] = (jnp.where(low_lanes, dk[0], dk[1]) * scale).astype(BF)
        gqkv[:, pl.ds(offv, 128)] = jnp.where(low_lanes, dv[0], dv[1]).astype(BF)
        return carry

    lax.fori_loop(0, half // 128, attend_back, 0, unroll=3)
    tick(3)
    for j in range(3):
        cols = pl.ds(j * half, half)
        lq[:, cols] = (dot(n1t[...], gqkv[:, cols]) * factor).astype(BF)
    sv[pl.ds(2, 1), pl.ds(0, half)] = jnp.sum(gqkv[:, pl.ds(0, half)].astype(F32), 0, keepdims=True) * factor
    sv[pl.ds(2, 1), pl.ds(half, half)] = (
        jnp.sum(gqkv[:, pl.ds(2 * half, half)].astype(F32), 0, keepdims=True) * factor
    )
    for step in range(AHEAD):
        y_ahead(qkv_pair, step)
    exs[2] = dot(gqkv[...], wqkv[...], NT).astype(BF)
    swap(2).start()
    tick(4)

    def finish(target, landing, value, sends, sem0):
        for k in range(2):
            val = value(seg_rows(2 * k + c)).astype(BF)
            @pl.when(y == k)
            def _():
                target[y] = val
            @pl.when(y != k)
            def _():
                landing[0] = val
        send = remote(landing.at[0], landing.at[1], o_send.at[sem0], o_recv.at[sem0], ydev)
        send.start()
        return send

    for send in mlp_sends:
        send.wait_recv()
    lo_send = finish(
        lo_out, lo_s,
        lambda r: res[r, :] + mps[r, :].astype(F32) + mpr[r, :].astype(F32) + fb2[...], None, 2,
    )
    swap(2).wait_recv()
    s_gain, s_bias, _, _ = norm_back(2, u1, inv1, g1, lambda r: gres[r, :])
    gt_send = finish(gt_out, gt_s, lambda r: gres[r, :], None, 3)
    sv[pl.ds(3, 1), pl.ds(0, half)] = mine(s_gain)
    sv[pl.ds(3, 1), pl.ds(half, half)] = mine(s_bias)

    lax.fori_loop(LOOP, max(a.gather + (RING if a.kind == "b" else RING - 1) for a in pairs) + 1, lambda t, carry: (tick(t), carry)[1], 0)
    s_over_core().wait()

    lo_send.wait()
    lo_out[1 - y] = lo_s[1]
    gt_send.wait()
    gt_out[1 - y] = gt_s[1]

    for copy in first[0] + first[1] + first[2][:2]:
        copy.wait_send()
    for copy in (swap_rows(0), swap_rows(1), swap(1), swap(2)):
        copy.wait_send()
    for send in mlp_sends:
        send.wait_send()

    for a in b_pairs:
        remote(y_bytes[a.k], y_bytes[a.k], yb_send.at[a.k], yb_recv.at[a.k, 0], ydev).wait_send()
        remote(y_bytes[a.k], y_bytes[a.k], yg_send.at[a.k], yg_recv.at[a.k, 0], ydev).wait_send()
    for i, arr in enumerate((f2, f1, fq, fo)):
        remote(arr.at[c], arr.at[c], c_send.at[i], c_recv.at[i], core).wait()


def write_kernel(
    lo, gt, f2, f1, fq, fo, sall,
    o_lo, o_gt, o_ln1g, o_ln1b, o_qkv, o_qb, o_vb, o_out, o_ob, o_ln2g, o_ln2b, o_fc1, o_fb1, o_fc2, o_fb2,
    stage, sems, small_sems,
):
    width = f2.shape[3]
    half = width // 2
    ffh = f2.shape[1] * f2.shape[2]
    n_buf = stage.shape[0]
    jobs = []
    for c in range(2):
        for k in range(RING):
            jobs.append((f2, c, [k], 0, width, o_fc2.at[pl.ds(c * ffh + 192 * k, 192), :]))
        for k in range(0, RING, 2):
            for h in range(2):
                jobs.append((f1, c, [k, k + 1], width * h, width, o_fc1.at[pl.ds(96 * k, 192), pl.ds(c * ffh + width * h, width)]))
            for j in range(3):
                jobs.append((fq, c, [k, k + 1], half * j, half, o_qkv.at[pl.ds(96 * k, 192), pl.ds(j * width + c * half, half)]))
        for k in range(0, RING, 4):
            jobs.append((fo, c, [k, k + 1, k + 2, k + 3], 0, width, o_out.at[pl.ds(c * half + 48 * k, 192), :]))
    small = [(lo, o_lo), (gt, o_gt)]
    for c in range(2):
        for row in range(2):
            small.append((sall.at[c, row], o_fb1.at[pl.ds(c * ffh + row * width, width)]))
        for row, first, second in ((2, o_qb, o_vb), (3, o_ln1g, o_ln1b), (4, o_ob, o_fb2), (5, o_ln2g, o_ln2b)):
            small.append((sall.at[c, row, pl.ds(0, half)], first.at[pl.ds(c * half, half)]))
            small.append((sall.at[c, row, pl.ds(half, half)], second.at[pl.ds(c * half, half)]))
    small = [pltpu.make_async_copy(src, target, small_sems.at[i]) for i, (src, target) in enumerate(small)]
    for copy in small:
        copy.start()
    copies = []
    for i, (src, c, chunks, col, cols, target) in enumerate(jobs):
        slot = i % n_buf
        if i >= n_buf:
            copies[i - n_buf].wait()
        rows = 192 // len(chunks)
        for at, k in enumerate(chunks):
            stage[slot, pl.ds(at * rows, rows), pl.ds(0, cols)] = src[c, k, :, pl.ds(col, cols)].astype(F32)
        copy = pltpu.make_async_copy(stage.at[slot, :, pl.ds(0, cols)], target, sems.at[slot])
        copy.start()
        copies.append(copy)
    for copy in small + copies[-n_buf:]:
        copy.wait()


def shards(n_wide, tokens, cotangent, row_counts, mask_flags, ln1_gain, ln1_bias, w_qkv, q_bias, v_bias, w_out, out_bias, ln2_gain, ln2_bias, w_fc1, fc1_bias, w_fc2, fc2_bias):
    images, slots, width = tokens.shape
    ff = w_fc1.shape[1]
    n_blk = lax.axis_size("blk")
    seq, half, ffh = slots * n_blk, width // 2, ff // 2
    groups = n_wide // RING
    factor = float(images * slots * n_wide * n_blk) ** -0.5
    vm, dma = pltpu.VMEM, pltpu.SemaphoreType.DMA
    vspec, anyspec = pl.BlockSpec(memory_space=pltpu.VMEM), pl.BlockSpec(memory_space=pl.ANY)
    n_heads = HEADS // 2
    scratch = [
        vm((width, 3 * half), BF), vm((half, width), BF), vm((width, ffh), BF), vm((ffh, width), BF),
        vm((seq, width), BF), vm((seq, width), BF), vm((6, 8, 128), F32),
        vm((seq, width), BF), vm((width, seq), BF), vm((seq, width), F32), vm((seq, 1), F32),
        vm((seq, 3 * half), BF), vm((n_heads, seq, seq), BF), vm((seq, half), F32), vm((seq, half), BF),
        vm((3, seq, width), BF), vm((3, seq, width), BF), vm((seq, width), F32),
        vm((seq, width), BF), vm((width, seq), BF), vm((seq, width), F32), vm((seq, 1), F32),
        vm((seq, ffh), BF), vm((seq, ffh), F32), vm((seq, ffh), BF), vm((seq, width), F32), vm((seq, width), BF),
        vm((seq, half), BF), vm((seq, 3 * half), BF), vm((seq, width), BF), vm((seq, width), BF),
        vm((2, slots, width), BF), vm((2, slots, width), BF),
        vm((RING, 8, width), F32), vm((2, 8, width), F32), vm((8, width), F32),
        vm((ffh, width), BF), vm((width, ffh), BF), vm((width, 3 * half), BF), vm((half, width), BF),
        vm((6, RING - 1, 48, width), BF), vm((2, RING - 1, 48, half), BF),
        vm((RING - 1, 48, 640), BF), vm((RING - 1, 48, 512), BF),
        vm((2, RING, 48, width), BF), vm((RING, 48, 640), BF), vm((RING, 48, 512), BF),
        vm((4, 48, width), BF), vm((2, 48, half), BF),
        vm((10, groups, 48, width) if groups > 1 else (1, 1, 16, 128), BF),
        vm((groups, 8, width) if groups > 1 else (1, 8, 128), F32),
        vm((16, width), F32), vm((1, 2), jnp.int32), vm((2, slots), jnp.int32), dma((6,)), dma((16,)), dma((9,)), dma((9,)), dma((4,)), dma((4,)), dma((4,)), dma((4,)),
        dma((5,)), dma((5, RING - 1)), dma((2,)), dma((2, RING)), dma((3,)), dma((3,)),
        dma((5,)), dma((5, RING - 1)), dma((2,)), dma((2, RING)),
        dma((4,)), dma((4,)), dma((4,)), dma((10,)),
        dma((11 if groups > 1 else 1, max(groups - 1, 1))), dma((11 if groups > 1 else 1, max(groups - 1, 1))),
    ]
    outs = [
        vm(tokens.shape, BF), vm(tokens.shape, BF),
        vm((2, RING, ffh // RING, width), BF), vm((2, RING, width // RING, ffh), BF),
        vm((2, RING, width // RING, 3 * half), BF), vm((2, RING, half // RING, width), BF),
        vm((2, 8, width), F32),
    ]
    lo, gt, f2, f1, fq, fo, sall = pl.pallas_call(
        functools.partial(layer_kernel, n_wide, factor),
        out_shape=outs,
        in_specs=[anyspec] * 17,
        out_specs=[vspec] * 7,
        scratch_shapes=scratch,
        compiler_params=pltpu.CompilerParams(collective_id=0, has_side_effects=True, vmem_limit_bytes=46 * 2**20),
        name="layer",
    )(
        tokens, cotangent, row_counts.T, mask_flags, ln1_gain, ln1_bias, q_bias, v_bias, out_bias,
        ln2_gain, ln2_bias, fc2_bias, fc1_bias, w_qkv, w_out, w_fc1, w_fc2,
    )
    vec = jax.ShapeDtypeStruct((width,), F32)
    mat = lambda *shape: jax.ShapeDtypeStruct(shape, F32)
    n_buf = 6
    return pl.pallas_call(
        write_kernel,
        out_shape=[
            jax.ShapeDtypeStruct(tokens.shape, BF), jax.ShapeDtypeStruct(tokens.shape, BF),
            vec, vec, mat(width, 3 * width), vec, vec, mat(width, width), vec, vec, vec, mat(width, ff), mat(ff), mat(ff, width), vec,
        ],
        in_specs=[vspec] * 7,
        out_specs=[anyspec] * 15,
        scratch_shapes=[vm((n_buf, 192, width), F32), dma((n_buf,)), dma((24,))],
        compiler_params=pltpu.CompilerParams(vmem_limit_bytes=8 * 2**20),
        name="write",
    )(lo, gt, f2, f1, fq, fo, sall)


def solution(mesh):
    rows, whole = P("wide", "blk", None), P()
    return jax.shard_map(
        functools.partial(shards, mesh.shape["wide"]),
        mesh=mesh,
        in_specs=(rows, rows, P("wide", "blk"), P("wide", "blk")) + (whole,) * 13,
        out_specs=(rows, rows) + (whole,) * 13,
        check_vma=False,
    )
```
